256 devices in a mesh: group: 4 (over x), patch: 64 (over y, z, core).
Axes of the slice: x: 4, y: 4, z: 8, core: 2. Of those that a mesh axis runs over, the one named last changes fastest.
Arguments:
- node_tape: bfloat16 [4, 65536, 512], P('group', 'patch'), may hold values from -6 to 6
- edge_tape: bfloat16 [4, 65536, 512], P('group', 'patch'), may hold values from -16 to 16
- node_cot: bfloat16 [4, 65536, 512], P('group', 'patch'), may hold values from -6 to 6
- edge_cot: bfloat16 [4, 65536, 512], P('group', 'patch'), may hold values from -6 to 6
- w_edge_in: bfloat16 [1536, 512], replicated, may hold values from -0.15625 to 0.15625
- w_edge_out: bfloat16 [512, 512], replicated, may hold values from -0.25 to 0.25
- gain_edge: float32 [512], replicated, may hold values from 0.1 to 1.9
- w_node_in: bfloat16 [1024, 512], replicated, may hold values from -0.1875 to 0.1875
- w_node_out: bfloat16 [512, 512], replicated, may hold values from -0.25 to 0.25
- gain_node: float32 [512], replicated, may hold values from 0.1 to 1.9
- senders: int32 [512, 128], P('patch'), may hold values from 0 to 1279
- receivers: int32 [512, 128], P('patch'), may hold values from 0 to 1023
- tile_count: int32 [64], P('patch'), may hold values from 1 to 8, as said below
- send_rows: int32 [64, 256], P('patch'), may hold values from 0 to 1023
Outputs:
- edge_grad: bfloat16 [4, 65536, 512], P('group', 'patch')
- node_grad: bfloat16 [4, 65536, 512], P('group', 'patch')
- grad_edge_in: float32 [1536, 512], P('patch')
- grad_edge_out: float32 [512, 512], P('patch')
- grad_gain_edge: float32 [512], P('patch')
- grad_node_in: float32 [1024, 512], P('patch')
- grad_node_out: float32 [512, 512], P('patch')
- grad_gain_node: float32 [512], P('patch')
The draws below stay inside these ranges and needn't reach their ends.
Inputs may be any that keep to these rules, and one draw needn't show every extreme that they name: Tiles 0 to tile_count - 1 of a patch's 8 slots hold edges, the rest are padding; some patch has all 8 live. `senders`: A value s below 1024 is a node of the edge's own patch; 1024 + k is the k-th halo row that patch receives, rows p * 4 to (p + 1) * 4 - 1 coming from patch p. `receivers`: A node of the edge's own patch. `send_rows`: entry p * 4 + j of patch q's list is the own node whose latent is the j-th halo row patch p receives from q; every patch sends exactly 4 rows to every patch.
All inputs are finite; a program needn't handle non-finite values.
Results may differ from the reference program's by a relative error of at most 0.014.
Values may be sent and summed in bfloat16 or wider, within the bound.
No kernel may reach another device: no remote copies, remote signals or barrier semaphores. Data moves between devices by JAX's collectives and lax.ppermute only.
A program may use at most 128 MiB of HBM per device.

```python
import jax
import jax.numpy as jnp
from jax import lax

L = 512
NODE_DEV = 1024
TCAP = 8
TILE = 128
HALO_DEV = 256
NODES = 65536
TILES = 512
EDGES = 65536
N_GROUP = 4
N_PATCH = 64


def draw_tile_count(key, part):
    devices = TILES // TCAP
    first_key, second_key, third_key = jax.random.split(jax.random.fold_in(key, 11), 3)
    lowest = jax.random.randint(first_key, (devices,), 1, TCAP // 2 + 1)
    crowded = jax.random.randint(second_key, (devices,), 0, 4) == 0
    chosen = jax.random.randint(third_key, (), 0, devices)
    filled = crowded | (jnp.arange(devices) == chosen)
    return jnp.where(filled, TCAP, lowest).astype(jnp.int32)


def set_ends(drawn, rng, smallest, top_value):
    longest = drawn.shape.index(max(drawn.shape))
    spots = []
    for shift in (0, 1):
        where = [jax.random.randint(jax.random.fold_in(rng, axis), (), 0, length) for axis, length in enumerate(drawn.shape)]
        where[longest] = (where[longest] + shift) % drawn.shape[longest]
        spots.append(tuple(where))
    return drawn.at[spots[0]].set(smallest).at[spots[1]].set(top_value)


def with_spikes(result, own_key, source, target, blocks, factor):
    def block_of(dim):
        return (jnp.arange(result.shape[dim]) // (result.shape[dim] // blocks)).reshape((-1,) + (1,) * (result.ndim - 1 - dim))

    first = jax.random.permutation(own_key, blocks)[block_of(target)]
    second = (block_of(target) + blocks // 2) % blocks
    return jnp.where((block_of(source) == first) | (block_of(source) == second), factor * result, result)


def block_levels(key, extent, cuts, least, largest):
    def one(position, shards_of):
        steps = jax.random.uniform(jax.random.fold_in(jax.random.fold_in(key, 6), position), (shards_of,), jnp.float32, least / len(cuts), largest / len(cuts))
        return jnp.repeat(jnp.exp(steps), extent[position] // shards_of).reshape((-1,) + (1,) * (len(extent) - position - 1))

    gain = one(*cuts[0])
    for cut in cuts[1:]:
        gain = gain * one(*cut)
    return gain


def bell_draw(key, shape, width, bound, cuts=(), kind=jnp.bfloat16):
    entries = jax.random.normal(key, shape, jnp.float32) * width
    if len(cuts) > 0:
        entries = block_levels(key, shape, cuts, -0.22, 0.18) * entries
    return jnp.clip(entries, min=-bound, max=bound).astype(kind)


def gaussian_with(own_key, extent, deviation, most, pieces, heavy, kind=jnp.bfloat16):
    values = deviation * jax.random.normal(own_key, extent, jnp.float32)
    if pieces:
        values = values * block_levels(own_key, extent, pieces, -0.22, 0.18)
    return jnp.clip(with_spikes(values, jax.random.fold_in(own_key, 3), *heavy), -most, most).astype(kind)


def setup_inputs(seed: int = 0) -> dict:
    arg_keys = jax.random.split(jax.random.key(seed), 15)
    node_tape = bell_draw(arg_keys[0], (N_GROUP, NODES, L), 1.0, 6.0, ((0, 4), (1, 64)))
    edge_tape = gaussian_with(arg_keys[1], (N_GROUP, EDGES, L), 1.0, 16.0, ((0, 4), (1, 64)), (1, 2, 64, 4.0))
    node_cot = bell_draw(arg_keys[2], (N_GROUP, NODES, L), 1.0, 6.0, ((0, 4), (1, 64)))
    edge_cot = bell_draw(arg_keys[3], (N_GROUP, EDGES, L), 1.0, 6.0, ((0, 4), (1, 64)))
    w_edge_in = bell_draw(arg_keys[4], (3 * L, L), (3 * L) ** -0.5, 0.15625)
    w_edge_out = bell_draw(arg_keys[5], (L, L), L ** -0.5, 0.25)
    gain_edge = jnp.clip(1.0 + 0.18 * jax.random.normal(arg_keys[6], (L,), jnp.float32), 0.1, 1.9)
    w_node_in = bell_draw(arg_keys[7], (2 * L, L), (2 * L) ** -0.5, 0.1875)
    w_node_out = bell_draw(arg_keys[8], (L, L), L ** -0.5, 0.25)
    gain_node = jnp.clip(1.0 + 0.18 * jax.random.normal(arg_keys[9], (L,), jnp.float32), 0.1, 1.9)
    senders = set_ends(jax.random.randint(arg_keys[10], (TILES, TILE), 0, NODE_DEV + HALO_DEV), jax.random.fold_in(arg_keys[10], 1), 0, (NODE_DEV + HALO_DEV) - 1).astype(jnp.int32)
    receivers = set_ends(jax.random.randint(arg_keys[11], (TILES, TILE), 0, NODE_DEV), jax.random.fold_in(arg_keys[11], 1), 0, NODE_DEV - 1).astype(jnp.int32)
    tile_count = draw_tile_count(jax.random.fold_in(arg_keys[14], 71), 0)
    send_rows = set_ends(jax.random.randint(arg_keys[13], (N_PATCH, HALO_DEV), 0, NODE_DEV), jax.random.fold_in(arg_keys[13], 1), 0, NODE_DEV - 1).astype(jnp.int32)
    return dict(node_tape=node_tape, edge_tape=edge_tape, node_cot=node_cot, edge_cot=edge_cot, w_edge_in=w_edge_in, w_edge_out=w_edge_out, gain_edge=gain_edge, w_node_in=w_node_in, w_node_out=w_node_out, gain_node=gain_node, senders=senders, receivers=receivers, tile_count=tile_count, send_rows=send_rows)


epsilon = 1e-05

def product(left, right):
    return jnp.dot(left, right, preferred_element_type=jnp.float32)

def silu_slope(values):
    squash = jax.nn.sigmoid(values)
    return squash * (1.0 + values * (1.0 - squash))

def normalize(values):
    centred = values - lax.optimization_barrier(jnp.mean(values, axis=1, keepdims=True))
    inverse = lax.rsqrt(lax.optimization_barrier(jnp.mean(centred * centred, axis=1, keepdims=True)) + epsilon)
    return (centred * inverse, inverse)

def normalize_back(upstream, normed, inverse):
    return inverse * (upstream - lax.optimization_barrier(jnp.mean(upstream, axis=1, keepdims=True)) - normed * lax.optimization_barrier(jnp.mean(upstream * normed, axis=1, keepdims=True)))

def member(node_rows, edge_rows, node_back, edge_back, weights, send_index, recv_index, live_mask):
    w_edge_in, w_edge_out, gain_edge, w_node_in, w_node_out, gain_node = weights
    features = node_rows.shape[1]
    node_count = node_rows.shape[0]
    edge_input = jnp.concatenate([edge_rows, node_rows[send_index], node_rows[recv_index]], axis=1)
    edge_first = product(edge_input, w_edge_in)
    hidden = jax.nn.silu(edge_first).astype(jnp.bfloat16)
    second = product(hidden, w_edge_out)
    normed_edge, inverse_edge = normalize(second)
    message = live_mask * (gain_edge.astype(jnp.float32) * normed_edge)
    gathered = jax.ops.segment_sum(message, recv_index, num_segments=node_count).astype(jnp.bfloat16)
    joined = jnp.concatenate([node_rows, gathered], axis=1)
    node_first = product(joined, w_node_in)
    node_hidden = jax.nn.silu(node_first).astype(jnp.bfloat16)
    node_second = product(node_hidden, w_node_out)
    normed_node, inverse_node = normalize(node_second)
    node_upstream = node_back.astype(jnp.float32)
    part_gain_node = lax.optimization_barrier(jnp.sum(node_upstream * normed_node, axis=0))
    grad_second = normalize_back(node_upstream * gain_node.astype(jnp.float32), normed_node, inverse_node).astype(jnp.bfloat16)
    part_node_out = product(node_hidden.T, grad_second)
    grad_first = (product(grad_second, w_node_out.T) * silu_slope(node_first)).astype(jnp.bfloat16)
    part_node_in = product(joined.T, grad_first)
    grad_joined = product(grad_first, w_node_in.T)
    grad_message = live_mask * (edge_back.astype(jnp.float32) + grad_joined[:, features:][recv_index])
    part_gain_edge = lax.optimization_barrier(jnp.sum(grad_message * normed_edge, axis=0))
    grad_edge_second = normalize_back(grad_message * gain_edge.astype(jnp.float32), normed_edge, inverse_edge).astype(jnp.bfloat16)
    part_edge_out = product(hidden.T, grad_edge_second)
    grad_edge_first = (product(grad_edge_second, w_edge_out.T) * silu_slope(edge_first)).astype(jnp.bfloat16)
    part_edge_in = product(edge_input.T, grad_edge_first)
    grad_input = product(grad_edge_first, w_edge_in.T)
    edge_grad = (live_mask * edge_back.astype(jnp.float32) + grad_input[:, :features]).astype(jnp.bfloat16)
    from_send = jax.ops.segment_sum(grad_input[:, features:2 * features], send_index, num_segments=node_count)
    from_recv = jax.ops.segment_sum(grad_input[:, 2 * features:], recv_index, num_segments=node_count)
    node_grad = (node_upstream + grad_joined[:, :features] + from_send + from_recv).astype(jnp.bfloat16)
    return (edge_grad, node_grad, (part_edge_in, part_edge_out, part_gain_edge, part_node_in, part_node_out, part_gain_node))

def reference(node_tape, edge_tape, node_cot, edge_cot, w_edge_in, w_edge_out, gain_edge, w_node_in, w_node_out, gain_node, senders, receivers, tile_count, send_rows):
    edge_slots = TCAP * TILE
    peer_rows = HALO_DEV // N_PATCH
    flat_send = senders.reshape(-1).astype(jnp.int32)
    slot_ids = jnp.arange(EDGES, dtype=jnp.int32)
    owner_dev = slot_ids // edge_slots
    halo_pos = jnp.maximum(flat_send - NODE_DEV, 0)
    source = halo_pos // peer_rows
    column = owner_dev * peer_rows + halo_pos % peer_rows
    remote = source * NODE_DEV + send_rows[source, column]
    send_index = jnp.where(flat_send < NODE_DEV, owner_dev * NODE_DEV + flat_send, remote).astype(jnp.int32)
    recv_index = (owner_dev * NODE_DEV + receivers.reshape(-1)).astype(jnp.int32)
    tile_slot = slot_ids % edge_slots // TILE
    live_mask = (tile_slot < tile_count[owner_dev]).astype(jnp.float32)[:, None]
    weights = (w_edge_in, w_edge_out, gain_edge, w_node_in, w_node_out, gain_node)

    def run_member(inputs):
        return member(inputs[0], inputs[1], inputs[2], inputs[3], weights, send_index, recv_index, live_mask)
    edge_grad, node_grad, partials = lax.map(run_member, (node_tape, edge_tape, node_cot, edge_cot))
    factor = (N_GROUP * EDGES) ** (-0.5)
    sums = [lax.optimization_barrier(jnp.sum(stack, axis=0)) * factor for stack in partials]
    return (edge_grad, node_grad, sums[0], sums[1], sums[2], sums[3], sums[4], sums[5])
```

```python
import functools

import jax
import jax.numpy as jnp
from jax import lax
from jax.experimental import pallas as pl
from jax.experimental.pallas import tpu as pltpu
from jax.sharding import PartitionSpec as P

epsilon = 1e-05
BF = jnp.bfloat16
F32 = jnp.float32
LANE = 128
ROWS = 256


def dot(a, b):
    return lax.dot_general(a, b, (((1,), (0,)), ((), ())), preferred_element_type=F32)


def dot_rt(a, b):
    return lax.dot_general(a, b, (((1,), (1,)), ((), ())), preferred_element_type=F32)


def dot_lt(a, b):
    return lax.dot_general(a, b, (((0,), (0,)), ((), ())), preferred_element_type=F32)


def iota(shape, dim):
    return lax.broadcasted_iota(jnp.int32, shape, dim)


def one_hot(mask):
    return jnp.where(mask, 1.0, 0.0).astype(BF)


def columns_of(index_ref, out_ref):
    tiles = index_ref.shape[0]
    full = jnp.concatenate(
        [index_ref[...], jnp.zeros((LANE - tiles, LANE), jnp.int32)], axis=0
    )
    turned = full.T
    for t in range(tiles):
        out_ref[t * LANE : (t + 1) * LANE, :] = jnp.broadcast_to(
            turned[:, t : t + 1], (LANE, LANE)
        )


def pick_rows(cols_ref, start, count, first, width):
    column = cols_ref[pl.ds(start, count), 0:1]
    return one_hot(column == iota((count, width), 1) + first)


def spread_rows(index_ref, start, count):
    tiles = index_ref.shape[0]
    base = iota((count, LANE), 0) + start
    return jnp.concatenate([one_hot(index_ref[t : t + 1, :] == base) for t in range(tiles)], axis=1)


def sigmoid(v):
    return 1.0 / (1.0 + jnp.exp(-v))


def live_rows(count_ref, start, count):
    return (iota((count, 1), 0) + start < count_ref[0] * LANE).astype(F32)


def normalize(values):
    centred = values - jnp.mean(values, axis=1, keepdims=True)
    inverse = lax.rsqrt(jnp.mean(centred * centred, axis=1, keepdims=True) + epsilon)
    return centred * inverse, inverse


def normalize_back(upstream, normed, inverse):
    return inverse * (
        upstream
        - jnp.mean(upstream, axis=1, keepdims=True)
        - normed * jnp.mean(upstream * normed, axis=1, keepdims=True)
    )


def loop(count, body):
    def step(i, carry):
        body(pl.multiple_of(i * ROWS, ROWS))
        return carry

    lax.fori_loop(0, count // ROWS, step, 0)


def outgoing_kernel(rows_ref, node_ref, out_ref):
    nodes, halo = node_ref.shape[0], rows_ref.shape[1]
    spread = one_hot(rows_ref[...] == iota((nodes, halo), 0))
    out_ref[...] = dot_lt(spread, node_ref[...]).astype(BF)


def own_kernel(node_ref, edge_ref, recv_ref, w_ref, out_ref, cols):
    nodes, width = node_ref.shape
    columns_of(recv_ref, cols)

    def body(start):
        here = pl.ds(start, ROWS)
        from_recv = dot(pick_rows(cols, start, ROWS, 0, nodes), node_ref[...]).astype(BF)
        out_ref[here, :] = dot(edge_ref[here, :], w_ref[0:width, :]) + dot(
            from_recv, w_ref[2 * width : 3 * width, :]
        )

    loop(edge_ref.shape[0], body)


def deal(place_ref, patches, pieces, send_ref, keep_ref):
    core, member = place_ref[0], place_ref[1]
    each = sum(rows for _, rows in pieces)
    batch = 1 if each % 16 == 0 else 2

    def step(i, carry):
        for which, out in ((core, keep_ref), (1 - core, send_ref)):
            for s in range(4):
                lanes = pl.ds(pl.multiple_of(((member + s) % 4) * LANE, LANE), LANE)
                found = []
                for b in range(batch):
                    patch = (i * batch + b) * 2 + which
                    for ref, rows in pieces:
                        found.append(ref[pl.ds(pl.multiple_of(patch * rows, 8), rows), lanes])
                where = pl.ds(pl.multiple_of(i * (batch * each), 16), batch * each)
                out[s, where, :] = jnp.concatenate(found, axis=0).astype(BF)
        return carry

    lax.fori_loop(0, patches // 2 // batch, step, 0)


def forward_kernel(
    patches,
    place_ref,
    count_ref,
    halo_ref,
    begun_ref,
    node_ref,
    cot_ref,
    send_ref,
    recv_ref,
    w_edge_ref,
    w_edge_out_ref,
    gain_edge_ref,
    w_node_ref,
    w_node_out_ref,
    gain_node_ref,
    hidden_ref,
    slope_ref,
    normed_ref,
    inverse_ref,
    node_acc_ref,
    back_ref,
    gain_ref,
    piece_send_ref,
    piece_keep_ref,
    cols,
    message,
    gathered,
    node_hidden,
    grad_second,
    grad_first,
    sum_in,
    sum_out,
):
    nodes, width = node_ref.shape
    halo = halo_ref.shape[0]
    columns_of(send_ref, cols)

    def edge_body(start):
        here = pl.ds(start, ROWS)
        latent = dot(pick_rows(cols, start, ROWS, 0, nodes), node_ref[...]) + dot(
            pick_rows(cols, start, ROWS, nodes, halo), halo_ref[...]
        )
        first = begun_ref[here, :] + dot(latent.astype(BF), w_edge_ref[width : 2 * width, :])
        squash = sigmoid(first)
        hidden = (first * squash).astype(BF)
        hidden_ref[here, :] = hidden
        slope_ref[here, :] = (squash * (1.0 + first * (1.0 - squash))).astype(BF)
        normed, inverse = normalize(dot(hidden, w_edge_out_ref[...]))
        normed_ref[here, :] = normed.astype(BF)
        inverse_ref[here, :] = jnp.broadcast_to(inverse, (ROWS, LANE))
        live = live_rows(count_ref, start, ROWS)
        message[here, :] = (live * (gain_edge_ref[...] * normed)).astype(BF)

    loop(begun_ref.shape[0], edge_body)
    gain_ref[...] = jnp.zeros_like(gain_ref)

    def node_body(start):
        here = pl.ds(start, ROWS)
        taken = dot(spread_rows(recv_ref, start, ROWS), message[...]).astype(BF)
        gathered[here, :] = taken
        first = dot(node_ref[here, :], w_node_ref[0:width, :]) + dot(
            taken, w_node_ref[width : 2 * width, :]
        )
        squash = sigmoid(first)
        hidden = (first * squash).astype(BF)
        node_hidden[here, :] = hidden
        slope = squash * (1.0 + first * (1.0 - squash))
        normed, inverse = normalize(dot(hidden, w_node_out_ref[...]))
        upstream = cot_ref[here, :].astype(F32)
        gain_ref[...] += jnp.sum(upstream * normed, axis=0, keepdims=True)
        second = normalize_back(upstream * gain_node_ref[...], normed, inverse).astype(BF)
        grad_second[here, :] = second
        grad = (dot_rt(second, w_node_out_ref[...]) * slope).astype(BF)
        grad_first[here, :] = grad
        node_acc_ref[here, :] = upstream + dot_rt(grad, w_node_ref[0:width, :])
        back_ref[here, :] = dot_rt(grad, w_node_ref[width : 2 * width, :]).astype(BF)

    loop(nodes, node_body)
    sum_out[...] = dot_lt(node_hidden[...], grad_second[...])
    sum_in[0:width, :] = dot_lt(node_ref[...], grad_first[...])
    sum_in[width : 2 * width, :] = dot_lt(gathered[...], grad_first[...])
    pieces = ((sum_in, 2 * width // patches), (sum_out, width // patches))
    deal(place_ref, patches, pieces, piece_send_ref, piece_keep_ref)


def backward_kernel(
    patches,
    count_ref,
    cot_ref,
    back_ref,
    send_ref,
    recv_ref,
    slope_ref,
    normed_ref,
    inverse_ref,
    node_acc_ref,
    gain_node_ref,
    w_edge_ref,
    w_edge_out_ref,
    gain_edge_ref,
    edge_grad_ref,
    node_out_ref,
    return_ref,
    second_ref,
    first_ref,
    from_send_ref,
    from_recv_ref,
    cols,
    gain,
):
    edges, width = cot_ref.shape
    nodes = back_ref.shape[0]
    halo = return_ref.shape[0]
    columns_of(recv_ref, cols)
    gain[...] = jnp.zeros_like(gain)

    def edge_body(start):
        here = pl.ds(start, ROWS)
        live = live_rows(count_ref, start, ROWS)
        upstream = live * cot_ref[here, :].astype(F32)
        taken = dot(pick_rows(cols, start, ROWS, 0, nodes), back_ref[...])
        message = upstream + live * taken
        normed = normed_ref[here, :].astype(F32)
        gain[...] += jnp.sum(message * normed, axis=0, keepdims=True)
        second = normalize_back(
            message * gain_edge_ref[...], normed, inverse_ref[here, 0:1]
        ).astype(BF)
        second_ref[here, :] = second
        grad = (dot_rt(second, w_edge_out_ref[...]) * slope_ref[here, :].astype(F32)).astype(BF)
        first_ref[here, :] = grad
        edge_grad_ref[here, :] = (upstream + dot_rt(grad, w_edge_ref[0:width, :])).astype(BF)

    loop(edges, edge_body)

    def halo_part(start):
        spread = spread_rows(send_ref, nodes + start, ROWS)
        total = dot(spread, first_ref[...]).astype(BF)
        from_send_ref[pl.ds(nodes + start, ROWS), :] = total
        return_ref[pl.ds(start, ROWS), 0:width] = dot_rt(
            total, w_edge_ref[width : 2 * width, :]
        ).astype(BF)

    loop(halo, halo_part)
    each, rows = width // patches, halo // patches
    row, lane = iota((halo, width), 0), iota((halo, width), 1)
    chosen = (row % rows == 0) & (lane // each == row // rows)
    deep, slot = iota((width, LANE), 0), iota((width, LANE), 1)
    for g, shift in ((gain, 0), (gain_node_ref, each)):
        part = dot(
            jnp.where(chosen, g[...], 0.0).astype(BF), one_hot(deep % each + shift == slot)
        )
        if shift == 0:
            both = part
        else:
            both = both + part
    return_ref[:, width : width + LANE] = both.astype(BF)

    def node_body(start):
        here = pl.ds(start, ROWS)
        sent = dot(spread_rows(send_ref, start, ROWS), first_ref[...]).astype(BF)
        received = dot(spread_rows(recv_ref, start, ROWS), first_ref[...]).astype(BF)
        from_send_ref[here, :] = sent
        from_recv_ref[here, :] = received
        node_out_ref[here, :] = (
            node_acc_ref[here, :]
            + dot_rt(sent, w_edge_ref[width : 2 * width, :])
            + dot_rt(received, w_edge_ref[2 * width : 3 * width, :])
        )

    loop(nodes, node_body)


def edge_weight_kernel(
    patches,
    place_ref,
    hidden_ref,
    second_ref,
    edge_ref,
    node_ref,
    halo_ref,
    first_ref,
    from_send_ref,
    from_recv_ref,
    piece_send_ref,
    piece_keep_ref,
    sum_in,
    sum_out,
):
    nodes, width = node_ref.shape
    halo = halo_ref.shape[0]
    sum_out[...] = dot_lt(hidden_ref[...], second_ref[...])
    sum_in[0:width, :] = dot_lt(edge_ref[...], first_ref[...])
    sum_in[width : 2 * width, :] = dot_lt(node_ref[...], from_send_ref[0:nodes, :]) + dot_lt(
        halo_ref[...], from_send_ref[nodes : nodes + halo, :]
    )
    sum_in[2 * width : 3 * width, :] = dot_lt(node_ref[...], from_recv_ref[...])
    pieces = ((sum_in, 3 * width // patches), (sum_out, width // patches))
    deal(place_ref, patches, pieces, piece_send_ref, piece_keep_ref)


def node_grad_kernel(rows_ref, returned_ref, acc_ref, out_ref, gain_ref):
    nodes, width = acc_ref.shape
    halo = returned_ref.shape[0]

    def body(start):
        here = pl.ds(start, ROWS)
        spread = one_hot(rows_ref[...] == iota((ROWS, halo), 0) + start)
        out_ref[here, :] = (acc_ref[here, :] + dot(spread, returned_ref[:, 0:width])).astype(BF)

    loop(nodes, body)
    total = jnp.sum(returned_ref[:, width : width + LANE].astype(F32), axis=0, keepdims=True)
    gain_ref[...] = jnp.broadcast_to(total, gain_ref.shape)


def pair_kernel(keep_ref, got_ref, *outs):
    for s in range(4):
        outs[s][...] = (keep_ref[s].astype(F32) + got_ref[s].astype(F32)).astype(BF)


def four_kernel(patches, *refs):
    out_ref = refs[-1]
    at = 0
    for part in range(2):
        a, b, c, d = refs[part * 4 : part * 4 + 4]
        total = a[...].astype(F32) + b[...].astype(F32) + c[...].astype(F32) + d[...].astype(F32)
        rows = total.shape[0] // patches
        out_ref[:, at : at + rows, :] = total.reshape(patches, rows, LANE).astype(BF)
        at += rows


def last_sum_kernel(got_ref, gain_ref, out_ref):
    rows = got_ref.shape[1]
    total = got_ref[0].astype(F32)
    for i in range(1, got_ref.shape[0]):
        total = total + got_ref[i].astype(F32)
    out_ref[...] = jnp.concatenate([total, gain_ref[...]], axis=0).astype(BF)


def finish_kernel(
    factor, place_ref, a, b, c, d, edge_in_ref, edge_out_ref, node_in_ref, node_out_ref, gain_ref
):
    member = place_ref[1]
    gain = jnp.zeros((8, LANE), F32)
    for s, ref in enumerate((a, b, c, d)):
        lanes = pl.ds(pl.multiple_of(((member - s + 4) % 4) * LANE, LANE), LANE)
        at = 0
        values = ref[...].astype(F32)
        for out in (node_in_ref, node_out_ref, edge_in_ref, edge_out_ref):
            rows = out.shape[0]
            out[:, lanes] = values[at : at + rows, :] * factor
            at += rows
        gain = gain + values[at : at + 8, :]
    gain_ref[...] = gain * factor


VM = pl.BlockSpec(memory_space=pltpu.VMEM)
SM = pl.BlockSpec(memory_space=pltpu.SMEM)


def call(kernel, outs, ins, scratch=(), scalars=0, flops=0, limit=40):
    shapes = [jax.ShapeDtypeStruct(s, d) for s, d in outs]
    single = len(shapes) == 1
    size = sum(int(a.size) * a.dtype.itemsize for a in list(ins) + shapes)
    return pl.pallas_call(
        kernel,
        out_shape=shapes[0] if single else shapes,
        in_specs=[SM] * scalars + [VM] * (len(ins) - scalars),
        out_specs=VM if single else [VM] * len(shapes),
        scratch_shapes=[pltpu.VMEM(s, d) for s, d in scratch],
        compiler_params=pltpu.CompilerParams(vmem_limit_bytes=limit * 2**20),
        cost_estimate=pl.CostEstimate(flops=flops, bytes_accessed=size, transcendentals=0),
    )(*ins)


def local(
    node_tape,
    edge_tape,
    node_cot,
    edge_cot,
    w_edge_in,
    w_edge_out,
    gain_edge,
    w_node_in,
    w_node_out,
    gain_node,
    senders,
    receivers,
    tile_count,
    send_rows,
):
    node, edge = node_tape[0], edge_tape[0]
    n_cot, e_cot = node_cot[0], edge_cot[0]
    nodes, width = node.shape
    edges = edge.shape[0]
    halo = send_rows.shape[1]
    patches = lax.axis_size("patch")
    members = lax.axis_size("group")
    half = patches // 2
    place = jnp.stack([lax.axis_index("patch") % 2, lax.axis_index("group")]).astype(jnp.int32)
    gain_edge = gain_edge.reshape(1, width)
    gain_node = gain_node.reshape(1, width)
    twins = [(i, i ^ 1) for i in range(patches)]
    same_core = [[2 * i + c for i in range(half)] for c in range(2)]
    unit = 2 * width * width

    def to_member(x, shift):
        return lax.ppermute(x, "group", [(g, (g + shift) % members) for g in range(members)])

    def node_rows_of(count):
        return count * unit

    outgoing = call(
        outgoing_kernel, [((halo, width), BF)], [send_rows, node], flops=2 * halo * nodes * width
    )
    incoming = lax.all_to_all(outgoing, "patch", split_axis=0, concat_axis=0, tiled=True)
    begun = call(
        own_kernel,
        [((edges, width), F32)],
        [node, edge, receivers, w_edge_in],
        [((edges, LANE), jnp.int32)],
        flops=4 * edges * unit,
    )
    per_node, per_edge = 3 * width // patches, 4 * width // patches
    (
        hidden,
        slope,
        normed,
        inverse,
        node_acc,
        back,
        sum_gain_node,
        node_send,
        node_keep,
    ) = call(
        functools.partial(forward_kernel, patches),
        [
            ((edges, width), BF),
            ((edges, width), BF),
            ((edges, width), BF),
            ((edges, LANE), F32),
            ((nodes, width), F32),
            ((nodes, width), BF),
            ((1, width), F32),
            ((4, half * per_node, LANE), BF),
            ((4, half * per_node, LANE), BF),
        ],
        [
            place,
            tile_count,
            incoming,
            begun,
            node,
            n_cot,
            senders,
            receivers,
            w_edge_in,
            w_edge_out,
            gain_edge,
            w_node_in,
            w_node_out,
            gain_node,
        ],
        [
            ((edges, LANE), jnp.int32),
            ((edges, width), BF),
            ((nodes, width), BF),
            ((nodes, width), BF),
            ((nodes, width), BF),
            ((nodes, width), BF),
            ((2 * width, width), F32),
            ((width, width), F32),
        ],
        scalars=2,
        flops=16 * nodes * unit,
    )
    node_got = lax.ppermute(node_send, "patch", twins)
    (edge_grad, node_part, outward, grad_second, grad_first, from_send, from_recv) = call(
        functools.partial(backward_kernel, patches),
        [
            ((edges, width), BF),
            ((nodes, width), F32),
            ((halo, width + LANE), BF),
            ((edges, width), BF),
            ((edges, width), BF),
            ((nodes + halo, width), BF),
            ((nodes, width), BF),
        ],
        [
            tile_count,
            e_cot,
            back,
            senders,
            receivers,
            slope,
            normed,
            inverse,
            node_acc,
            sum_gain_node,
            w_edge_in,
            w_edge_out,
            gain_edge,
        ],
        [((edges, LANE), jnp.int32), ((1, width), F32)],
        scalars=1,
        flops=12 * nodes * unit,
    )

    def after_pair(keep, got):
        shape = keep.shape[1:]
        parts = call(pair_kernel, [(shape, BF)] * 4, [keep, got])
        return [parts[0]] + [to_member(parts[s], s) for s in range(1, 4)]

    node_parts = after_pair(node_keep, node_got)
    edge_send, edge_keep = call(
        functools.partial(edge_weight_kernel, patches),
        [((4, half * per_edge, LANE), BF)] * 2,
        [place, hidden, grad_second, edge, node, incoming, grad_first, from_send, from_recv],
        [((3 * width, width), F32), ((width, width), F32)],
        scalars=1,
        flops=4 * nodes * unit,
    )
    edge_got = lax.ppermute(edge_send, "patch", twins)
    returned = lax.all_to_all(outward, "patch", split_axis=0, concat_axis=0, tiled=True)
    edge_parts = after_pair(edge_keep, edge_got)
    node_grad, gains = call(
        node_grad_kernel,
        [((nodes, width), BF), ((8, LANE), F32)],
        [send_rows, returned, node_part],
        flops=2 * nodes * halo * width,
    )
    rows = per_node + per_edge
    blocks = call(
        functools.partial(four_kernel, half),
        [((half, rows, LANE), BF)],
        node_parts + edge_parts,
    )
    got = lax.all_to_all(
        blocks, "patch", split_axis=0, concat_axis=0, axis_index_groups=same_core, tiled=True
    )
    mine = call(last_sum_kernel, [((rows + 8, LANE), BF)], [got, gains])
    shared = [mine] + [to_member(mine, s) for s in range(1, 4)]
    factor = float(members * patches * edges) ** (-0.5)
    each = width // patches
    out_edge_in, out_edge_out, out_node_in, out_node_out, out_gain = call(
        functools.partial(finish_kernel, factor),
        [
            ((3 * each, width), F32),
            ((each, width), F32),
            ((2 * each, width), F32),
            ((each, width), F32),
            ((8, LANE), F32),
        ],
        [place] + shared,
        scalars=1,
    )
    return (
        edge_grad[None],
        node_grad[None],
        out_edge_in,
        out_edge_out,
        out_gain[0, 0:each],
        out_node_in,
        out_node_out,
        out_gain[0, each : 2 * each],
    )


def solution(mesh):
    placed = (
        P("group", "patch", None),
        P("group", "patch", None),
        P("group", "patch", None),
        P("group", "patch", None),
        P(),
        P(),
        P(),
        P(),
        P(),
        P(),
        P("patch", None),
        P("patch", None),
        P("patch"),
        P("patch", None),
    )
    return jax.shard_map(
        local,
        mesh=mesh,
        in_specs=placed,
        out_specs=(
            P("group", "patch", None),
            P("group", "patch", None),
            P("patch", None),
            P("patch", None),
            P("patch"),
            P("patch", None),
            P("patch", None),
            P("patch"),
        ),
        check_vma=False,
    )
```

```python
import functools

import jax
import jax.numpy as jnp
from jax import lax
from jax.experimental import pallas as pl
from jax.experimental.pallas import tpu as pltpu
from jax.sharding import PartitionSpec as P

epsilon = 1e-05
BF = jnp.bfloat16
F32 = jnp.float32
LANE = 128
ROWS = 256
FULL = 60 * 2**20


def dot(a, b):
    return lax.dot_general(a, b, (((1,), (0,)), ((), ())), preferred_element_type=F32)


def dot_rt(a, b):
    return lax.dot_general(a, b, (((1,), (1,)), ((), ())), preferred_element_type=F32)


def dot_lt(a, b):
    return lax.dot_general(a, b, (((0,), (0,)), ((), ())), preferred_element_type=F32)


def iota(shape, dim):
    return lax.broadcasted_iota(jnp.int32, shape, dim)


def one_hot(mask):
    return jnp.where(mask, 1.0, 0.0).astype(BF)


def columns_of(index_ref, out_ref):
    tiles = index_ref.shape[0]
    full = jnp.concatenate(
        [index_ref[...], jnp.zeros((LANE - tiles, LANE), jnp.int32)], axis=0
    )
    turned = full.T
    for t in range(tiles):
        out_ref[t * LANE : (t + 1) * LANE, :] = jnp.broadcast_to(
            turned[:, t : t + 1], (LANE, LANE)
        )


def pick_rows(cols_ref, start, count, first, width):
    column = cols_ref[pl.ds(start, count), 0:1]
    return one_hot(column == iota((count, width), 1) + first)


def spread_rows(index_ref, start, count):
    tiles = index_ref.shape[0]
    base = iota((count, LANE), 0) + start
    return jnp.concatenate([one_hot(index_ref[t : t + 1, :] == base) for t in range(tiles)], axis=1)


def sigmoid(v):
    return 1.0 / (1.0 + jnp.exp(-v))


def live_rows(count_ref, start, count):
    return (iota((count, 1), 0) + start < count_ref[0] * LANE).astype(F32)


def normalize(values):
    centred = values - jnp.mean(values, axis=1, keepdims=True)
    inverse = lax.rsqrt(jnp.mean(centred * centred, axis=1, keepdims=True) + epsilon)
    return centred * inverse, inverse


def normalize_back(upstream, normed, inverse):
    return inverse * (
        upstream
        - jnp.mean(upstream, axis=1, keepdims=True)
        - normed * jnp.mean(upstream * normed, axis=1, keepdims=True)
    )


def loop(count, body):
    def step(i, carry):
        body(pl.multiple_of(i * ROWS, ROWS), i)
        return carry

    lax.fori_loop(0, count // ROWS, step, 0)


def outgoing_kernel(rows_ref, node, out_ref):
    nodes, halo = node.shape[0], rows_ref.shape[1]
    spread = one_hot(rows_ref[...] == iota((nodes, halo), 0))
    out_ref[...] = dot_lt(spread, node.ready()[...]).astype(BF)


def own_kernel(
    send_ref,
    recv_ref,
    node,
    edge,
    w_edge,
    spread_recv,
    spread_send,
    node_turned,
    edge_turned,
    pick,
    begun,
    send_cols,
    recv_cols,
):
    nodes, width = node.shape
    columns_of(send_ref, send_cols)
    columns_of(recv_ref, recv_cols)
    for index_ref, out in ((recv_ref, spread_recv), (send_ref, spread_send)):

        def spread(start, i):
            out.buffer[pl.ds(start, ROWS), :] = spread_rows(index_ref, start, ROWS)
            out.send(i)

        loop(out.shape[0], spread)
    node_ref, edge_ref, w_ref = node.ready(), edge.ready(), w_edge.ready()
    for source, out in ((node_ref, node_turned), (edge_ref, edge_turned)):
        for i in range(0, source.shape[0], ROWS):
            out.buffer[:, i : i + ROWS] = source[i : i + ROWS, :].T
        out.send(0)

    def body(start, i):
        here = pl.ds(start, ROWS)
        picked = pick_rows(recv_cols, start, ROWS, 0, nodes)
        pick.buffer[here, :] = picked
        from_send = dot(pick_rows(send_cols, start, ROWS, 0, nodes), node_ref[...]).astype(BF)
        from_recv = dot(picked, node_ref[...]).astype(BF)
        begun.buffer[here, :] = (
            dot(edge_ref[here, :], w_ref[0:width, :])
            + dot(from_send, w_ref[width : 2 * width, :])
            + dot(from_recv, w_ref[2 * width : 3 * width, :])
        )
        pick.send(i)
        begun.send(i)

    loop(edge_ref.shape[0], body)


def deal(place_ref, depth, pieces, send, keep):
    core, column = place_ref[0], place_ref[1]
    each = sum(rows for _, rows in pieces)
    batch = 1 if each % 16 == 0 else 2
    for which, out in ((1 - core, send), (core, keep)):

        def step(s, carry):
            for i in range(0, depth, batch):
                found = []
                for b in range(batch):
                    patch = (((column + s) % 4) * depth + i + b) * 2 + which
                    for ref, rows in pieces:
                        found.append(ref[pl.ds(pl.multiple_of(patch * rows, 8), rows), :])
                out.buffer[s, i * each : (i + batch) * each, :] = jnp.concatenate(
                    found, axis=0
                ).astype(BF)
            out.send(s)
            return carry

        lax.fori_loop(0, 4, step, 0)


def forward_kernel(
    patches,
    place_ref,
    count_ref,
    send_ref,
    gain_edge_ref,
    gain_node_ref,
    incoming,
    begun,
    w_send,
    w_edge_out,
    spread_recv,
    node,
    w_node,
    w_node_out,
    cot,
    node_turned,
    gain_ref,
    slope,
    normed_out,
    inverse_out,
    hidden_out,
    node_acc,
    back,
    piece_send,
    piece_keep,
    cols,
    message,
    gathered,
    node_hidden,
    grad_second,
    grad_first,
    sum_in,
    sum_out,
):
    nodes, width = node.shape
    halo = incoming.shape[0]
    columns_of(send_ref, cols)
    halo_ref, w_send_ref, w_edge_out_ref = incoming.ready(), w_send.ready(), w_edge_out.ready()

    def edge_body(start, i):
        here = pl.ds(start, ROWS)
        latent = dot(pick_rows(cols, start, ROWS, nodes, halo), halo_ref[...])
        begun_ref = begun.part(i)
        first = begun_ref[here, :] + dot(latent.astype(BF), w_send_ref[...])
        squash = sigmoid(first)
        hidden = (first * squash).astype(BF)
        hidden_out.buffer[here, :] = hidden
        slope.buffer[here, :] = (squash * (1.0 + first * (1.0 - squash))).astype(BF)
        normed, inverse = normalize(dot(hidden, w_edge_out_ref[...]))
        normed_out.buffer[here, :] = normed.astype(BF)
        inverse_out.buffer[here, :] = jnp.broadcast_to(inverse, (ROWS, LANE))
        live = live_rows(count_ref, start, ROWS)
        message[here, :] = (live * (gain_edge_ref[...] * normed)).astype(BF)

        for out in (hidden_out, slope, normed_out, inverse_out):
            out.send(i)

    loop(begun.shape[0], edge_body)
    gain_ref[...] = jnp.zeros_like(gain_ref)
    node_ref, w_node_ref, w_node_out_ref = node.ready(), w_node.ready(), w_node_out.ready()
    cot_ref = cot.ready()

    def node_body(start, i):
        here = pl.ds(start, ROWS)
        spread_recv_ref = spread_recv.part(i)
        taken = dot(spread_recv_ref[here, :], message[...]).astype(BF)
        gathered[here, :] = taken
        first = dot(node_ref[here, :], w_node_ref[0:width, :]) + dot(
            taken, w_node_ref[width : 2 * width, :]
        )
        squash = sigmoid(first)
        hidden = (first * squash).astype(BF)
        node_hidden[here, :] = hidden
        node_slope = squash * (1.0 + first * (1.0 - squash))
        normed, inverse = normalize(dot(hidden, w_node_out_ref[...]))
        upstream = cot_ref[here, :].astype(F32)
        gain_ref[...] += jnp.sum(upstream * normed, axis=0, keepdims=True)
        second = normalize_back(upstream * gain_node_ref[...], normed, inverse).astype(BF)
        grad_second[here, :] = second
        grad = (dot_rt(second, w_node_out_ref[...]) * node_slope).astype(BF)
        grad_first[here, :] = grad
        node_acc.buffer[here, :] = upstream + dot_rt(grad, w_node_ref[0:width, :])
        back.buffer[here, :] = dot_rt(grad, w_node_ref[width : 2 * width, :]).astype(BF)
        node_acc.send(i)
        back.send(i)

    loop(nodes, node_body)
    sum_out[...] = dot_lt(node_hidden[...], grad_second[...])
    node_turned_ref = node_turned.ready()
    sum_in[0:width, :] = dot(node_turned_ref[...], grad_first[...])
    sum_in[width : 2 * width, :] = dot_lt(gathered[...], grad_first[...])
    pieces = ((sum_in, 2 * width // patches), (sum_out, width // patches))
    deal(place_ref, patches // 8, pieces, piece_send, piece_keep)


def backward_kernel(
    count_ref,
    gain_edge_ref,
    w_edge_out,
    back,
    pick,
    cot,
    normed_in,
    inverse,
    slope,
    gain_ref,
    token_ref,
    second_out,
    first_out,
):
    edges = cot.shape[0]
    gain_ref[...] = jnp.zeros_like(gain_ref)
    token_ref[...] = jnp.zeros_like(token_ref)
    w_edge_out_ref, back_ref = w_edge_out.ready(), back.ready()

    def edge_body(start, i):
        here = pl.ds(start, ROWS)
        live = live_rows(count_ref, start, ROWS)
        for part in (pick, cot, normed_in, inverse, slope):
            part.part(i)
        taken = dot(pick.buffer[here, :], back_ref[...])
        message = live * (cot.buffer[here, :].astype(F32) + taken)
        normed = normed_in.buffer[here, :].astype(F32)
        gain_ref[...] += jnp.sum(message * normed, axis=0, keepdims=True)
        second = normalize_back(
            message * gain_edge_ref[...], normed, inverse.buffer[here, 0:1]
        ).astype(BF)
        second_out.buffer[here, :] = second
        first_out.buffer[here, :] = (
            dot_rt(second, w_edge_out_ref[...]) * slope.buffer[here, :].astype(F32)
        ).astype(BF)
        second_out.send(i)
        first_out.send(i)

    loop(edges, edge_body)


def edge_weight_kernel(
    patches,
    place_ref,
    gain_edge_ref,
    gain_node_ref,
    after_ref,
    first,
    spread_send,
    spread_recv,
    hidden,
    second,
    edge_turned,
    node_turned,
    incoming,
    token_ref,
    from_send,
    from_recv,
    piece_send,
    piece_keep,
    sum_in,
    sum_out,
):
    width, nodes = node_turned.shape
    halo = incoming.shape[0]
    token_ref[...] = jnp.zeros_like(token_ref)
    first_ref = first.ready()
    for out, spread in ((from_send, spread_send), (from_recv, spread_recv)):

        def body(start, i):
            here = pl.ds(start, ROWS)
            out.buffer[here, :] = dot(spread.part(i)[here, :], first_ref[...]).astype(BF)
            out.send(i)

        loop(out.shape[0], body)
    sent, received = from_send.buffer, from_recv.buffer
    node_turned_ref = node_turned.ready()
    sum_in[0:width, :] = dot(edge_turned.ready()[...], first_ref[...])
    sum_in[width : 2 * width, :] = dot(node_turned_ref[...], sent[0:nodes, :]) + dot_lt(
        incoming.ready()[...], sent[nodes : nodes + halo, :]
    )
    sum_in[2 * width : 3 * width, :] = dot(node_turned_ref[...], received[...])
    sum_out[...] = dot_lt(hidden.ready()[...], second.ready()[...])
    extra = jnp.concatenate(
        [gain_edge_ref[...], gain_node_ref[...], jnp.zeros((14, width), F32)], axis=0
    ).astype(BF)
    rows = piece_keep.shape[1]
    for out in (piece_send, piece_keep):
        for s in range(4):
            out.buffer[s, rows - 16 : rows, :] = extra
    pieces = ((sum_in, 3 * width // patches), (sum_out, width // patches))
    deal(place_ref, patches // 8, pieces, piece_send, piece_keep)


def gate_kernel(after_ref, x_ref, out_ref):
    pass


def return_kernel(after_ref, halo_part, w_send, return_ref):
    return_ref[...] = dot_rt(halo_part.ready()[...], w_send.ready()[...]).astype(BF)


def input_kernel(
    count_ref,
    after_ref,
    w_edge,
    node_acc,
    from_send,
    from_recv,
    first,
    cot,
    token_ref,
    node_out,
    edge_grad,
):
    nodes, width = node_acc.shape
    token_ref[...] = jnp.zeros_like(token_ref)
    w_edge_ref = w_edge.ready()

    def node_body(start, i):
        here = pl.ds(start, ROWS)
        node_out.buffer[here, :] = (
            node_acc.part(i)[here, :]
            + dot_rt(from_send.part(i)[here, :], w_edge_ref[width : 2 * width, :])
            + dot_rt(from_recv.part(i)[here, :], w_edge_ref[2 * width : 3 * width, :])
        )
        node_out.send(i)

    loop(nodes, node_body)

    def edge_body(start, i):
        here = pl.ds(start, ROWS)
        live = live_rows(count_ref, start, ROWS)
        edge_grad.buffer[here, :] = (
            live * cot.part(i)[here, :].astype(F32)
            + dot_rt(first.part(i)[here, :], w_edge_ref[0:width, :])
        ).astype(BF)
        edge_grad.send(i)

    loop(cot.shape[0], edge_body)


def node_grad_kernel(rows_ref, after_ref, returned, acc, out):
    nodes = acc.shape[0]
    halo = returned.shape[0]
    returned_ref = returned.ready()

    def body(start, i):
        here = pl.ds(start, ROWS)
        spread = one_hot(rows_ref[...] == iota((ROWS, halo), 0) + start)
        out.buffer[here, :] = (acc.part(i)[here, :] + dot(spread, returned_ref[...])).astype(BF)
        out.send(i)

    loop(nodes, body)


def pair_kernel(after_ref, got, keep, token_ref, *outs):
    token_ref[...] = jnp.zeros_like(token_ref)
    for s in (1, 2, 3, 0):
        got.part(s)
        keep.part(s)
        outs[s].buffer[...] = (keep.buffer[s].astype(F32) + got.buffer[s].astype(F32)).astype(BF)
        outs[s].send(0)


def four_kernel(a, b, c, d, after_ref, out_ref, token_ref):
    total = a[...].astype(F32) + b[...].astype(F32) + c[...].astype(F32) + d[...].astype(F32)
    token_ref[...] = jnp.zeros_like(token_ref)
    depth, rows = out_ref.shape[0:2]
    if total.shape[0] == depth * rows:
        out_ref[...] = total.reshape(depth, rows, total.shape[1]).astype(BF)
    else:
        for z in range(depth):
            out_ref[z] = jnp.concatenate(
                [total[z * (rows - 8) : (z + 1) * (rows - 8)], total[depth * (rows - 8) :][0:8]],
                axis=0,
            ).astype(BF)


def depth_kernel(node_ref, edge_ref, out_ref):
    found = []
    for ref in (node_ref, edge_ref):
        total = ref[0].astype(F32)
        for i in range(1, ref.shape[0]):
            total = total + ref[i].astype(F32)
        found.append(total)
    out_ref[...] = jnp.concatenate(found, axis=0).astype(BF)


def finish_kernel(
    factor,
    place_ref,
    a,
    b,
    c,
    d,
    edge_in_ref,
    edge_out_ref,
    node_in_ref,
    node_out_ref,
    gain_ref,
    rows,
):
    member = place_ref[2]
    for s, ref in enumerate((a, b, c, d)):
        rows[(member - s + 4) % 4] = ref[...].astype(F32)
    total = ((rows[0] + rows[1]) + (rows[2] + rows[3])) * factor
    at = 0
    for out in (node_in_ref, node_out_ref, edge_in_ref, edge_out_ref, gain_ref):
        out[...] = total[at : at + out.shape[0], :]
        at += out.shape[0]


VM = pl.BlockSpec(memory_space=pltpu.VMEM)
SM = pl.BlockSpec(memory_space=pltpu.SMEM)
TOKEN = ((8, LANE), F32)


class Moved:
    def __init__(self, far, buffer, semaphores, parts, first, outward):
        self.far, self.buffer, self.semaphores = far, buffer, semaphores
        self.parts, self.first, self.outward = parts, first, outward
        self.shape = buffer.shape
        self.step = buffer.shape[0] // parts

    def copy(self, i):
        near = self.buffer.at[pl.ds(i * self.step, self.step)]
        far = self.far.at[pl.ds(self.first + i * self.step, self.step)]
        ends = (near, far) if self.outward else (far, near)
        return pltpu.make_async_copy(*ends, self.semaphores.at[i])

    def send(self, i):
        self.copy(i).start()

    def part(self, i):
        self.copy(i).wait()
        return self.buffer

    def ready(self):
        for i in range(self.parts):
            self.copy(i).wait()
        return self.buffer


class Part:
    def __init__(self, array, parts=1, first=0, rows=None):
        self.array, self.parts, self.first = array, parts, first
        self.rows = array.shape[0] if rows is None else rows


def call(kernel, outs, ins, scratch=(), scalars=0, flops=0, fetch=(), store=(), limit=None):
    ins = list(ins)
    fetch = [f if isinstance(f, Part) else Part(f) for f in fetch]
    shapes = [jax.ShapeDtypeStruct(s, d) for s, d in list(outs) + [o[:2] for o in store]]
    single = len(shapes) == 1
    buffers = [((f.rows, *f.array.shape[1:]), f.array.dtype) for f in fetch]
    size = sum(int(a.size) * a.dtype.itemsize for a in ins + shapes)
    held = list(scratch) + buffers + [o[:2] for o in store]
    bytes_here = sum(
        functools.reduce(lambda x, y: x * y, s) * jnp.dtype(d).itemsize for s, d in held
    )
    many, kept, given = len(fetch), len(store), len(outs)

    def take(refs, count):
        return refs[:count], refs[count:]

    def body(*refs):
        args, refs = take(refs, len(ins))
        sources, refs = take(refs, many)
        results, refs = take(refs, given)
        targets, refs = take(refs, kept)
        own, refs = take(refs, len(scratch))
        slots, refs = take(refs, many)
        rooms, refs = take(refs, kept)
        marks, ends = take(refs, many)
        arriving = [
            Moved(src, slot, mark, f.parts, f.first, False)
            for src, f, slot, mark in zip(sources, fetch, slots, marks)
        ]
        for one in arriving:
            for i in range(one.parts):
                one.send(i)
        leaving = [
            Moved(t, room, end, o[2], 0, True)
            for t, room, end, o in zip(targets, rooms, ends, store)
        ]
        kernel(*args, *arriving, *results, *leaving, *own)
        for one in leaving:
            one.ready()

    far = pl.BlockSpec(memory_space=pltpu.HBM)
    out_specs = [VM] * given + [far] * kept
    return pl.pallas_call(
        body,
        out_shape=shapes[0] if single else shapes,
        in_specs=[SM] * scalars + [VM] * (len(ins) - scalars) + [far] * many,
        out_specs=out_specs[0] if single else out_specs,
        scratch_shapes=[pltpu.VMEM(s, d) for s, d in held]
        + [pltpu.SemaphoreType.DMA((f.parts,)) for f in fetch]
        + [pltpu.SemaphoreType.DMA((o[2],)) for o in store],
        compiler_params=pltpu.CompilerParams(
            vmem_limit_bytes=bytes_here + 4 * 2**20 if limit is None else limit
        ),
        cost_estimate=pl.CostEstimate(flops=flops, bytes_accessed=size, transcendentals=0),
    )(*ins, *[f.array for f in fetch])


def gate(x, token):
    return pl.pallas_call(
        gate_kernel,
        out_shape=jax.ShapeDtypeStruct(x.shape, x.dtype),
        in_specs=[VM, pl.BlockSpec(memory_space=pltpu.HBM)],
        out_specs=pl.BlockSpec(memory_space=pltpu.HBM),
        input_output_aliases={1: 0},
        compiler_params=pltpu.CompilerParams(vmem_limit_bytes=FULL),
    )(token, x)


def local(
    node_tape,
    edge_tape,
    node_cot,
    edge_cot,
    w_edge_in,
    w_edge_out,
    gain_edge,
    w_node_in,
    w_node_out,
    gain_node,
    senders,
    receivers,
    tile_count,
    send_rows,
):
    node, edge = node_tape[0], edge_tape[0]
    n_cot, e_cot = node_cot[0], edge_cot[0]
    nodes, width = node.shape
    edges = edge.shape[0]
    halo = send_rows.shape[1]
    patches = lax.axis_size("patch")
    members = lax.axis_size("group")
    depth = patches // 8
    here = lax.axis_index("patch")
    place = jnp.stack([here % 2, here // (2 * depth), lax.axis_index("group")]).astype(jnp.int32)
    gain_edge = gain_edge.reshape(1, width)
    gain_node = gain_node.reshape(1, width)
    twins = [(i, i ^ 1) for i in range(patches)]
    column = 2 * depth
    lines = [[y * column + 2 * z + c for z in range(depth)] for y in range(4) for c in range(2)]
    unit = 2 * width * width

    def to_member(x, shift):
        return lax.ppermute(x, "group", [(g, (g + shift) % members) for g in range(members)])

    def to_column(x, shift):
        return lax.ppermute(x, "patch", [(i, (i + shift * column) % patches) for i in range(patches)])

    def along_depth(x, rows):
        return lax.all_to_all(
            x.reshape(depth, rows, width), "patch", 0, 0, axis_index_groups=lines, tiled=True
        )

    parts = edges // ROWS

    def wide(rows, kind=BF):
        return ((rows, width), kind, rows // ROWS)

    outgoing = call(
        outgoing_kernel,
        [((halo, width), BF)],
        [send_rows],
        flops=2 * halo * nodes * width,
        fetch=[node],
        limit=FULL,
    )
    incoming = lax.all_to_all(outgoing, "patch", split_axis=0, concat_axis=0, tiled=True)
    spread_recv, spread_send, node_turned, edge_turned, pick_recv, begun = call(
        own_kernel,
        [],
        [senders, receivers],
        [((edges, LANE), jnp.int32)] * 2,
        flops=7 * edges * unit,
        fetch=[node, edge, w_edge_in],
        store=[
            ((nodes, edges), BF, nodes // ROWS),
            ((nodes + halo, edges), BF, (nodes + halo) // ROWS),
            ((width, nodes), BF, 1),
            ((width, edges), BF, 1),
            ((edges, nodes), BF, parts),
            wide(edges, F32),
        ],
        limit=FULL,
    )
    per_node, per_edge = 3 * width // patches, 4 * width // patches
    node_piece = ((4, depth * per_node, width), BF, 4)
    edge_piece = ((4, depth * per_edge + 16, width), BF, 4)
    w_send = Part(w_edge_in, 1, width, width)
    (
        sum_gain_node,
        slope,
        normed,
        inverse,
        hidden,
        node_acc,
        back,
        node_send,
        node_keep,
    ) = call(
        functools.partial(forward_kernel, patches),
        [((1, width), F32)],
        [place, tile_count, senders, gain_edge, gain_node],
        [
            ((edges, LANE), jnp.int32),
            ((edges, width), BF),
            ((nodes, width), BF),
            ((nodes, width), BF),
            ((nodes, width), BF),
            ((nodes, width), BF),
            ((2 * width, width), F32),
            ((width, width), F32),
        ],
        scalars=2,
        flops=14 * nodes * unit,
        fetch=[
            incoming,
            Part(begun, parts),
            w_send,
            w_edge_out,
            Part(spread_recv, nodes // ROWS),
            node,
            w_node_in,
            w_node_out,
            n_cot,
            node_turned,
        ],
        store=[
            wide(edges),
            wide(edges),
            ((edges, LANE), F32, parts),
            wide(edges),
            wide(nodes, F32),
            wide(nodes),
            node_piece,
            node_piece,
        ],
        limit=FULL,
    )
    node_got = lax.ppermute(node_send, "patch", twins)
    sum_gain_edge, token, grad_second, grad_first = call(
        backward_kernel,
        [((1, width), F32), TOKEN],
        [tile_count, gain_edge],
        scalars=1,
        flops=3 * nodes * unit,
        fetch=[
            w_edge_out,
            back,
            Part(pick_recv, parts),
            Part(e_cot, parts),
            Part(normed, parts),
            Part(inverse, parts),
            Part(slope, parts),
        ],
        store=[wide(edges), wide(edges)],
        limit=FULL,
    )

    def after_pair(keep, got, after):
        shape = keep.shape[1:]
        token, *found = call(
            pair_kernel,
            [TOKEN],
            [after],
            fetch=[Part(got, 4), Part(keep, 4)],
            store=[(shape, BF, 1)] * 4,
        )
        return token, [found[0]] + [to_column(found[s], s) for s in range(1, 4)]

    token, node_parts = after_pair(node_keep, node_got, token)
    token, from_send, from_recv, edge_send, edge_keep = call(
        functools.partial(edge_weight_kernel, patches),
        [TOKEN],
        [place, sum_gain_edge, sum_gain_node, token],
        [((3 * width, width), F32), ((width, width), F32)],
        scalars=1,
        flops=9 * nodes * unit,
        fetch=[
            grad_first,
            Part(spread_send, (nodes + halo) // ROWS),
            Part(spread_recv, nodes // ROWS),
            hidden,
            grad_second,
            edge_turned,
            node_turned,
            incoming,
        ],
        store=[wide(nodes + halo), wide(nodes), edge_piece, edge_piece],
        limit=FULL,
    )
    node_blocks, token = call(
        four_kernel, [((depth, per_node, width), BF), TOKEN], node_parts + [token]
    )
    node_lines = along_depth(node_blocks, per_node)
    edge_got = lax.ppermute(gate(edge_send, token), "patch", twins)
    token, edge_parts = after_pair(edge_keep, edge_got, token)
    outward = call(
        return_kernel,
        [((halo, width), BF)],
        [token],
        flops=unit * halo,
        fetch=[Part(from_send, 1, nodes, halo), w_send],
    )
    returned = lax.all_to_all(outward, "patch", split_axis=0, concat_axis=0, tiled=True)
    token, node_part, edge_grad = call(
        input_kernel,
        [TOKEN],
        [tile_count, token],
        scalars=1,
        flops=3 * nodes * unit,
        fetch=[
            w_edge_in,
            Part(node_acc, nodes // ROWS),
            Part(from_send, nodes // ROWS, 0, nodes),
            Part(from_recv, nodes // ROWS),
            Part(grad_first, parts),
            Part(e_cot, parts),
        ],
        store=[wide(nodes, F32), wide(edges)],
        limit=FULL,
    )
    edge_blocks, token = call(
        four_kernel, [((depth, per_edge + 8, width), BF), TOKEN], edge_parts + [token]
    )
    edge_lines = along_depth(edge_blocks, per_edge + 8)
    node_grad = call(
        node_grad_kernel,
        [],
        [send_rows, token],
        flops=2 * nodes * halo * width,
        fetch=[returned, Part(node_part, nodes // ROWS)],
        store=[wide(nodes)],
        limit=FULL,
    )
    rows = per_node + per_edge + 8
    mine = call(depth_kernel, [((rows, width), BF)], [node_lines, edge_lines])
    shared = [mine] + [to_member(mine, s) for s in range(1, 4)]
    factor = float(members * patches * edges) ** (-0.5)
    each = width // patches
    out_edge_in, out_edge_out, out_node_in, out_node_out, out_gain = call(
        functools.partial(finish_kernel, factor),
        [
            ((3 * each, width), F32),
            ((each, width), F32),
            ((2 * each, width), F32),
            ((each, width), F32),
            ((8, width), F32),
        ],
        [place] + shared,
        [((4, rows, width), F32)],
        scalars=1,
    )
    out_gain = lax.dynamic_slice(out_gain, (0, here * each), (2, each))
    return (
        edge_grad[None],
        node_grad[None],
        out_edge_in,
        out_edge_out,
        out_gain[0],
        out_node_in,
        out_node_out,
        out_gain[1],
    )


def solution(mesh):
    placed = (
        P("group", "patch", None),
        P("group", "patch", None),
        P("group", "patch", None),
        P("group", "patch", None),
        P(),
        P(),
        P(),
        P(),
        P(),
        P(),
        P("patch", None),
        P("patch", None),
        P("patch"),
        P("patch", None),
    )
    return jax.shard_map(
        local,
        mesh=mesh,
        in_specs=placed,
        out_specs=(
            P("group", "patch", None),
            P("group", "patch", None),
            P("patch", None),
            P("patch", None),
            P("patch"),
            P("patch", None),
            P("patch", None),
            P("patch"),
        ),
        check_vma=False,
    )
```

```python
import functools

import jax
import jax.numpy as jnp
from jax import lax
from jax.experimental import pallas as pl
from jax.experimental.pallas import tpu as pltpu
from jax.sharding import PartitionSpec as P

epsilon = 1e-05
BF = jnp.bfloat16
F32 = jnp.float32
LANE = 128
ROWS = 256
FULL = 60 * 2**20


def dot(a, b):
    return lax.dot_general(a, b, (((1,), (0,)), ((), ())), preferred_element_type=F32)


def dot_rt(a, b):
    return lax.dot_general(a, b, (((1,), (1,)), ((), ())), preferred_element_type=F32)


def dot_lt(a, b):
    return lax.dot_general(a, b, (((0,), (0,)), ((), ())), preferred_element_type=F32)


def iota(shape, dim):
    return lax.broadcasted_iota(jnp.int32, shape, dim)


def one_hot(mask):
    return jnp.where(mask, 1.0, 0.0).astype(BF)


def columns_of(index_ref, out_ref):
    tiles = index_ref.shape[0]
    full = jnp.concatenate(
        [index_ref[...], jnp.zeros((LANE - tiles, LANE), jnp.int32)], axis=0
    )
    turned = full.T
    for t in range(tiles):
        out_ref[t * LANE : (t + 1) * LANE, :] = jnp.broadcast_to(
            turned[:, t : t + 1], (LANE, LANE)
        )


def pick_rows(cols_ref, start, count, first, width):
    column = cols_ref[pl.ds(start, count), 0:1]
    return one_hot(column == iota((count, width), 1) + first)


def spread_rows(index_ref, start, count):
    tiles = index_ref.shape[0]
    base = iota((count, LANE), 0) + start
    return jnp.concatenate([one_hot(index_ref[t : t + 1, :] == base) for t in range(tiles)], axis=1)


def sigmoid(v):
    return 0.5 * jnp.tanh(0.5 * v) + 0.5


def live_rows(count_ref, start, count):
    return (iota((count, 1), 0) + start < count_ref[0] * LANE).astype(F32)


def normalize(values):
    centred = values - jnp.mean(values, axis=1, keepdims=True)
    inverse = lax.rsqrt(jnp.mean(centred * centred, axis=1, keepdims=True) + epsilon)
    return centred * inverse, inverse


def normalize_back(upstream, normed, inverse):
    return inverse * (
        upstream
        - jnp.mean(upstream, axis=1, keepdims=True)
        - normed * jnp.mean(upstream * normed, axis=1, keepdims=True)
    )


def loop(count, body):
    def step(i, carry):
        body(pl.multiple_of(i * ROWS, ROWS), i)
        return carry

    lax.fori_loop(0, count // ROWS, step, 0)


def outgoing_kernel(rows_ref, node_ref, out_ref):
    nodes, halo = node_ref.shape[0], rows_ref.shape[1]
    spread = one_hot(rows_ref[...] == iota((nodes, halo), 0))
    out_ref[...] = dot_lt(spread, node_ref[...]).astype(BF)


def own_kernel(
    send_ref,
    recv_ref,
    node,
    edge,
    w_edge,
    node_turned,
    edge_turned,
    begun,
    send_cols,
    recv_cols,
):
    nodes, width = node.shape
    columns_of(send_ref, send_cols)
    columns_of(recv_ref, recv_cols)
    node_ref, edge_ref, w_ref = node.ready(), edge.ready(), w_edge.ready()

    def body(start, i):
        here = pl.ds(start, ROWS)
        from_send = dot(pick_rows(send_cols, start, ROWS, 0, nodes), node_ref[...]).astype(BF)
        from_recv = dot(pick_rows(recv_cols, start, ROWS, 0, nodes), node_ref[...]).astype(BF)
        begun.buffer[here, :] = (
            dot(edge_ref[here, :], w_ref[0:width, :])
            + dot(from_send, w_ref[width : 2 * width, :])
            + dot(from_recv, w_ref[2 * width : 3 * width, :])
        )
        begun.send(i)

    loop(edge_ref.shape[0], body)
    for source, out in ((node_ref, node_turned), (edge_ref, edge_turned)):
        for i in range(0, source.shape[0], ROWS):
            out.buffer[:, i : i + ROWS] = source[i : i + ROWS, :].T
        out.send(0)


def deal(place_ref, depth, pieces, first, send, keep):
    core, column = place_ref[0], place_ref[1]
    each = sum(rows for _, rows in pieces)
    batch = 1 if each % 16 == 0 else 2
    for which, out in ((1 - core, send), (core, keep)):

        def step(s, carry):
            for i in range(0, depth, batch):
                found = []
                for b in range(batch):
                    patch = (((column + s) % 4) * depth + i + b) * 2 + which
                    for ref, rows in pieces:
                        found.append(ref[pl.ds(pl.multiple_of(patch * rows, 8), rows), :])
                at = first + i * each
                out.buffer[s, at : at + batch * each, :] = jnp.concatenate(found, axis=0).astype(BF)
            return carry

        lax.fori_loop(0, 4, step, 0)


def main_kernel(
    patches,
    place_ref,
    count_ref,
    send_ref,
    recv_ref,
    gain_edge_ref,
    gain_node_ref,
    incoming,
    w_edge_send,
    begun,
    w_edge_out,
    node,
    w_node,
    w_node_out,
    node_cot,
    node_turned,
    edge_cot,
    edge_turned,
    node_acc,
    first_out,
    from_send,
    from_recv,
    outward,
    piece_send,
    piece_keep,
    send_cols,
    recv_cols,
    hidden_ref,
    slope_ref,
    normed_ref,
    inverse_ref,
    message,
    gathered,
    node_hidden,
    grad_second,
    grad_first,
    back_ref,
    gains,
    sum_in,
    sum_out,
    edge_sum_in,
    edge_sum_out,
):
    nodes, width = node.shape
    edges = begun.shape[0]
    halo = incoming.shape[0]
    columns_of(send_ref, send_cols)
    columns_of(recv_ref, recv_cols)
    halo_ref, w_send_ref, w_edge_out_ref = incoming.ready(), w_edge_send.ready(), None
    w_edge_out_ref = w_edge_out.ready()

    def edge_body(start, i):
        here = pl.ds(start, ROWS)
        latent = dot(pick_rows(send_cols, start, ROWS, nodes, halo), halo_ref[...])
        first = begun.part(i)[here, :] + dot(latent.astype(BF), w_send_ref[...])
        squash = sigmoid(first)
        hidden = (first * squash).astype(BF)
        hidden_ref[here, :] = hidden
        slope_ref[here, :] = (squash * (1.0 + first * (1.0 - squash))).astype(BF)
        normed, inverse = normalize(dot(hidden, w_edge_out_ref[...]))
        normed_ref[here, :] = normed.astype(BF)
        inverse_ref[here, :] = jnp.broadcast_to(inverse, (ROWS, LANE))
        live = live_rows(count_ref, start, ROWS)
        message[here, :] = (live * (gain_edge_ref[...] * normed)).astype(BF)

    loop(edges, edge_body)
    gains[...] = jnp.zeros_like(gains)
    node_ref, w_node_ref, w_node_out_ref = node.ready(), w_node.ready(), w_node_out.ready()

    def node_body(start, i):
        here = pl.ds(start, ROWS)
        taken = dot(spread_rows(recv_ref, start, ROWS), message[...]).astype(BF)
        gathered[here, :] = taken
        first = dot(node_ref[here, :], w_node_ref[0:width, :]) + dot(
            taken, w_node_ref[width : 2 * width, :]
        )
        squash = sigmoid(first)
        hidden = (first * squash).astype(BF)
        node_hidden[here, :] = hidden
        slope = squash * (1.0 + first * (1.0 - squash))
        normed, inverse = normalize(dot(hidden, w_node_out_ref[...]))
        upstream = node_cot.part(i)[here, :].astype(F32)
        gains[1:2, :] += jnp.sum(upstream * normed, axis=0, keepdims=True)
        second = normalize_back(upstream * gain_node_ref[...], normed, inverse).astype(BF)
        grad_second[here, :] = second
        grad = (dot_rt(second, w_node_out_ref[...]) * slope).astype(BF)
        grad_first[here, :] = grad
        node_acc.buffer[here, :] = (upstream + dot_rt(grad, w_node_ref[0:width, :])).astype(BF)
        back_ref[here, :] = dot_rt(grad, w_node_ref[width : 2 * width, :]).astype(BF)
        node_acc.send(i)

    loop(nodes, node_body)
    node_turned_ref = node_turned.ready()
    sum_out[...] = dot_lt(node_hidden[...], grad_second[...])
    sum_in[0:width, :] = dot(node_turned_ref[...], grad_first[...])
    sum_in[width : 2 * width, :] = dot_lt(gathered[...], grad_first[...])

    def back_body(start, i):
        here = pl.ds(start, ROWS)
        live = live_rows(count_ref, start, ROWS)
        taken = dot(pick_rows(recv_cols, start, ROWS, 0, nodes), back_ref[...])
        arrived = live * (edge_cot.part(i)[here, :].astype(F32) + taken)
        normed = normed_ref[here, :].astype(F32)
        gains[0:1, :] += jnp.sum(arrived * normed, axis=0, keepdims=True)
        second = normalize_back(
            arrived * gain_edge_ref[...], normed, inverse_ref[here, 0:1]
        ).astype(BF)
        grad_second[here, :] = second
        first_out.buffer[here, :] = (
            dot_rt(second, w_edge_out_ref[...]) * slope_ref[here, :].astype(F32)
        ).astype(BF)
        first_out.send(i)

    loop(edges, back_body)
    first_ref = first_out.buffer
    for out, index_ref in ((from_send, send_ref), (from_recv, recv_ref)):

        def body(start, i):
            out.buffer[pl.ds(start, ROWS), :] = dot(
                spread_rows(index_ref, start, ROWS), first_ref[...]
            ).astype(BF)
            out.send(i)

        loop(out.shape[0], body)
    sent, received = from_send.buffer, from_recv.buffer
    outward.buffer[...] = dot_rt(sent[nodes : nodes + halo, :], w_send_ref[...]).astype(BF)
    outward.send(0)
    edge_sum_out[...] = dot_lt(hidden_ref[...], grad_second[...])
    edge_sum_in[0:width, :] = dot(edge_turned.ready()[...], first_ref[...])
    edge_sum_in[width : 2 * width, :] = dot(node_turned_ref[...], sent[0:nodes, :]) + dot_lt(
        halo_ref[...], sent[nodes : nodes + halo, :]
    )
    edge_sum_in[2 * width : 3 * width, :] = dot(node_turned_ref[...], received[...])
    extra = jnp.concatenate([gains[...], jnp.zeros((8, width), F32)], axis=0).astype(BF)
    rows = piece_keep.shape[1]
    for out in (piece_send, piece_keep):
        for s in range(4):
            out.buffer[s, rows - 16 : rows, :] = extra
    depth = patches // 8
    each = width // patches
    pieces = ((sum_in, 2 * each), (sum_out, each))
    deal(place_ref, depth, pieces, 0, piece_send, piece_keep)
    pieces = ((edge_sum_in, 3 * each), (edge_sum_out, each))
    deal(place_ref, depth, pieces, depth * 3 * each, piece_send, piece_keep)
    for s in range(4):
        piece_send.send(s)
        piece_keep.send(s)


def edge_grad_kernel(count_ref, w_own, first, cot, edge_grad, token):
    token.buffer[...] = jnp.zeros(token.shape, F32)
    token.send(0)
    w_ref = w_own.ready()

    def edge_body(start, i):
        here = pl.ds(start, ROWS)
        live = live_rows(count_ref, start, ROWS)
        edge_grad.buffer[here, :] = (
            live * cot.part(i)[here, :].astype(F32) + dot_rt(first.part(i)[here, :], w_ref[...])
        ).astype(BF)
        edge_grad.send(i)

    loop(cot.shape[0], edge_body)


def node_grad_kernel(rows_ref, w_both, returned, acc, from_send, from_recv, out, token):
    token.buffer[...] = jnp.zeros(token.shape, F32)
    token.send(0)
    nodes, width = acc.shape
    halo = returned.shape[0]
    w_ref, returned_ref = w_both.ready(), returned.ready()

    def body(start, i):
        here = pl.ds(start, ROWS)
        spread = one_hot(rows_ref[...] == iota((ROWS, halo), 0) + start)
        out.buffer[here, :] = (
            acc.part(i)[here, :].astype(F32)
            + dot(spread, returned_ref[...])
            + dot_rt(from_send.part(i)[here, :], w_ref[0:width, :])
            + dot_rt(from_recv.part(i)[here, :], w_ref[width : 2 * width, :])
        ).astype(BF)
        out.send(i)

    loop(nodes, body)


def pair_kernel(keep_ref, got_ref, *outs):
    for s in range(4):
        outs[s][...] = (keep_ref[s].astype(F32) + got_ref[s].astype(F32)).astype(BF)


def four_kernel(counts, a, b, c, d, out_ref):
    total = a[...].astype(F32) + b[...].astype(F32) + c[...].astype(F32) + d[...].astype(F32)
    depth = out_ref.shape[0]
    last = total[depth * sum(counts) :][0:8]
    for z in range(depth):
        found, base = [], 0
        for rows in counts:
            found.append(total[base + z * rows : base + (z + 1) * rows])
            base += depth * rows
        out_ref[z] = jnp.concatenate(found + [last], axis=0).astype(BF)


def depth_kernel(got_ref, out_ref):
    total = got_ref[0].astype(F32)
    for i in range(1, got_ref.shape[0]):
        total = total + got_ref[i].astype(F32)
    out_ref[...] = total.astype(BF)


def finish_kernel(
    factor,
    place_ref,
    a,
    b,
    c,
    d,
    edge_in_ref,
    edge_out_ref,
    node_in_ref,
    node_out_ref,
    gain_ref,
    rows,
):
    member = place_ref[2]
    for s, ref in enumerate((a, b, c, d)):
        rows[(member - s + 4) % 4] = ref[...].astype(F32)
    total = ((rows[0] + rows[1]) + (rows[2] + rows[3])) * factor
    at = 0
    for out in (node_in_ref, node_out_ref, edge_in_ref, edge_out_ref, gain_ref):
        out[...] = total[at : at + out.shape[0], :]
        at += out.shape[0]


VM = pl.BlockSpec(memory_space=pltpu.VMEM)
SM = pl.BlockSpec(memory_space=pltpu.SMEM)

TOKEN = ((8, LANE), F32, 1)


class Moved:
    def __init__(self, far, buffer, semaphores, parts, first, outward):
        self.far, self.buffer, self.semaphores = far, buffer, semaphores
        self.parts, self.first, self.outward = parts, first, outward
        self.shape = buffer.shape
        self.step = buffer.shape[0] // parts

    def copy(self, i):
        near = self.buffer.at[pl.ds(i * self.step, self.step)]
        far = self.far.at[pl.ds(self.first + i * self.step, self.step)]
        ends = (near, far) if self.outward else (far, near)
        return pltpu.make_async_copy(*ends, self.semaphores.at[i])

    def send(self, i):
        self.copy(i).start()

    def part(self, i):
        self.copy(i).wait()
        return self.buffer

    def ready(self):
        for i in range(self.parts):
            self.copy(i).wait()
        return self.buffer


class Part:
    def __init__(self, array, parts=1, first=0, rows=None):
        self.array, self.parts, self.first = array, parts, first
        self.rows = array.shape[0] if rows is None else rows


def call(kernel, outs, ins, scratch=(), scalars=0, flops=0, fetch=(), store=(), limit=None, after=()):
    ins = list(ins)
    fetch = [f if isinstance(f, Part) else Part(f) for f in fetch]
    shapes = [jax.ShapeDtypeStruct(s, d) for s, d in list(outs) + [o[:2] for o in store]]
    single = len(shapes) == 1
    buffers = [((f.rows, *f.array.shape[1:]), f.array.dtype) for f in fetch]
    size = sum(int(a.size) * a.dtype.itemsize for a in ins + shapes)
    held = list(scratch) + buffers + [o[:2] for o in store]
    bytes_here = sum(
        functools.reduce(lambda x, y: x * y, s) * jnp.dtype(d).itemsize for s, d in held
    )
    many, kept, given = len(fetch), len(store), len(outs)

    def take(refs, count):
        return refs[:count], refs[count:]

    def body(*refs):
        args, refs = take(refs, len(ins))
        _, refs = take(refs, len(after))
        sources, refs = take(refs, many)
        results, refs = take(refs, given)
        targets, refs = take(refs, kept)
        own, refs = take(refs, len(scratch))
        slots, refs = take(refs, many)
        rooms, refs = take(refs, kept)
        marks, ends = take(refs, many)
        arriving = [
            Moved(src, slot, mark, f.parts, f.first, False)
            for src, f, slot, mark in zip(sources, fetch, slots, marks)
        ]
        for one in arriving:
            for i in range(one.parts):
                one.send(i)
        leaving = [
            Moved(t, room, end, o[2], 0, True)
            for t, room, end, o in zip(targets, rooms, ends, store)
        ]
        kernel(*args, *arriving, *results, *leaving, *own)
        for one in leaving:
            one.ready()

    far = pl.BlockSpec(memory_space=pltpu.HBM)
    out_specs = [VM] * given + [far] * kept
    return pl.pallas_call(
        body,
        out_shape=shapes[0] if single else shapes,
        in_specs=[SM] * scalars
        + [VM] * (len(ins) - scalars)
        + [pl.BlockSpec(memory_space=pl.ANY)] * len(after)
        + [far] * many,
        out_specs=out_specs[0] if single else out_specs,
        scratch_shapes=[pltpu.VMEM(s, d) for s, d in held]
        + [pltpu.SemaphoreType.DMA((f.parts,)) for f in fetch]
        + [pltpu.SemaphoreType.DMA((o[2],)) for o in store],
        compiler_params=pltpu.CompilerParams(
            vmem_limit_bytes=bytes_here + 4 * 2**20 if limit is None else limit
        ),
        cost_estimate=pl.CostEstimate(flops=flops, bytes_accessed=size, transcendentals=0),
    )(*ins, *after, *[f.array for f in fetch])


def local(
    node_tape,
    edge_tape,
    node_cot,
    edge_cot,
    w_edge_in,
    w_edge_out,
    gain_edge,
    w_node_in,
    w_node_out,
    gain_node,
    senders,
    receivers,
    tile_count,
    send_rows,
):
    node, edge = node_tape[0], edge_tape[0]
    n_cot, e_cot = node_cot[0], edge_cot[0]
    nodes, width = node.shape
    edges = edge.shape[0]
    halo = send_rows.shape[1]
    patches = lax.axis_size("patch")
    members = lax.axis_size("group")
    depth = patches // 8
    here = lax.axis_index("patch")
    place = jnp.stack([here % 2, here // (2 * depth), lax.axis_index("group")]).astype(jnp.int32)
    gain_edge = gain_edge.reshape(1, width)
    gain_node = gain_node.reshape(1, width)
    twins = [(i, i ^ 1) for i in range(patches)]
    column = 2 * depth
    lines = [[y * column + 2 * z + c for z in range(depth)] for y in range(4) for c in range(2)]
    unit = 2 * width * width

    def to_member(x, shift):
        return lax.ppermute(x, "group", [(g, (g + shift) % members) for g in range(members)])

    def to_column(x, shift):
        return lax.ppermute(x, "patch", [(i, (i + shift * column) % patches) for i in range(patches)])

    def along_depth(x, rows):
        return lax.all_to_all(
            x.reshape(depth, rows, width), "patch", 0, 0, axis_index_groups=lines, tiled=True
        )

    parts = edges // ROWS

    def wide(rows, kind=BF):
        return ((rows, width), kind, rows // ROWS)

    parts = edges // ROWS

    def wide(rows, kind=BF):
        return ((rows, width), kind, rows // ROWS)

    outgoing = call(
        outgoing_kernel,
        [((halo, width), BF)],
        [send_rows, node],
        flops=2 * halo * nodes * width,
        limit=16 * 2**20,
    )
    incoming = lax.all_to_all(outgoing, "patch", split_axis=0, concat_axis=0, tiled=True)
    node_turned, edge_turned, begun = call(
        own_kernel,
        [],
        [senders, receivers],
        [((edges, LANE), jnp.int32)] * 2,
        flops=7 * edges * unit,
        fetch=[node, edge, w_edge_in],
        store=[((width, nodes), BF, 1), ((width, edges), BF, 1), wide(edges, F32)],
        limit=FULL,
    )
    each = width // patches
    per_node, per_edge = 3 * each, 4 * each
    piece = ((4, depth * (per_node + per_edge) + 16, width), BF, 4)
    w_send = Part(w_edge_in, 1, width, width)
    node_acc, grad_first, from_send, from_recv, outward, send, keep = call(
        functools.partial(main_kernel, patches),
        [],
        [place, tile_count, senders, receivers, gain_edge, gain_node],
        [((edges, LANE), jnp.int32)] * 2
        + [((edges, width), BF)] * 3
        + [((edges, LANE), F32)]
        + [((edges, width), BF)]
        + [((nodes, width), BF)] * 5
        + [
            ((8, width), F32),
            ((2 * width, width), F32),
            ((width, width), F32),
            ((3 * width, width), F32),
            ((width, width), F32),
        ],
        scalars=2,
        flops=26 * nodes * unit,
        fetch=[
            incoming,
            w_send,
            Part(begun, parts),
            w_edge_out,
            node,
            w_node_in,
            w_node_out,
            Part(n_cot, nodes // ROWS),
            node_turned,
            Part(e_cot, parts),
            edge_turned,
        ],
        store=[
            wide(nodes),
            wide(edges),
            wide(nodes + halo),
            wide(nodes),
            ((halo, width), BF, 1),
            piece,
            piece,
        ],
        limit=FULL,
    )
    got = lax.ppermute(send, "patch", twins)
    sums = call(pair_kernel, [(keep.shape[1:], BF)] * 4, [keep, got])
    columns = [sums[0]] + [to_column(sums[s], s) for s in range(1, 4)]
    returned = lax.all_to_all(outward, "patch", split_axis=0, concat_axis=0, tiled=True)
    edge_grad, edge_token = call(
        edge_grad_kernel,
        [],
        [tile_count],
        scalars=1,
        flops=nodes * unit,
        fetch=[Part(w_edge_in, 1, 0, width), Part(grad_first, parts), Part(e_cot, parts)],
        store=[wide(edges), TOKEN],
        limit=FULL,
    )
    rows = per_node + per_edge + 8
    node_grad, node_token = call(
        node_grad_kernel,
        [],
        [send_rows],
        flops=3 * nodes * unit,
        fetch=[
            Part(w_edge_in, 1, width, 2 * width),
            returned,
            Part(node_acc, nodes // ROWS),
            Part(from_send, nodes // ROWS, 0, nodes),
            Part(from_recv, nodes // ROWS),
        ],
        store=[wide(nodes), TOKEN],
        limit=FULL,
    )
    blocks = call(
        functools.partial(four_kernel, (per_node, per_edge)),
        [((depth, rows, width), BF)],
        columns,
        after=[edge_token, node_token],
    )
    lines_got = along_depth(blocks, rows)
    mine = call(depth_kernel, [((rows, width), BF)], [lines_got])
    shared = [mine] + [to_member(mine, s) for s in range(1, 4)]
    factor = float(members * patches * edges) ** (-0.5)
    out_edge_in, out_edge_out, out_node_in, out_node_out, out_gain = call(
        functools.partial(finish_kernel, factor),
        [
            ((3 * each, width), F32),
            ((each, width), F32),
            ((2 * each, width), F32),
            ((each, width), F32),
            ((8, width), F32),
        ],
        [place] + shared,
        [((4, rows, width), F32)],
        scalars=1,
    )
    out_gain = lax.dynamic_slice(out_gain, (0, here * each), (2, each))
    return (
        edge_grad[None],
        node_grad[None],
        out_edge_in,
        out_edge_out,
        out_gain[0],
        out_node_in,
        out_node_out,
        out_gain[1],
    )


def solution(mesh):
    placed = (
        P("group", "patch", None),
        P("group", "patch", None),
        P("group", "patch", None),
        P("group", "patch", None),
        P(),
        P(),
        P(),
        P(),
        P(),
        P(),
        P("patch", None),
        P("patch", None),
        P("patch"),
        P("patch", None),
    )
    return jax.shard_map(
        local,
        mesh=mesh,
        in_specs=placed,
        out_specs=(
            P("group", "patch", None),
            P("group", "patch", None),
            P("patch", None),
            P("patch", None),
            P("patch"),
            P("patch", None),
            P("patch", None),
            P("patch"),
        ),
        check_vma=False,
    )
```

```python
import functools

import jax
import jax.numpy as jnp
from jax import lax
from jax.experimental import pallas as pl
from jax.experimental.pallas import tpu as pltpu
from jax.sharding import PartitionSpec as P

epsilon = 1e-05
BF = jnp.bfloat16
F32 = jnp.float32
LANE = 128
ROWS = 256
BIG = 1024
FULL = 60 * 2**20


def dot(a, b):
    return lax.dot_general(a, b, (((1,), (0,)), ((), ())), preferred_element_type=F32)


def dot_rt(a, b):
    return lax.dot_general(a, b, (((1,), (1,)), ((), ())), preferred_element_type=F32)


def dot_lt(a, b):
    return lax.dot_general(a, b, (((0,), (0,)), ((), ())), preferred_element_type=F32)


def iota(shape, dim):
    return lax.broadcasted_iota(jnp.int32, shape, dim)


def one_hot(mask):
    return jnp.where(mask, 1.0, 0.0).astype(BF)


def columns_of(index_ref, out_ref):
    tiles = index_ref.shape[0]
    full = jnp.concatenate(
        [index_ref[...], jnp.zeros((LANE - tiles, LANE), jnp.int32)], axis=0
    )
    turned = full.T
    for t in range(tiles):
        out_ref[t * LANE : (t + 1) * LANE, :] = jnp.broadcast_to(
            turned[:, t : t + 1], (LANE, LANE)
        )


def pick_rows(cols_ref, start, count, first, width):
    column = cols_ref[pl.ds(start, count), 0:1]
    return one_hot(column == iota((count, width), 1) + first)


def spread_rows(index_ref, start, count):
    tiles = index_ref.shape[0]
    base = iota((count, LANE), 0) + start
    return jnp.concatenate([one_hot(index_ref[t : t + 1, :] == base) for t in range(tiles)], axis=1)


def sigmoid(v):
    return 0.5 * jnp.tanh(0.5 * v) + 0.5


def live_rows(count_ref, start, count):
    return (iota((count, 1), 0) + start < count_ref[0] * LANE).astype(F32)


def normalize(values):
    centred = values - jnp.mean(values, axis=1, keepdims=True)
    inverse = lax.rsqrt(jnp.mean(centred * centred, axis=1, keepdims=True) + epsilon)
    return centred * inverse, inverse


def normalize_back(upstream, normed, inverse):
    return inverse * (
        upstream
        - jnp.mean(upstream, axis=1, keepdims=True)
        - normed * jnp.mean(upstream * normed, axis=1, keepdims=True)
    )


def loop(count, body, rows=ROWS):
    def step(i, carry):
        body(pl.multiple_of(i * rows, rows), i)
        return carry

    if count == rows:
        body(0, 0)
    else:
        lax.fori_loop(0, count // rows, step, 0)


def outgoing_kernel(rows_ref, node_ref, out_ref):
    nodes, halo = node_ref.shape[0], rows_ref.shape[1]
    spread = one_hot(rows_ref[...] == iota((nodes, halo), 0))
    out_ref[...] = dot_lt(spread, node_ref[...]).astype(BF)


def own_kernel(
    send_ref,
    recv_ref,
    node,
    edge,
    w_edge,
    node_turned,
    edge_turned,
    begun,
    send_cols,
    recv_cols,
):
    nodes, width = node.shape
    columns_of(send_ref, send_cols)
    columns_of(recv_ref, recv_cols)
    node_ref, edge_ref, w_ref = node.ready(), edge.ready(), w_edge.ready()

    def body(start, i):
        here = pl.ds(start, BIG)
        from_send = dot(pick_rows(send_cols, start, BIG, 0, nodes), node_ref[...]).astype(BF)
        from_recv = dot(pick_rows(recv_cols, start, BIG, 0, nodes), node_ref[...]).astype(BF)
        begun.buffer[here, :] = (
            dot(edge_ref[here, :], w_ref[0:width, :])
            + dot(from_send, w_ref[width : 2 * width, :])
            + dot(from_recv, w_ref[2 * width : 3 * width, :])
        )
        begun.send(i)

    loop(edge_ref.shape[0], body, BIG)
    for source, out in ((node_ref, node_turned), (edge_ref, edge_turned)):
        for i in range(0, source.shape[0], BIG):
            out.buffer[:, i : i + BIG] = source[i : i + BIG, :].T
        out.send(0)


def deal(place_ref, depth, pieces, first, send, keep):
    core, column = place_ref[0], place_ref[1]
    each = sum(rows for _, rows in pieces)
    batch = 1 if each % 16 == 0 else 2
    for which, out in ((1 - core, send), (core, keep)):

        def step(s, carry):
            for i in range(0, depth, batch):
                found = []
                for b in range(batch):
                    patch = (((column + s) % 4) * depth + i + b) * 2 + which
                    for ref, rows in pieces:
                        found.append(ref[pl.ds(pl.multiple_of(patch * rows, 8), rows), :])
                at = first + i * each
                out.buffer[s, at : at + batch * each, :] = jnp.concatenate(found, axis=0).astype(BF)
            return carry

        lax.fori_loop(0, 4, step, 0)


def main_kernel(
    patches,
    place_ref,
    count_ref,
    send_ref,
    recv_ref,
    gain_edge_ref,
    gain_node_ref,
    incoming,
    w_edge_send,
    begun,
    w_edge_out,
    node,
    w_node,
    w_node_out,
    node_cot,
    node_turned,
    edge_cot,
    edge_turned,
    node_acc,
    first_out,
    from_send,
    from_recv,
    outward,
    piece_send,
    piece_keep,
    send_cols,
    recv_cols,
    hidden_ref,
    slope_ref,
    normed_ref,
    inverse_ref,
    message,
    gathered,
    node_hidden,
    grad_second,
    grad_first,
    back_ref,
    gains,
    sum_in,
    sum_out,
    edge_sum_in,
    edge_sum_out,
):
    nodes, width = node.shape
    edges = begun.shape[0]
    halo = incoming.shape[0]
    columns_of(send_ref, send_cols)
    columns_of(recv_ref, recv_cols)
    halo_ref, w_send_ref, w_edge_out_ref = (
        incoming.ready(),
        w_edge_send.ready(),
        w_edge_out.ready(),
    )

    def edge_body(start, i):
        here = pl.ds(start, BIG)
        latent = dot(pick_rows(send_cols, start, BIG, nodes, halo), halo_ref[...])
        first = begun.part(i)[here, :] + dot(latent.astype(BF), w_send_ref[...])
        squash = sigmoid(first)
        hidden = (first * squash).astype(BF)
        hidden_ref[here, :] = hidden
        slope_ref[here, :] = (squash * (1.0 + first * (1.0 - squash))).astype(BF)
        normed, inverse = normalize(dot(hidden, w_edge_out_ref[...]))
        normed_ref[here, :] = normed.astype(BF)
        inverse_ref[here, :] = jnp.broadcast_to(inverse, (BIG, LANE))
        live = live_rows(count_ref, start, BIG)
        message[here, :] = (live * (gain_edge_ref[...] * normed)).astype(BF)

    loop(edges, edge_body, BIG)
    gains[...] = jnp.zeros_like(gains)
    node_ref, w_node_ref, w_node_out_ref = node.ready(), w_node.ready(), w_node_out.ready()

    def node_body(start, i):
        here = pl.ds(start, BIG)
        taken = dot(spread_rows(recv_ref, start, BIG), message[...]).astype(BF)
        gathered[here, :] = taken
        first = dot(node_ref[here, :], w_node_ref[0:width, :]) + dot(
            taken, w_node_ref[width : 2 * width, :]
        )
        squash = sigmoid(first)
        hidden = (first * squash).astype(BF)
        node_hidden[here, :] = hidden
        slope = squash * (1.0 + first * (1.0 - squash))
        normed, inverse = normalize(dot(hidden, w_node_out_ref[...]))
        upstream = node_cot.part(i)[here, :].astype(F32)
        gains[1:2, :] += jnp.sum(upstream * normed, axis=0, keepdims=True)
        second = normalize_back(upstream * gain_node_ref[...], normed, inverse).astype(BF)
        grad_second[here, :] = second
        grad = (dot_rt(second, w_node_out_ref[...]) * slope).astype(BF)
        grad_first[here, :] = grad
        node_acc.buffer[here, :] = (upstream + dot_rt(grad, w_node_ref[0:width, :])).astype(BF)
        back_ref[here, :] = dot_rt(grad, w_node_ref[width : 2 * width, :]).astype(BF)
        node_acc.send(i)

    loop(nodes, node_body, BIG)
    node_turned_ref = node_turned.ready()
    sum_out[...] = dot_lt(node_hidden[...], grad_second[...])
    sum_in[0:width, :] = dot(node_turned_ref[...], grad_first[...])
    sum_in[width : 2 * width, :] = dot_lt(gathered[...], grad_first[...])
    depth = patches // 8
    each = width // patches
    pieces = ((sum_in, 2 * each), (sum_out, each))
    deal(place_ref, depth, pieces, 0, piece_send, piece_keep)
    for s in range(4):
        piece_send.send(s)
        piece_keep.send(s)

    def back_body(start, i):
        here = pl.ds(start, BIG)
        live = live_rows(count_ref, start, BIG)
        taken = dot(pick_rows(recv_cols, start, BIG, 0, nodes), back_ref[...])
        arrived = live * (edge_cot.part(i)[here, :].astype(F32) + taken)
        normed = normed_ref[here, :].astype(F32)
        gains[0:1, :] += jnp.sum(arrived * normed, axis=0, keepdims=True)
        second = normalize_back(
            arrived * gain_edge_ref[...], normed, inverse_ref[here, 0:1]
        ).astype(BF)
        grad_second[here, :] = second
        first_out.buffer[here, :] = (
            dot_rt(second, w_edge_out_ref[...]) * slope_ref[here, :].astype(F32)
        ).astype(BF)
        first_out.send(i)

    loop(edges, back_body, BIG)
    first_ref = first_out.buffer
    for out, index_ref in ((from_send, send_ref), (from_recv, recv_ref)):

        def body(start, i):
            count = out.shape[0]
            out.buffer[pl.ds(start, count), :] = dot(
                spread_rows(index_ref, start, count), first_ref[...]
            ).astype(BF)
            out.send(i)

        loop(out.shape[0], body, out.shape[0])
    sent, received = from_send.buffer, from_recv.buffer
    outward.buffer[...] = dot_rt(sent[nodes : nodes + halo, :], w_send_ref[...]).astype(BF)
    outward.send(0)
    edge_sum_out[...] = dot_lt(hidden_ref[...], grad_second[...])
    edge_sum_in[0:width, :] = dot(edge_turned.ready()[...], first_ref[...])
    edge_sum_in[width : 2 * width, :] = dot(node_turned_ref[...], sent[0:nodes, :]) + dot_lt(
        halo_ref[...], sent[nodes : nodes + halo, :]
    )
    edge_sum_in[2 * width : 3 * width, :] = dot(node_turned_ref[...], received[...])
    extra = jnp.concatenate([gains[...], jnp.zeros((8, width), F32)], axis=0).astype(BF)
    rows = piece_keep.shape[1]
    for out in (piece_send, piece_keep):
        for s in range(4):
            out.buffer[s, rows - 16 : rows, :] = extra
    pieces = ((edge_sum_in, 3 * each), (edge_sum_out, each))
    deal(place_ref, depth, pieces, depth * 3 * each, piece_send, piece_keep)
    for s in range(4):
        piece_send.send(s + 4)
    for s in range(4):
        piece_keep.send(s + 4)


def edge_grad_kernel(count_ref, w_own, first, cot, edge_grad, token):
    token.buffer[...] = jnp.zeros(token.shape, F32)
    token.send(0)
    w_ref = w_own.ready()

    def edge_body(start, i):
        here = pl.ds(start, ROWS)
        live = live_rows(count_ref, start, ROWS)
        edge_grad.buffer[here, :] = (
            live * cot.part(i)[here, :].astype(F32) + dot_rt(first.part(i)[here, :], w_ref[...])
        ).astype(BF)
        edge_grad.send(i)

    loop(cot.shape[0], edge_body)


def node_grad_kernel(rows_ref, w_both, returned, acc, from_send, from_recv, out, token):
    token.buffer[...] = jnp.zeros(token.shape, F32)
    token.send(0)
    nodes, width = acc.shape
    halo = returned.shape[0]
    w_ref, returned_ref = w_both.ready(), returned.ready()

    def body(start, i):
        here = pl.ds(start, ROWS)
        spread = one_hot(rows_ref[...] == iota((ROWS, halo), 0) + start)
        out.buffer[here, :] = (
            acc.part(i)[here, :].astype(F32)
            + dot(spread, returned_ref[...])
            + dot_rt(from_send.part(i)[here, :], w_ref[0:width, :])
            + dot_rt(from_recv.part(i)[here, :], w_ref[width : 2 * width, :])
        ).astype(BF)
        out.send(i)

    loop(nodes, body)


def pair_kernel(keep_ref, got_ref, *outs):
    for s in range(4):
        outs[s][...] = (keep_ref[s].astype(F32) + got_ref[s].astype(F32)).astype(BF)


def four_kernel(counts, a, b, c, d, out_ref):
    total = a[...].astype(F32) + b[...].astype(F32) + c[...].astype(F32) + d[...].astype(F32)
    depth = out_ref.shape[0]
    last = total[depth * sum(counts) :][0:8]
    for z in range(depth):
        found, base = [], 0
        for rows in counts:
            found.append(total[base + z * rows : base + (z + 1) * rows])
            base += depth * rows
        out_ref[z] = jnp.concatenate(found + [last], axis=0).astype(BF)


def depth_kernel(got_ref, out_ref):
    total = got_ref[0].astype(F32)
    for i in range(1, got_ref.shape[0]):
        total = total + got_ref[i].astype(F32)
    out_ref[...] = total.astype(BF)


def finish_kernel(
    factor,
    place_ref,
    a,
    b,
    c,
    d,
    edge_in_ref,
    edge_out_ref,
    node_in_ref,
    node_out_ref,
    gain_ref,
    rows,
):
    member = place_ref[2]
    for s, ref in enumerate((a, b, c, d)):
        rows[(member - s + 4) % 4] = ref[...].astype(F32)
    total = ((rows[0] + rows[1]) + (rows[2] + rows[3])) * factor
    at = 0
    for out in (node_in_ref, node_out_ref, edge_in_ref, edge_out_ref, gain_ref):
        out[...] = total[at : at + out.shape[0], :]
        at += out.shape[0]


VM = pl.BlockSpec(memory_space=pltpu.VMEM)
SM = pl.BlockSpec(memory_space=pltpu.SMEM)

TOKEN = ((8, LANE), F32, 1)


class Moved:
    def __init__(self, far, buffer, semaphores, parts, first, outward, cuts=None):
        self.far, self.buffer, self.semaphores, self.cuts = far, buffer, semaphores, cuts
        self.parts, self.first, self.outward = parts, first, outward
        self.shape = buffer.shape
        self.step = buffer.shape[0] // parts

    def copy(self, i):
        if self.cuts is not None:
            lead, cut = i % self.shape[0], i // self.shape[0]
            rows = pl.ds(self.cuts[cut], self.cuts[cut + 1] - self.cuts[cut])
            return pltpu.make_async_copy(
                self.buffer.at[lead, rows], self.far.at[lead, rows], self.semaphores.at[i]
            )
        near = self.buffer.at[pl.ds(i * self.step, self.step)]
        far = self.far.at[pl.ds(self.first + i * self.step, self.step)]
        ends = (near, far) if self.outward else (far, near)
        return pltpu.make_async_copy(*ends, self.semaphores.at[i])

    def send(self, i):
        self.copy(i).start()

    def part(self, i):
        self.copy(i).wait()
        return self.buffer

    def ready(self):
        for i in range(self.parts):
            self.copy(i).wait()
        return self.buffer


class Part:
    def __init__(self, array, parts=1, first=0, rows=None):
        self.array, self.parts, self.first = array, parts, first
        self.rows = array.shape[0] if rows is None else rows


def call(kernel, outs, ins, scratch=(), scalars=0, flops=0, fetch=(), store=(), limit=None, after=()):
    ins = list(ins)
    fetch = [f if isinstance(f, Part) else Part(f) for f in fetch]
    shapes = [jax.ShapeDtypeStruct(s, d) for s, d in list(outs) + [o[:2] for o in store]]
    single = len(shapes) == 1
    buffers = [((f.rows, *f.array.shape[1:]), f.array.dtype) for f in fetch]
    size = sum(int(a.size) * a.dtype.itemsize for a in ins + shapes)
    held = list(scratch) + buffers + [o[:2] for o in store]
    bytes_here = sum(
        functools.reduce(lambda x, y: x * y, s) * jnp.dtype(d).itemsize for s, d in held
    )
    many, kept, given = len(fetch), len(store), len(outs)

    def take(refs, count):
        return refs[:count], refs[count:]

    def body(*refs):
        args, refs = take(refs, len(ins))
        _, refs = take(refs, len(after))
        sources, refs = take(refs, many)
        results, refs = take(refs, given)
        targets, refs = take(refs, kept)
        own, refs = take(refs, len(scratch))
        slots, refs = take(refs, many)
        rooms, refs = take(refs, kept)
        marks, ends = take(refs, many)
        arriving = [
            Moved(src, slot, mark, f.parts, f.first, False)
            for src, f, slot, mark in zip(sources, fetch, slots, marks)
        ]
        for one in arriving:
            for i in range(one.parts):
                one.send(i)
        leaving = [
            Moved(t, room, end, o[2], 0, True, *o[3:])
            for t, room, end, o in zip(targets, rooms, ends, store)
        ]
        kernel(*args, *arriving, *results, *leaving, *own)
        for one in leaving:
            one.ready()

    far = pl.BlockSpec(memory_space=pltpu.HBM)
    out_specs = [VM] * given + [far] * kept
    return pl.pallas_call(
        body,
        out_shape=shapes[0] if single else shapes,
        in_specs=[SM] * scalars
        + [VM] * (len(ins) - scalars)
        + [pl.BlockSpec(memory_space=pl.ANY)] * len(after)
        + [far] * many,
        out_specs=out_specs[0] if single else out_specs,
        scratch_shapes=[pltpu.VMEM(s, d) for s, d in held]
        + [pltpu.SemaphoreType.DMA((f.parts,)) for f in fetch]
        + [pltpu.SemaphoreType.DMA((o[2],)) for o in store],
        compiler_params=pltpu.CompilerParams(
            vmem_limit_bytes=bytes_here + 4 * 2**20 if limit is None else limit
        ),
        cost_estimate=pl.CostEstimate(flops=flops, bytes_accessed=size, transcendentals=0),
    )(*ins, *after, *[f.array for f in fetch])


def main_call(
    patches,
    piece,
    place,
    tile_count,
    senders,
    receivers,
    gain_edge,
    gain_node,
    incoming,
    begun,
    node,
    n_cot,
    node_turned,
    e_cot,
    edge_turned,
    w_edge_in,
    w_edge_out,
    w_node_in,
    w_node_out,
):
    nodes, width = node.shape
    edges, halo = e_cot.shape[0], incoming.shape[0]

    def wide(rows, kind=BF, step=ROWS):
        return ((rows, width), kind, rows // step)

    return call(
        functools.partial(main_kernel, patches),
        [],
        [place, tile_count, senders, receivers, gain_edge, gain_node],
        [((edges, LANE), jnp.int32)] * 2
        + [((edges, width), BF)] * 3
        + [((edges, LANE), F32)]
        + [((edges, width), BF)]
        + [((nodes, width), BF)] * 5
        + [
            ((8, width), F32),
            ((2 * width, width), F32),
            ((width, width), F32),
            ((3 * width, width), F32),
            ((width, width), F32),
        ],
        scalars=2,
        flops=52 * nodes * width * width,
        fetch=[
            incoming,
            Part(w_edge_in, 1, width, width),
            Part(begun, edges // BIG),
            w_edge_out,
            node,
            w_node_in,
            w_node_out,
            Part(n_cot, nodes // BIG),
            node_turned,
            Part(e_cot, edges // BIG),
            edge_turned,
        ],
        store=[
            wide(nodes, BF, BIG),
            wide(edges, BF, BIG),
            wide(nodes + halo, BF, nodes + halo),
            wide(nodes, BF, nodes),
            ((halo, width), BF, 1),
            piece,
            piece,
        ],
        limit=FULL,
    )


def local(
    node_tape,
    edge_tape,
    node_cot,
    edge_cot,
    w_edge_in,
    w_edge_out,
    gain_edge,
    w_node_in,
    w_node_out,
    gain_node,
    senders,
    receivers,
    tile_count,
    send_rows,
):
    node, edge = node_tape[0], edge_tape[0]
    n_cot, e_cot = node_cot[0], edge_cot[0]
    nodes, width = node.shape
    edges = edge.shape[0]
    halo = send_rows.shape[1]
    patches = lax.axis_size("patch")
    members = lax.axis_size("group")
    depth = patches // 8
    here = lax.axis_index("patch")
    place = jnp.stack([here % 2, here // (2 * depth), lax.axis_index("group")]).astype(jnp.int32)
    gain_edge = gain_edge.reshape(1, width)
    gain_node = gain_node.reshape(1, width)
    twins = [(i, i ^ 1) for i in range(patches)]
    column = 2 * depth
    lines = [[y * column + 2 * z + c for z in range(depth)] for y in range(4) for c in range(2)]
    unit = 2 * width * width

    def to_member(x, shift):
        return lax.ppermute(x, "group", [(g, (g + shift) % members) for g in range(members)])

    def to_column(x, shift):
        return lax.ppermute(x, "patch", [(i, (i + shift * column) % patches) for i in range(patches)])

    def along_depth(x, rows):
        return lax.all_to_all(
            x.reshape(depth, rows, width), "patch", 0, 0, axis_index_groups=lines, tiled=True
        )

    parts = edges // ROWS

    def wide(rows, kind=BF):
        return ((rows, width), kind, rows // ROWS)

    parts = edges // ROWS

    def wide(rows, kind=BF):
        return ((rows, width), kind, rows // ROWS)

    outgoing = call(
        outgoing_kernel,
        [((halo, width), BF)],
        [send_rows, node],
        flops=2 * halo * nodes * width,
        limit=16 * 2**20,
    )
    incoming = lax.all_to_all(outgoing, "patch", split_axis=0, concat_axis=0, tiled=True)
    node_turned, edge_turned, begun = call(
        own_kernel,
        [],
        [senders, receivers],
        [((edges, LANE), jnp.int32)] * 2,
        flops=7 * edges * unit,
        fetch=[node, edge, w_edge_in],
        store=[((width, nodes), BF, 1), ((width, edges), BF, 1), ((edges, width), F32, edges // BIG)],
        limit=FULL,
    )
    each = width // patches
    per_node, per_edge = 3 * each, 4 * each
    all_rows = depth * (per_node + per_edge) + 16
    piece = ((4, all_rows, width), BF, 8, (0, depth * per_node, all_rows))
    node_acc, grad_first, from_send, from_recv, outward, send, keep = main_call(
        patches,
        piece,
        place,
        tile_count,
        senders,
        receivers,
        gain_edge,
        gain_node,
        incoming,
        begun,
        node,
        n_cot,
        node_turned,
        e_cot,
        edge_turned,
        w_edge_in,
        w_edge_out,
        w_node_in,
        w_node_out,
    )
    got = lax.ppermute(send, "patch", twins)
    sums = call(pair_kernel, [(keep.shape[1:], BF)] * 4, [keep, got])
    columns = [sums[0]] + [to_column(sums[s], s) for s in range(1, 4)]
    returned = lax.all_to_all(outward, "patch", split_axis=0, concat_axis=0, tiled=True)
    edge_grad, edge_token = call(
        edge_grad_kernel,
        [],
        [tile_count],
        scalars=1,
        flops=nodes * unit,
        fetch=[Part(w_edge_in, 1, 0, width), Part(grad_first, parts), Part(e_cot, parts)],
        store=[wide(edges), TOKEN],
        limit=FULL,
    )
    rows = per_node + per_edge + 8
    blocks = call(
        functools.partial(four_kernel, (per_node, per_edge)),
        [((depth, rows, width), BF)],
        columns,
        flops=40 * nodes * unit,
        after=[],
    )
    lines_got = along_depth(blocks, rows)
    node_grad, node_token = call(
        node_grad_kernel,
        [],
        [send_rows],
        flops=3 * nodes * unit,
        fetch=[
            Part(w_edge_in, 1, width, 2 * width),
            returned,
            Part(node_acc, nodes // ROWS),
            Part(from_send, nodes // ROWS, 0, nodes),
            Part(from_recv, nodes // ROWS),
        ],
        store=[wide(nodes), TOKEN],
        limit=FULL,
        after=[edge_token],
    )
    mine = call(depth_kernel, [((rows, width), BF)], [lines_got], after=[node_token])
    shared = [mine] + [to_member(mine, s) for s in range(1, 4)]
    factor = float(members * patches * edges) ** (-0.5)
    out_edge_in, out_edge_out, out_node_in, out_node_out, out_gain = call(
        functools.partial(finish_kernel, factor),
        [
            ((3 * each, width), F32),
            ((each, width), F32),
            ((2 * each, width), F32),
            ((each, width), F32),
            ((8, width), F32),
        ],
        [place] + shared,
        [((4, rows, width), F32)],
        scalars=1,
    )
    out_gain = lax.dynamic_slice(out_gain, (0, here * each), (2, each))
    return (
        edge_grad[None],
        node_grad[None],
        out_edge_in,
        out_edge_out,
        out_gain[0],
        out_node_in,
        out_node_out,
        out_gain[1],
    )


def solution(mesh):
    placed = (
        P("group", "patch", None),
        P("group", "patch", None),
        P("group", "patch", None),
        P("group", "patch", None),
        P(),
        P(),
        P(),
        P(),
        P(),
        P(),
        P("patch", None),
        P("patch", None),
        P("patch"),
        P("patch", None),
    )
    return jax.shard_map(
        local,
        mesh=mesh,
        in_specs=placed,
        out_specs=(
            P("group", "patch", None),
            P("group", "patch", None),
            P("patch", None),
            P("patch", None),
            P("patch"),
            P("patch", None),
            P("patch", None),
            P("patch"),
        ),
        check_vma=False,
    )
```

```python
import functools

import jax
import jax.numpy as jnp
from jax import lax
from jax.experimental import pallas as pl
from jax.experimental.pallas import tpu as pltpu
from jax.sharding import PartitionSpec as P

epsilon = 1e-05
BF = jnp.bfloat16
F32 = jnp.float32
LANE = 128
ROWS = 256
BIG = 1024
FULL = 60 * 2**20


def dot(a, b):
    return lax.dot_general(a, b, (((1,), (0,)), ((), ())), preferred_element_type=F32)


def dot_rt(a, b):
    return lax.dot_general(a, b, (((1,), (1,)), ((), ())), preferred_element_type=F32)


def dot_lt(a, b):
    return lax.dot_general(a, b, (((0,), (0,)), ((), ())), preferred_element_type=F32)


def iota(shape, dim):
    return lax.broadcasted_iota(jnp.int32, shape, dim)


def one_hot(mask):
    return jnp.where(mask, 1.0, 0.0).astype(BF)


def columns_of(index_ref, out_ref):
    tiles = index_ref.shape[0]
    full = jnp.concatenate(
        [index_ref[...], jnp.zeros((LANE - tiles, LANE), jnp.int32)], axis=0
    )
    turned = full.T
    for t in range(tiles):
        out_ref[t * LANE : (t + 1) * LANE, :] = jnp.broadcast_to(
            turned[:, t : t + 1], (LANE, LANE)
        )


def pick_rows(cols_ref, start, count, first, width):
    column = cols_ref[pl.ds(start, count), 0:1]
    return one_hot(column == iota((count, width), 1) + first)


def spread_rows(index_ref, start, count):
    tiles = index_ref.shape[0]
    base = iota((count, LANE), 0) + start
    return jnp.concatenate([one_hot(index_ref[t : t + 1, :] == base) for t in range(tiles)], axis=1)


def sigmoid(v):
    return 0.5 * jnp.tanh(0.5 * v) + 0.5


def live_rows(count_ref, start, count):
    return (iota((count, 1), 0) + start < count_ref[0] * LANE).astype(F32)


def normalize(values):
    centred = values - jnp.mean(values, axis=1, keepdims=True)
    inverse = lax.rsqrt(jnp.mean(centred * centred, axis=1, keepdims=True) + epsilon)
    return centred * inverse, inverse


def normalize_back(upstream, normed, inverse):
    return inverse * (
        upstream
        - jnp.mean(upstream, axis=1, keepdims=True)
        - normed * jnp.mean(upstream * normed, axis=1, keepdims=True)
    )


def loop(count, body, rows=ROWS):
    def step(i, carry):
        body(pl.multiple_of(i * rows, rows), i)
        return carry

    if count == rows:
        body(0, 0)
    else:
        lax.fori_loop(0, count // rows, step, 0)


def outgoing_kernel(rows_ref, node_ref, out_ref):
    nodes, halo = node_ref.shape[0], rows_ref.shape[1]
    spread = one_hot(rows_ref[...] == iota((nodes, halo), 0))
    out_ref[...] = dot_lt(spread, node_ref[...]).astype(BF)


def own_kernel(
    send_ref,
    recv_ref,
    node,
    edge,
    w_edge,
    node_turned,
    edge_turned,
    begun,
    send_cols,
    recv_cols,
):
    nodes, width = node.shape
    columns_of(send_ref, send_cols)
    columns_of(recv_ref, recv_cols)
    node_ref, edge_ref, w_ref = node.ready(), edge.ready(), w_edge.ready()

    def body(start, i):
        here = pl.ds(start, BIG)
        from_send = dot(pick_rows(send_cols, start, BIG, 0, nodes), node_ref[...]).astype(BF)
        from_recv = dot(pick_rows(recv_cols, start, BIG, 0, nodes), node_ref[...]).astype(BF)
        begun.buffer[here, :] = (
            dot(edge_ref[here, :], w_ref[0:width, :])
            + dot(from_send, w_ref[width : 2 * width, :])
            + dot(from_recv, w_ref[2 * width : 3 * width, :])
        )
        begun.send(i)

    loop(edge_ref.shape[0], body, BIG)
    for source, out in ((node_ref, node_turned), (edge_ref, edge_turned)):
        for i in range(0, source.shape[0], BIG):
            out.buffer[:, i : i + BIG] = source[i : i + BIG, :].T
        out.send(0)


def deal(place_ref, depth, pieces, send, keep):
    core, column, member = place_ref[0], place_ref[1], place_ref[2]
    half = pieces[0][0].shape[1] // 2
    rows = sum(count for _, count in pieces)
    part = rows // 4
    for which, out in ((1 - core, send), (core, keep)):

        def step(s, carry):
            line = (column + s) % 4
            for z in range(depth):
                patch = (line * depth + z) * 2 + which
                found = []
                for ref, count in pieces:
                    if ref.shape[0] == count:
                        found.append(ref[...])
                    else:
                        found.append(ref[pl.ds(pl.multiple_of(patch * count, 8), count), :])
                block = jnp.concatenate(found, axis=0).astype(BF)
                out.buffer[s, z * rows : (z + 1) * rows, :] = block[:, 0:half]
                at = pl.multiple_of((s * depth + z) * part, 16)
                for x in range(4):
                    out.buffer[4 + (x - member + 4) % 4, pl.ds(at, part), :] = block[
                        x * part : (x + 1) * part, half:
                    ]
            out.send(s)
            return carry

        lax.fori_loop(0, 4, step, 0)
        for s in range(4, 8):
            out.send(s)


def main_kernel(
    patches,
    place_ref,
    count_ref,
    send_ref,
    recv_ref,
    gain_edge_ref,
    gain_node_ref,
    incoming,
    w_edge_send,
    begun,
    w_edge_out,
    node,
    w_node,
    w_node_out,
    node_cot,
    node_turned,
    edge_cot,
    edge_turned,
    node_acc,
    first_out,
    from_send,
    from_recv,
    outward,
    piece_send,
    piece_keep,
    send_cols,
    recv_cols,
    hidden_ref,
    slope_ref,
    normed_ref,
    inverse_ref,
    message,
    gathered,
    node_hidden,
    grad_second,
    grad_first,
    back_ref,
    gains,
    sum_in,
    sum_out,
    edge_sum_in,
    edge_sum_out,
):
    nodes, width = node.shape
    edges = begun.shape[0]
    halo = incoming.shape[0]
    columns_of(send_ref, send_cols)
    columns_of(recv_ref, recv_cols)
    halo_ref, w_send_ref, w_edge_out_ref = (
        incoming.ready(),
        w_edge_send.ready(),
        w_edge_out.ready(),
    )

    def edge_body(start, i):
        here = pl.ds(start, BIG)
        latent = dot(pick_rows(send_cols, start, BIG, nodes, halo), halo_ref[...])
        first = begun.part(i)[here, :] + dot(latent.astype(BF), w_send_ref[...])
        squash = sigmoid(first)
        hidden = (first * squash).astype(BF)
        hidden_ref[here, :] = hidden
        slope_ref[here, :] = (squash * (1.0 + first * (1.0 - squash))).astype(BF)
        normed, inverse = normalize(dot(hidden, w_edge_out_ref[...]))
        normed_ref[here, :] = normed.astype(BF)
        inverse_ref[here, :] = jnp.broadcast_to(inverse, (BIG, LANE))
        live = live_rows(count_ref, start, BIG)
        message[here, :] = (live * (gain_edge_ref[...] * normed)).astype(BF)

    loop(edges, edge_body, BIG)
    gains[...] = jnp.zeros_like(gains)
    node_ref, w_node_ref, w_node_out_ref = node.ready(), w_node.ready(), w_node_out.ready()

    def node_body(start, i):
        here = pl.ds(start, BIG)
        taken = dot(spread_rows(recv_ref, start, BIG), message[...]).astype(BF)
        gathered[here, :] = taken
        first = dot(node_ref[here, :], w_node_ref[0:width, :]) + dot(
            taken, w_node_ref[width : 2 * width, :]
        )
        squash = sigmoid(first)
        hidden = (first * squash).astype(BF)
        node_hidden[here, :] = hidden
        slope = squash * (1.0 + first * (1.0 - squash))
        normed, inverse = normalize(dot(hidden, w_node_out_ref[...]))
        upstream = node_cot.part(i)[here, :].astype(F32)
        gains[1:2, :] += jnp.sum(upstream * normed, axis=0, keepdims=True)
        second = normalize_back(upstream * gain_node_ref[...], normed, inverse).astype(BF)
        grad_second[here, :] = second
        grad = (dot_rt(second, w_node_out_ref[...]) * slope).astype(BF)
        grad_first[here, :] = grad
        node_acc.buffer[here, :] = (upstream + dot_rt(grad, w_node_ref[0:width, :])).astype(BF)
        back_ref[here, :] = dot_rt(grad, w_node_ref[width : 2 * width, :]).astype(BF)
        node_acc.send(i)

    loop(nodes, node_body, BIG)
    node_turned_ref = node_turned.ready()
    sum_out[...] = dot_lt(node_hidden[...], grad_second[...])
    sum_in[0:width, :] = dot(node_turned_ref[...], grad_first[...])
    sum_in[width : 2 * width, :] = dot_lt(gathered[...], grad_first[...])

    def back_body(start, i):
        here = pl.ds(start, BIG)
        live = live_rows(count_ref, start, BIG)
        taken = dot(pick_rows(recv_cols, start, BIG, 0, nodes), back_ref[...])
        arrived = live * (edge_cot.part(i)[here, :].astype(F32) + taken)
        normed = normed_ref[here, :].astype(F32)
        gains[0:1, :] += jnp.sum(arrived * normed, axis=0, keepdims=True)
        second = normalize_back(
            arrived * gain_edge_ref[...], normed, inverse_ref[here, 0:1]
        ).astype(BF)
        grad_second[here, :] = second
        first_out.buffer[here, :] = (
            dot_rt(second, w_edge_out_ref[...]) * slope_ref[here, :].astype(F32)
        ).astype(BF)
        first_out.send(i)

    loop(edges, back_body, BIG)
    first_ref = first_out.buffer
    for out, index_ref in ((from_send, send_ref), (from_recv, recv_ref)):

        def body(start, i):
            count = out.shape[0]
            out.buffer[pl.ds(start, count), :] = dot(
                spread_rows(index_ref, start, count), first_ref[...]
            ).astype(BF)
            out.send(i)

        loop(out.shape[0], body, out.shape[0])
    sent, received = from_send.buffer, from_recv.buffer
    outward.buffer[...] = dot_rt(sent[nodes : nodes + halo, :], w_send_ref[...]).astype(BF)
    outward.send(0)
    edge_sum_out[...] = dot_lt(hidden_ref[...], grad_second[...])
    edge_sum_in[0:width, :] = dot(edge_turned.ready()[...], first_ref[...])
    edge_sum_in[width : 2 * width, :] = dot(node_turned_ref[...], sent[0:nodes, :]) + dot_lt(
        halo_ref[...], sent[nodes : nodes + halo, :]
    )
    edge_sum_in[2 * width : 3 * width, :] = dot(node_turned_ref[...], received[...])
    each = width // patches
    pieces = (
        (sum_in, 2 * each),
        (sum_out, each),
        (edge_sum_in, 3 * each),
        (edge_sum_out, each),
        (gains, 8),
    )
    deal(place_ref, patches // 8, pieces, piece_send, piece_keep)


def edge_grad_kernel(count_ref, w_own, first, cot, edge_grad, token):
    token.buffer[...] = jnp.zeros(token.shape, F32)
    token.send(0)
    w_ref = w_own.ready()

    def edge_body(start, i):
        here = pl.ds(start, ROWS)
        live = live_rows(count_ref, start, ROWS)
        edge_grad.buffer[here, :] = (
            live * cot.part(i)[here, :].astype(F32) + dot_rt(first.part(i)[here, :], w_ref[...])
        ).astype(BF)
        edge_grad.send(i)

    loop(cot.shape[0], edge_body)


def node_grad_kernel(rows_ref, w_both, returned, acc, from_send, from_recv, out, token):
    token.buffer[...] = jnp.zeros(token.shape, F32)
    token.send(0)
    nodes, width = acc.shape
    halo = returned.shape[0]
    w_ref, returned_ref = w_both.ready(), returned.ready()

    def body(start, i):
        here = pl.ds(start, ROWS)
        spread = one_hot(rows_ref[...] == iota((ROWS, halo), 0) + start)
        out.buffer[here, :] = (
            acc.part(i)[here, :].astype(F32)
            + dot(spread, returned_ref[...])
            + dot_rt(from_send.part(i)[here, :], w_ref[0:width, :])
            + dot_rt(from_recv.part(i)[here, :], w_ref[width : 2 * width, :])
        ).astype(BF)
        out.send(i)

    loop(nodes, body)


def pair_kernel(keep_ref, got_ref, *outs):
    for s in range(8):
        outs[s][...] = (keep_ref[s].astype(F32) + got_ref[s].astype(F32)).astype(BF)


def sum_of(refs):
    a, b, c, d = [ref[...].astype(F32) for ref in refs]
    return (a + b) + (c + d)


def right_kernel(a, b, c, d, *outs):
    total = sum_of((a, b, c, d))
    rows = total.shape[0] // 4
    for s in range(4):
        outs[s][...] = total[s * rows : (s + 1) * rows].astype(BF)


def four_kernel(*refs):
    left, right, out = sum_of(refs[0:4]), sum_of(refs[4:8]), refs[8]
    depth = out.shape[0]
    many, few = left.shape[0] // depth, right.shape[0] // depth
    for z in range(depth):
        out[z] = jnp.concatenate(
            [left[z * many : (z + 1) * many], right[z * few : (z + 1) * few]], axis=0
        ).astype(BF)


def depth_kernel(got_ref, out_ref):
    total = got_ref[0].astype(F32)
    for i in range(1, got_ref.shape[0]):
        total = total + got_ref[i].astype(F32)
    out_ref[...] = total.astype(BF)


def finish_kernel(
    factor,
    place_ref,
    a,
    b,
    c,
    d,
    edge_in_ref,
    edge_out_ref,
    node_in_ref,
    node_out_ref,
    gain_ref,
    left,
    right,
):
    member = place_ref[2]
    rows, half = left.shape[1:]
    for s, ref in enumerate((a, b, c, d)):
        source = (member - s + 4) % 4
        values = ref[...].astype(F32)
        left[source] = values[0:rows]
        right[source] = values[rows : rows + right.shape[1]]
    total = ((left[0] + left[1]) + (left[2] + left[3])) * factor
    other = right[...].reshape(rows, half) * factor
    at = 0
    for out in (node_in_ref, node_out_ref, edge_in_ref, edge_out_ref, gain_ref):
        out[:, 0:half] = total[at : at + out.shape[0], :]
        out[:, half : 2 * half] = other[at : at + out.shape[0], :]
        at += out.shape[0]


VM = pl.BlockSpec(memory_space=pltpu.VMEM)
SM = pl.BlockSpec(memory_space=pltpu.SMEM)

TOKEN = ((8, LANE), F32, 1)


class Moved:
    def __init__(self, far, buffer, semaphores, parts, first, outward):
        self.far, self.buffer, self.semaphores = far, buffer, semaphores
        self.parts, self.first, self.outward = parts, first, outward
        self.shape = buffer.shape
        self.step = buffer.shape[0] // parts

    def copy(self, i):
        near = self.buffer.at[pl.ds(i * self.step, self.step)]
        far = self.far.at[pl.ds(self.first + i * self.step, self.step)]
        ends = (near, far) if self.outward else (far, near)
        return pltpu.make_async_copy(*ends, self.semaphores.at[i])

    def send(self, i):
        self.copy(i).start()

    def part(self, i):
        self.copy(i).wait()
        return self.buffer

    def ready(self):
        for i in range(self.parts):
            self.copy(i).wait()
        return self.buffer


class Part:
    def __init__(self, array, parts=1, first=0, rows=None):
        self.array, self.parts, self.first = array, parts, first
        self.rows = array.shape[0] if rows is None else rows


def call(kernel, outs, ins, scratch=(), scalars=0, flops=0, fetch=(), store=(), limit=None, after=()):
    ins = list(ins)
    fetch = [f if isinstance(f, Part) else Part(f) for f in fetch]
    shapes = [jax.ShapeDtypeStruct(s, d) for s, d in list(outs) + [o[:2] for o in store]]
    single = len(shapes) == 1
    buffers = [((f.rows, *f.array.shape[1:]), f.array.dtype) for f in fetch]
    size = sum(int(a.size) * a.dtype.itemsize for a in ins + shapes)
    held = list(scratch) + buffers + [o[:2] for o in store]
    bytes_here = sum(
        functools.reduce(lambda x, y: x * y, s) * jnp.dtype(d).itemsize for s, d in held
    )
    many, kept, given = len(fetch), len(store), len(outs)

    def take(refs, count):
        return refs[:count], refs[count:]

    def body(*refs):
        args, refs = take(refs, len(ins))
        _, refs = take(refs, len(after))
        sources, refs = take(refs, many)
        results, refs = take(refs, given)
        targets, refs = take(refs, kept)
        own, refs = take(refs, len(scratch))
        slots, refs = take(refs, many)
        rooms, refs = take(refs, kept)
        marks, ends = take(refs, many)
        arriving = [
            Moved(src, slot, mark, f.parts, f.first, False)
            for src, f, slot, mark in zip(sources, fetch, slots, marks)
        ]
        for one in arriving:
            for i in range(one.parts):
                one.send(i)
        leaving = [
            Moved(t, room, end, o[2], 0, True)
            for t, room, end, o in zip(targets, rooms, ends, store)
        ]
        kernel(*args, *arriving, *results, *leaving, *own)
        for one in leaving:
            one.ready()

    far = pl.BlockSpec(memory_space=pltpu.HBM)
    out_specs = [VM] * given + [far] * kept
    return pl.pallas_call(
        body,
        out_shape=shapes[0] if single else shapes,
        in_specs=[SM] * scalars
        + [VM] * (len(ins) - scalars)
        + [pl.BlockSpec(memory_space=pl.ANY)] * len(after)
        + [far] * many,
        out_specs=out_specs[0] if single else out_specs,
        scratch_shapes=[pltpu.VMEM(s, d) for s, d in held]
        + [pltpu.SemaphoreType.DMA((f.parts,)) for f in fetch]
        + [pltpu.SemaphoreType.DMA((o[2],)) for o in store],
        compiler_params=pltpu.CompilerParams(
            vmem_limit_bytes=bytes_here + 4 * 2**20 if limit is None else limit
        ),
        cost_estimate=pl.CostEstimate(flops=flops, bytes_accessed=size, transcendentals=0),
    )(*ins, *after, *[f.array for f in fetch])


def main_call(
    patches,
    piece,
    place,
    tile_count,
    senders,
    receivers,
    gain_edge,
    gain_node,
    incoming,
    begun,
    node,
    n_cot,
    node_turned,
    e_cot,
    edge_turned,
    w_edge_in,
    w_edge_out,
    w_node_in,
    w_node_out,
):
    nodes, width = node.shape
    edges, halo = e_cot.shape[0], incoming.shape[0]

    def wide(rows, kind=BF, step=ROWS):
        return ((rows, width), kind, rows // step)

    return call(
        functools.partial(main_kernel, patches),
        [],
        [place, tile_count, senders, receivers, gain_edge, gain_node],
        [((edges, LANE), jnp.int32)] * 2
        + [((edges, width), BF)] * 3
        + [((edges, LANE), F32)]
        + [((edges, width), BF)]
        + [((nodes, width), BF)] * 5
        + [
            ((8, width), F32),
            ((2 * width, width), F32),
            ((width, width), F32),
            ((3 * width, width), F32),
            ((width, width), F32),
        ],
        scalars=2,
        flops=52 * nodes * width * width,
        fetch=[
            incoming,
            Part(w_edge_in, 1, width, width),
            Part(begun, edges // BIG),
            w_edge_out,
            node,
            w_node_in,
            w_node_out,
            Part(n_cot, nodes // BIG),
            node_turned,
            Part(e_cot, edges // BIG),
            edge_turned,
        ],
        store=[
            wide(nodes, BF, BIG),
            wide(edges, BF, BIG),
            wide(nodes + halo, BF, nodes + halo),
            wide(nodes, BF, nodes),
            ((halo, width), BF, 1),
            piece,
            piece,
        ],
        limit=FULL,
    )


def local(
    node_tape,
    edge_tape,
    node_cot,
    edge_cot,
    w_edge_in,
    w_edge_out,
    gain_edge,
    w_node_in,
    w_node_out,
    gain_node,
    senders,
    receivers,
    tile_count,
    send_rows,
):
    node, edge = node_tape[0], edge_tape[0]
    n_cot, e_cot = node_cot[0], edge_cot[0]
    nodes, width = node.shape
    edges = edge.shape[0]
    halo = send_rows.shape[1]
    patches = lax.axis_size("patch")
    members = lax.axis_size("group")
    depth = patches // 8
    here = lax.axis_index("patch")
    place = jnp.stack([here % 2, here // (2 * depth), lax.axis_index("group")]).astype(jnp.int32)
    gain_edge = gain_edge.reshape(1, width)
    gain_node = gain_node.reshape(1, width)
    twins = [(i, i ^ 1) for i in range(patches)]
    column = 2 * depth
    lines = [[y * column + 2 * z + c for z in range(depth)] for y in range(4) for c in range(2)]
    unit = 2 * width * width

    def to_member(x, shift):
        return lax.ppermute(x, "group", [(g, (g + shift) % members) for g in range(members)])

    def to_column(x, shift):
        return lax.ppermute(x, "patch", [(i, (i + shift * column) % patches) for i in range(patches)])

    def along_depth(x):
        return lax.all_to_all(x, "patch", 0, 0, axis_index_groups=lines, tiled=True)

    parts = edges // ROWS

    def wide(rows, kind=BF):
        return ((rows, width), kind, rows // ROWS)

    parts = edges // ROWS

    def wide(rows, kind=BF):
        return ((rows, width), kind, rows // ROWS)

    outgoing = call(
        outgoing_kernel,
        [((halo, width), BF)],
        [send_rows, node],
        flops=2 * halo * nodes * width,
        limit=16 * 2**20,
    )
    incoming = lax.all_to_all(outgoing, "patch", split_axis=0, concat_axis=0, tiled=True)
    node_turned, edge_turned, begun = call(
        own_kernel,
        [],
        [senders, receivers],
        [((edges, LANE), jnp.int32)] * 2,
        flops=7 * edges * unit,
        fetch=[node, edge, w_edge_in],
        store=[((width, nodes), BF, 1), ((width, edges), BF, 1), ((edges, width), F32, edges // BIG)],
        limit=FULL,
    )
    each = width // patches
    rows, half = 8 * each, width // 2
    piece = ((8, depth * rows, half), BF, 8)
    node_acc, grad_first, from_send, from_recv, outward, send, keep = main_call(
        patches,
        piece,
        place,
        tile_count,
        senders,
        receivers,
        gain_edge,
        gain_node,
        incoming,
        begun,
        node,
        n_cot,
        node_turned,
        e_cot,
        edge_turned,
        w_edge_in,
        w_edge_out,
        w_node_in,
        w_node_out,
    )
    got = lax.ppermute(send, "patch", twins)
    sums = call(pair_kernel, [(keep.shape[1:], BF)] * 8, [keep, got])
    columns = [sums[0]] + [to_column(sums[s], s) for s in range(1, 4)]
    rights = call(
        right_kernel,
        [((depth * rows // 4, half), BF)] * 4,
        [sums[4]] + [to_member(sums[4 + s], s) for s in range(1, 4)],
    )
    columns += [rights[0]] + [to_column(rights[s], s) for s in range(1, 4)]
    returned = lax.all_to_all(outward, "patch", split_axis=0, concat_axis=0, tiled=True)
    edge_grad, edge_token = call(
        edge_grad_kernel,
        [],
        [tile_count],
        scalars=1,
        flops=nodes * unit,
        fetch=[Part(w_edge_in, 1, 0, width), Part(grad_first, parts), Part(e_cot, parts)],
        store=[wide(edges), TOKEN],
        limit=FULL,
    )
    blocks = call(
        four_kernel,
        [((depth, rows + rows // 4, half), BF)],
        columns,
        flops=8 * nodes * unit,
    )
    lines_got = along_depth(blocks)
    node_grad, node_token = call(
        node_grad_kernel,
        [],
        [send_rows],
        flops=3 * nodes * unit,
        fetch=[
            Part(w_edge_in, 1, width, 2 * width),
            returned,
            Part(node_acc, nodes // ROWS),
            Part(from_send, nodes // ROWS, 0, nodes),
            Part(from_recv, nodes // ROWS),
        ],
        store=[wide(nodes), TOKEN],
        limit=FULL,
        after=[edge_token],
    )
    mine = call(
        depth_kernel,
        [((rows + rows // 4, half), BF)],
        [lines_got],
        after=[node_token],
    )
    shared = [mine] + [to_member(mine, s) for s in range(1, 4)]
    factor = float(members * patches * edges) ** (-0.5)
    out_edge_in, out_edge_out, out_node_in, out_node_out, out_gain = call(
        functools.partial(finish_kernel, factor),
        [
            ((3 * each, width), F32),
            ((each, width), F32),
            ((2 * each, width), F32),
            ((each, width), F32),
            ((8, width), F32),
        ],
        [place] + shared,
        [((4, rows, half), F32), ((4, rows // 4, half), F32)],
        scalars=1,
    )
    out_gain = lax.dynamic_slice(out_gain, (0, here * each), (2, each))
    return (
        edge_grad[None],
        node_grad[None],
        out_edge_in,
        out_edge_out,
        out_gain[0],
        out_node_in,
        out_node_out,
        out_gain[1],
    )


def solution(mesh):
    placed = (
        P("group", "patch", None),
        P("group", "patch", None),
        P("group", "patch", None),
        P("group", "patch", None),
        P(),
        P(),
        P(),
        P(),
        P(),
        P(),
        P("patch", None),
        P("patch", None),
        P("patch"),
        P("patch", None),
    )
    return jax.shard_map(
        local,
        mesh=mesh,
        in_specs=placed,
        out_specs=(
            P("group", "patch", None),
            P("group", "patch", None),
            P("patch", None),
            P("patch", None),
            P("patch"),
            P("patch", None),
            P("patch", None),
            P("patch"),
        ),
        check_vma=False,
    )
```

```python
import functools

import jax
import jax.numpy as jnp
from jax import lax
from jax.experimental import pallas as pl
from jax.experimental.pallas import tpu as pltpu
from jax.sharding import PartitionSpec as P

epsilon = 1e-05
BF = jnp.bfloat16
F32 = jnp.float32
LANE = 128
ROWS = 256
BIG = 1024
FULL = 60 * 2**20


def dot(a, b):
    return lax.dot_general(a, b, (((1,), (0,)), ((), ())), preferred_element_type=F32)


def dot_rt(a, b):
    return lax.dot_general(a, b, (((1,), (1,)), ((), ())), preferred_element_type=F32)


def dot_lt(a, b):
    return lax.dot_general(a, b, (((0,), (0,)), ((), ())), preferred_element_type=F32)


def iota(shape, dim):
    return lax.broadcasted_iota(jnp.int32, shape, dim)


def one_hot(mask):
    return jnp.where(mask, 1.0, 0.0).astype(BF)


def columns_of(index_ref, out_ref):
    tiles = index_ref.shape[0]
    full = jnp.concatenate(
        [index_ref[...], jnp.zeros((LANE - tiles, LANE), jnp.int32)], axis=0
    )
    turned = full.T
    for t in range(tiles):
        out_ref[t * LANE : (t + 1) * LANE, :] = jnp.broadcast_to(
            turned[:, t : t + 1], (LANE, LANE)
        )


def pick_rows(cols_ref, start, count, first, width):
    column = cols_ref[pl.ds(start, count), 0:1]
    return one_hot(column == iota((count, width), 1) + first)


def spread_rows(index_ref, start, count):
    tiles = index_ref.shape[0]
    base = iota((count, LANE), 0) + start
    return jnp.concatenate([one_hot(index_ref[t : t + 1, :] == base) for t in range(tiles)], axis=1)


def sigmoid(v):
    return 0.5 * jnp.tanh(0.5 * v) + 0.5


def live_rows(count_ref, start, count):
    return (iota((count, 1), 0) + start < count_ref[0] * LANE).astype(F32)


def normalize(values):
    centred = values - jnp.mean(values, axis=1, keepdims=True)
    inverse = lax.rsqrt(jnp.mean(centred * centred, axis=1, keepdims=True) + epsilon)
    return centred * inverse, inverse


def normalize_back(upstream, normed, inverse):
    return inverse * (
        upstream
        - jnp.mean(upstream, axis=1, keepdims=True)
        - normed * jnp.mean(upstream * normed, axis=1, keepdims=True)
    )


def loop(count, body, rows=ROWS):
    def step(i, carry):
        body(pl.multiple_of(i * rows, rows), i)
        return carry

    if count == rows:
        body(0, 0)
    else:
        lax.fori_loop(0, count // rows, step, 0)


def outgoing_kernel(rows_ref, node_ref, out_ref):
    nodes, halo = node_ref.shape[0], rows_ref.shape[1]
    spread = one_hot(rows_ref[...] == iota((nodes, halo), 0))
    out_ref[...] = dot_lt(spread, node_ref[...]).reshape(out_ref.shape).astype(BF)


def own_kernel(
    send_ref,
    recv_ref,
    node,
    edge,
    w_edge,
    node_turned,
    edge_turned,
    begun,
    send_cols,
    recv_cols,
):
    nodes, width = node.shape
    columns_of(send_ref, send_cols)
    columns_of(recv_ref, recv_cols)
    node_ref, edge_ref, w_ref = node.ready(), edge.ready(), w_edge.ready()

    def body(start, i):
        here = pl.ds(start, BIG)
        from_send = dot(pick_rows(send_cols, start, BIG, 0, nodes), node_ref[...]).astype(BF)
        from_recv = dot(pick_rows(recv_cols, start, BIG, 0, nodes), node_ref[...]).astype(BF)
        begun.buffer[here, :] = (
            dot(edge_ref[here, :], w_ref[0:width, :])
            + dot(from_send, w_ref[width : 2 * width, :])
            + dot(from_recv, w_ref[2 * width : 3 * width, :])
        )
        begun.send(i)

    loop(edge_ref.shape[0], body, BIG)
    for source, out in ((node_ref, node_turned), (edge_ref, edge_turned)):
        for i in range(0, source.shape[0], BIG):
            out.buffer[:, i : i + BIG] = source[i : i + BIG, :].T
        out.send(0)


def deal(place_ref, depth, pieces, send, keep):
    core, column, member = place_ref[0], place_ref[1], place_ref[2]
    half = pieces[0][0].shape[1] // 2
    rows = sum(count for _, count in pieces)
    part = rows // 4
    for which, out in ((1 - core, send), (core, keep)):

        def step(s, carry):
            line = (column + s) % 4
            for z in range(depth):
                patch = (line * depth + z) * 2 + which
                found = []
                for ref, count in pieces:
                    if ref.shape[0] == count:
                        found.append(ref[...])
                    else:
                        found.append(ref[pl.ds(pl.multiple_of(patch * count, 8), count), :])
                block = jnp.concatenate(found, axis=0).astype(BF)
                out.buffer[s, z * rows : (z + 1) * rows, :] = block[:, 0:half]
                at = pl.multiple_of((s * depth + z) * part, 16)
                for x in range(4):
                    out.buffer[4 + (x - member + 4) % 4, pl.ds(at, part), :] = block[
                        x * part : (x + 1) * part, half:
                    ]
            out.send(s)
            return carry

        lax.fori_loop(0, 4, step, 0)
        for s in range(4, 8):
            out.send(s)


def main_kernel(
    patches,
    place_ref,
    count_ref,
    send_ref,
    recv_ref,
    gain_edge_ref,
    gain_node_ref,
    incoming,
    w_edge_send,
    begun,
    w_edge_out,
    node,
    w_node,
    w_node_out,
    node_cot,
    node_turned,
    edge_cot,
    edge_turned,
    node_acc,
    first_out,
    from_send,
    from_recv,
    outward,
    piece_send,
    piece_keep,
    send_cols,
    recv_cols,
    hidden_ref,
    slope_ref,
    normed_ref,
    inverse_ref,
    message,
    gathered,
    node_hidden,
    grad_second,
    grad_first,
    back_ref,
    gains,
    sum_in,
    sum_out,
    edge_sum_in,
    edge_sum_out,
):
    nodes, width = node.shape
    edges = begun.shape[0]
    halo = incoming.shape[0] * incoming.shape[1]
    columns_of(send_ref, send_cols)
    columns_of(recv_ref, recv_cols)
    halo_ref, w_send_ref, w_edge_out_ref = (
        incoming.ready()[...].astype(F32).reshape(halo, width).astype(BF),
        w_edge_send.ready(),
        w_edge_out.ready(),
    )

    def edge_body(start, i):
        here = pl.ds(start, BIG)
        latent = dot(pick_rows(send_cols, start, BIG, nodes, halo), halo_ref)
        first = begun.part(i)[here, :] + dot(latent.astype(BF), w_send_ref[...])
        squash = sigmoid(first)
        hidden = (first * squash).astype(BF)
        hidden_ref[here, :] = hidden
        slope_ref[here, :] = (squash * (1.0 + first * (1.0 - squash))).astype(BF)
        normed, inverse = normalize(dot(hidden, w_edge_out_ref[...]))
        normed_ref[here, :] = normed.astype(BF)
        inverse_ref[here, :] = jnp.broadcast_to(inverse, (BIG, LANE))
        live = live_rows(count_ref, start, BIG)
        message[here, :] = (live * (gain_edge_ref[...] * normed)).astype(BF)

    loop(edges, edge_body, BIG)
    gains[...] = jnp.zeros_like(gains)
    node_ref, w_node_ref, w_node_out_ref = node.ready(), w_node.ready(), w_node_out.ready()

    def node_body(start, i):
        here = pl.ds(start, BIG)
        taken = dot(spread_rows(recv_ref, start, BIG), message[...]).astype(BF)
        gathered[here, :] = taken
        first = dot(node_ref[here, :], w_node_ref[0:width, :]) + dot(
            taken, w_node_ref[width : 2 * width, :]
        )
        squash = sigmoid(first)
        hidden = (first * squash).astype(BF)
        node_hidden[here, :] = hidden
        slope = squash * (1.0 + first * (1.0 - squash))
        normed, inverse = normalize(dot(hidden, w_node_out_ref[...]))
        upstream = node_cot.part(i)[here, :].astype(F32)
        gains[1:2, :] += jnp.sum(upstream * normed, axis=0, keepdims=True)
        second = normalize_back(upstream * gain_node_ref[...], normed, inverse).astype(BF)
        grad_second[here, :] = second
        grad = (dot_rt(second, w_node_out_ref[...]) * slope).astype(BF)
        grad_first[here, :] = grad
        node_acc.buffer[here, :] = (upstream + dot_rt(grad, w_node_ref[0:width, :])).astype(BF)
        back_ref[here, :] = dot_rt(grad, w_node_ref[width : 2 * width, :]).astype(BF)
        node_acc.send(i)

    loop(nodes, node_body, BIG)
    node_turned_ref = node_turned.ready()
    sum_out[...] = dot_lt(node_hidden[...], grad_second[...])
    sum_in[0:width, :] = dot(node_turned_ref[...], grad_first[...])
    sum_in[width : 2 * width, :] = dot_lt(gathered[...], grad_first[...])

    def back_body(start, i):
        here = pl.ds(start, BIG)
        live = live_rows(count_ref, start, BIG)
        taken = dot(pick_rows(recv_cols, start, BIG, 0, nodes), back_ref[...])
        arrived = live * (edge_cot.part(i)[here, :].astype(F32) + taken)
        normed = normed_ref[here, :].astype(F32)
        gains[0:1, :] += jnp.sum(arrived * normed, axis=0, keepdims=True)
        second = normalize_back(
            arrived * gain_edge_ref[...], normed, inverse_ref[here, 0:1]
        ).astype(BF)
        grad_second[here, :] = second
        first_out.buffer[here, :] = (
            dot_rt(second, w_edge_out_ref[...]) * slope_ref[here, :].astype(F32)
        ).astype(BF)
        first_out.send(i)

    loop(edges, back_body, BIG)
    first_ref = first_out.buffer
    for out, index_ref in ((from_send, send_ref), (from_recv, recv_ref)):

        def body(start, i):
            count = out.shape[0]
            out.buffer[pl.ds(start, count), :] = dot(
                spread_rows(index_ref, start, count), first_ref[...]
            ).astype(BF)
            out.send(i)

        loop(out.shape[0], body, out.shape[0])
    sent, received = from_send.buffer, from_recv.buffer
    back = dot_rt(sent[nodes : nodes + halo, :], w_send_ref[...])
    outward.buffer[...] = back.reshape(outward.shape).astype(BF)
    outward.send(0)
    edge_sum_out[...] = dot_lt(hidden_ref[...], grad_second[...])
    edge_sum_in[0:width, :] = dot(edge_turned.ready()[...], first_ref[...])
    edge_sum_in[width : 2 * width, :] = dot(node_turned_ref[...], sent[0:nodes, :]) + dot_lt(
        halo_ref, sent[nodes : nodes + halo, :]
    )
    edge_sum_in[2 * width : 3 * width, :] = dot(node_turned_ref[...], received[...])
    each = width // patches
    pieces = (
        (sum_in, 2 * each),
        (sum_out, each),
        (edge_sum_in, 3 * each),
        (edge_sum_out, each),
        (gains, 8),
    )
    deal(place_ref, patches // 8, pieces, piece_send, piece_keep)


def edge_grad_kernel(count_ref, w_own, first, cot, edge_grad, token):
    token.buffer[...] = jnp.zeros(token.shape, F32)
    token.send(0)
    w_ref = w_own.ready()

    def edge_body(start, i):
        here = pl.ds(start, ROWS)
        live = live_rows(count_ref, start, ROWS)
        edge_grad.buffer[here, :] = (
            live * cot.part(i)[here, :].astype(F32) + dot_rt(first.part(i)[here, :], w_ref[...])
        ).astype(BF)
        edge_grad.send(i)

    loop(cot.shape[0], edge_body)


def node_grad_kernel(rows_ref, w_both, returned, acc, from_send, from_recv, out, token):
    token.buffer[...] = jnp.zeros(token.shape, F32)
    token.send(0)
    nodes, width = acc.shape
    halo = returned.shape[0] * returned.shape[1]
    w_ref = w_both.ready()
    returned_ref = returned.ready()[...].astype(F32).reshape(halo, width).astype(BF)

    def body(start, i):
        here = pl.ds(start, ROWS)
        spread = one_hot(rows_ref[...] == iota((ROWS, halo), 0) + start)
        out.buffer[here, :] = (
            acc.part(i)[here, :].astype(F32)
            + dot(spread, returned_ref)
            + dot_rt(from_send.part(i)[here, :], w_ref[0:width, :])
            + dot_rt(from_recv.part(i)[here, :], w_ref[width : 2 * width, :])
        ).astype(BF)
        out.send(i)

    loop(nodes, body)


def pair_kernel(keep_ref, got_ref, *outs):
    for s in range(8):
        outs[s][...] = (keep_ref[s].astype(F32) + got_ref[s].astype(F32)).astype(BF)


def sum_of(refs):
    a, b, c, d = [ref[...].astype(F32) for ref in refs]
    return (a + b) + (c + d)


def right_kernel(a, b, c, d, *outs):
    total = sum_of((a, b, c, d))
    rows = total.shape[0] // 4
    for s in range(4):
        outs[s][...] = total[s * rows : (s + 1) * rows].astype(BF)


def four_kernel(*refs):
    left, right, out = sum_of(refs[0:4]), sum_of(refs[4:8]), refs[8]
    depth = out.shape[0]
    many, few = left.shape[0] // depth, right.shape[0] // depth
    for z in range(depth):
        out[z] = jnp.concatenate(
            [left[z * many : (z + 1) * many], right[z * few : (z + 1) * few]], axis=0
        ).astype(BF)


def depth_kernel(got_ref, out_ref):
    total = got_ref[0].astype(F32)
    for i in range(1, got_ref.shape[0]):
        total = total + got_ref[i].astype(F32)
    out_ref[...] = total.astype(BF)


def finish_kernel(
    factor,
    place_ref,
    a,
    b,
    c,
    d,
    edge_in_ref,
    edge_out_ref,
    node_in_ref,
    node_out_ref,
    gain_ref,
    left,
    right,
):
    member = place_ref[2]
    rows, half = left.shape[1:]
    for s, ref in enumerate((a, b, c, d)):
        source = (member - s + 4) % 4
        values = ref[...].astype(F32)
        left[source] = values[0:rows]
        right[source] = values[rows : rows + right.shape[1]]
    total = ((left[0] + left[1]) + (left[2] + left[3])) * factor
    other = right[...].reshape(rows, half) * factor
    at = 0
    for out in (node_in_ref, node_out_ref, edge_in_ref, edge_out_ref, gain_ref):
        out[:, 0:half] = total[at : at + out.shape[0], :]
        out[:, half : 2 * half] = other[at : at + out.shape[0], :]
        at += out.shape[0]


VM = pl.BlockSpec(memory_space=pltpu.VMEM)
SM = pl.BlockSpec(memory_space=pltpu.SMEM)

TOKEN = ((8, LANE), F32, 1)


class Moved:
    def __init__(self, far, buffer, semaphores, parts, first, outward):
        self.far, self.buffer, self.semaphores = far, buffer, semaphores
        self.parts, self.first, self.outward = parts, first, outward
        self.shape = buffer.shape
        self.step = buffer.shape[0] // parts

    def copy(self, i):
        near = self.buffer.at[pl.ds(i * self.step, self.step)]
        far = self.far.at[pl.ds(self.first + i * self.step, self.step)]
        ends = (near, far) if self.outward else (far, near)
        return pltpu.make_async_copy(*ends, self.semaphores.at[i])

    def send(self, i):
        self.copy(i).start()

    def part(self, i):
        self.copy(i).wait()
        return self.buffer

    def ready(self):
        for i in range(self.parts):
            self.copy(i).wait()
        return self.buffer


class Part:
    def __init__(self, array, parts=1, first=0, rows=None):
        self.array, self.parts, self.first = array, parts, first
        self.rows = array.shape[0] if rows is None else rows


def call(kernel, outs, ins, scratch=(), scalars=0, flops=0, fetch=(), store=(), limit=None, after=()):
    ins = list(ins)
    fetch = [f if isinstance(f, Part) else Part(f) for f in fetch]
    shapes = [jax.ShapeDtypeStruct(s, d) for s, d in list(outs) + [o[:2] for o in store]]
    single = len(shapes) == 1
    buffers = [((f.rows, *f.array.shape[1:]), f.array.dtype) for f in fetch]
    size = sum(int(a.size) * a.dtype.itemsize for a in ins + shapes)
    held = list(scratch) + buffers + [o[:2] for o in store]
    bytes_here = sum(
        functools.reduce(lambda x, y: x * y, s) * jnp.dtype(d).itemsize for s, d in held
    )
    many, kept, given = len(fetch), len(store), len(outs)

    def take(refs, count):
        return refs[:count], refs[count:]

    def body(*refs):
        args, refs = take(refs, len(ins))
        _, refs = take(refs, len(after))
        sources, refs = take(refs, many)
        results, refs = take(refs, given)
        targets, refs = take(refs, kept)
        own, refs = take(refs, len(scratch))
        slots, refs = take(refs, many)
        rooms, refs = take(refs, kept)
        marks, ends = take(refs, many)
        arriving = [
            Moved(src, slot, mark, f.parts, f.first, False)
            for src, f, slot, mark in zip(sources, fetch, slots, marks)
        ]
        for one in arriving:
            for i in range(one.parts):
                one.send(i)
        leaving = [
            Moved(t, room, end, o[2], 0, True)
            for t, room, end, o in zip(targets, rooms, ends, store)
        ]
        kernel(*args, *arriving, *results, *leaving, *own)
        for one in leaving:
            one.ready()

    far = pl.BlockSpec(memory_space=pltpu.HBM)
    out_specs = [VM] * given + [far] * kept
    return pl.pallas_call(
        body,
        out_shape=shapes[0] if single else shapes,
        in_specs=[SM] * scalars
        + [VM] * (len(ins) - scalars)
        + [pl.BlockSpec(memory_space=pl.ANY)] * len(after)
        + [far] * many,
        out_specs=out_specs[0] if single else out_specs,
        scratch_shapes=[pltpu.VMEM(s, d) for s, d in held]
        + [pltpu.SemaphoreType.DMA((f.parts,)) for f in fetch]
        + [pltpu.SemaphoreType.DMA((o[2],)) for o in store],
        compiler_params=pltpu.CompilerParams(
            vmem_limit_bytes=bytes_here + 4 * 2**20 if limit is None else limit
        ),
        cost_estimate=pl.CostEstimate(flops=flops, bytes_accessed=size, transcendentals=0),
    )(*ins, *after, *[f.array for f in fetch])


def main_call(
    patches,
    piece,
    place,
    tile_count,
    senders,
    receivers,
    gain_edge,
    gain_node,
    incoming,
    begun,
    node,
    n_cot,
    node_turned,
    e_cot,
    edge_turned,
    w_edge_in,
    w_edge_out,
    w_node_in,
    w_node_out,
):
    nodes, width = node.shape
    edges, halo = e_cot.shape[0], incoming.shape[0] * incoming.shape[1]

    def wide(rows, kind=BF, step=ROWS):
        return ((rows, width), kind, rows // step)

    return call(
        functools.partial(main_kernel, patches),
        [],
        [place, tile_count, senders, receivers, gain_edge, gain_node],
        [((edges, LANE), jnp.int32)] * 2
        + [((edges, width), BF)] * 3
        + [((edges, LANE), F32)]
        + [((edges, width), BF)]
        + [((nodes, width), BF)] * 5
        + [
            ((8, width), F32),
            ((2 * width, width), F32),
            ((width, width), F32),
            ((3 * width, width), F32),
            ((width, width), F32),
        ],
        scalars=2,
        flops=52 * nodes * width * width,
        fetch=[
            incoming,
            Part(w_edge_in, 1, width, width),
            Part(begun, edges // BIG),
            w_edge_out,
            node,
            w_node_in,
            w_node_out,
            Part(n_cot, nodes // BIG),
            node_turned,
            Part(e_cot, edges // BIG),
            edge_turned,
        ],
        store=[
            wide(nodes, BF, BIG),
            wide(edges, BF, BIG),
            wide(nodes + halo, BF, nodes + halo),
            wide(nodes, BF, nodes),
            ((patches, halo // patches, width), BF, 1),
            piece,
            piece,
        ],
        limit=FULL,
    )


def local(
    node_tape,
    edge_tape,
    node_cot,
    edge_cot,
    w_edge_in,
    w_edge_out,
    gain_edge,
    w_node_in,
    w_node_out,
    gain_node,
    senders,
    receivers,
    tile_count,
    send_rows,
):
    node, edge = node_tape[0], edge_tape[0]
    n_cot, e_cot = node_cot[0], edge_cot[0]
    nodes, width = node.shape
    edges = edge.shape[0]
    halo = send_rows.shape[1]
    patches = lax.axis_size("patch")
    members = lax.axis_size("group")
    depth = patches // 8
    here = lax.axis_index("patch")
    place = jnp.stack([here % 2, here // (2 * depth), lax.axis_index("group")]).astype(jnp.int32)
    gain_edge = gain_edge.reshape(1, width)
    gain_node = gain_node.reshape(1, width)
    twins = [(i, i ^ 1) for i in range(patches)]
    column = 2 * depth
    lines = [[y * column + 2 * z + c for z in range(depth)] for y in range(4) for c in range(2)]
    unit = 2 * width * width

    def to_member(x, shift):
        return lax.ppermute(x, "group", [(g, (g + shift) % members) for g in range(members)])

    def to_column(x, shift):
        return lax.ppermute(x, "patch", [(i, (i + shift * column) % patches) for i in range(patches)])

    def along_depth(x):
        return lax.all_to_all(x, "patch", 0, 0, axis_index_groups=lines, tiled=True)

    parts = edges // ROWS

    def wide(rows, kind=BF):
        return ((rows, width), kind, rows // ROWS)

    parts = edges // ROWS

    def wide(rows, kind=BF):
        return ((rows, width), kind, rows // ROWS)

    outgoing = call(
        outgoing_kernel,
        [((patches, halo // patches, width), BF)],
        [send_rows, node],
        flops=2 * halo * nodes * width,
        limit=16 * 2**20,
    )
    incoming = lax.all_to_all(outgoing, "patch", split_axis=0, concat_axis=0, tiled=True)
    node_turned, edge_turned, begun = call(
        own_kernel,
        [],
        [senders, receivers],
        [((edges, LANE), jnp.int32)] * 2,
        flops=7 * edges * unit,
        fetch=[node, edge, w_edge_in],
        store=[((width, nodes), BF, 1), ((width, edges), BF, 1), ((edges, width), F32, edges // BIG)],
        limit=FULL,
    )
    each = width // patches
    rows, half = 8 * each, width // 2
    piece = ((8, depth * rows, half), BF, 8)
    node_acc, grad_first, from_send, from_recv, outward, send, keep = main_call(
        patches,
        piece,
        place,
        tile_count,
        senders,
        receivers,
        gain_edge,
        gain_node,
        incoming,
        begun,
        node,
        n_cot,
        node_turned,
        e_cot,
        edge_turned,
        w_edge_in,
        w_edge_out,
        w_node_in,
        w_node_out,
    )
    got = lax.ppermute(send, "patch", twins)
    edge_grad, edge_token = call(
        edge_grad_kernel,
        [],
        [tile_count],
        scalars=1,
        flops=nodes * unit,
        fetch=[Part(w_edge_in, 1, 0, width), Part(grad_first, parts), Part(e_cot, parts)],
        store=[wide(edges), TOKEN],
        limit=FULL,
    )
    sums = call(pair_kernel, [(keep.shape[1:], BF)] * 8, [keep, got], after=[edge_token])
    columns = [sums[0]] + [to_column(sums[s], s) for s in range(1, 4)]
    rights = call(
        right_kernel,
        [((depth * rows // 4, half), BF)] * 4,
        [sums[4]] + [to_member(sums[4 + s], s) for s in range(1, 4)],
    )
    columns += [rights[0]] + [to_column(rights[s], s) for s in range(1, 4)]
    returned = lax.all_to_all(outward, "patch", split_axis=0, concat_axis=0, tiled=True)
    blocks = call(
        four_kernel,
        [((depth, rows + rows // 4, half), BF)],
        columns,
        flops=8 * nodes * unit,
    )
    lines_got = along_depth(blocks)
    node_grad, node_token = call(
        node_grad_kernel,
        [],
        [send_rows],
        flops=3 * nodes * unit,
        fetch=[
            Part(w_edge_in, 1, width, 2 * width),
            returned,
            Part(node_acc, nodes // ROWS),
            Part(from_send, nodes // ROWS, 0, nodes),
            Part(from_recv, nodes // ROWS),
        ],
        store=[wide(nodes), TOKEN],
        limit=FULL,
    )
    mine = call(
        depth_kernel,
        [((rows + rows // 4, half), BF)],
        [lines_got],
        after=[node_token],
    )
    shared = [mine] + [to_member(mine, s) for s in range(1, 4)]
    factor = float(members * patches * edges) ** (-0.5)
    out_edge_in, out_edge_out, out_node_in, out_node_out, out_gain = call(
        functools.partial(finish_kernel, factor),
        [
            ((3 * each, width), F32),
            ((each, width), F32),
            ((2 * each, width), F32),
            ((each, width), F32),
            ((8, width), F32),
        ],
        [place] + shared,
        [((4, rows, half), F32), ((4, rows // 4, half), F32)],
        scalars=1,
    )
    out_gain = lax.dynamic_slice(out_gain, (0, here * each), (2, each))
    return (
        edge_grad[None],
        node_grad[None],
        out_edge_in,
        out_edge_out,
        out_gain[0],
        out_node_in,
        out_node_out,
        out_gain[1],
    )


def solution(mesh):
    placed = (
        P("group", "patch", None),
        P("group", "patch", None),
        P("group", "patch", None),
        P("group", "patch", None),
        P(),
        P(),
        P(),
        P(),
        P(),
        P(),
        P("patch", None),
        P("patch", None),
        P("patch"),
        P("patch", None),
    )
    return jax.shard_map(
        local,
        mesh=mesh,
        in_specs=placed,
        out_specs=(
            P("group", "patch", None),
            P("group", "patch", None),
            P("patch", None),
            P("patch", None),
            P("patch"),
            P("patch", None),
            P("patch", None),
            P("patch"),
        ),
        check_vma=False,
    )
```

```python
import functools

import jax
import jax.numpy as jnp
from jax import lax
from jax.experimental import pallas as pl
from jax.experimental.pallas import tpu as pltpu
from jax.sharding import PartitionSpec as P

epsilon = 1e-05
BF = jnp.bfloat16
F32 = jnp.float32
LANE = 128
ROWS = 256
BIG = 1024
FULL = 60 * 2**20


def dot(a, b):
    return lax.dot_general(a, b, (((1,), (0,)), ((), ())), preferred_element_type=F32)


def dot_rt(a, b):
    return lax.dot_general(a, b, (((1,), (1,)), ((), ())), preferred_element_type=F32)


def dot_lt(a, b):
    return lax.dot_general(a, b, (((0,), (0,)), ((), ())), preferred_element_type=F32)


def iota(shape, dim):
    return lax.broadcasted_iota(jnp.int32, shape, dim)


def one_hot(mask):
    return jnp.where(mask, 1.0, 0.0).astype(BF)


def columns_of(index_ref, out_ref):
    tiles = index_ref.shape[0]
    full = jnp.concatenate(
        [index_ref[...], jnp.zeros((LANE - tiles, LANE), jnp.int32)], axis=0
    )
    turned = full.T
    for t in range(tiles):
        out_ref[t * LANE : (t + 1) * LANE, :] = jnp.broadcast_to(
            turned[:, t : t + 1], (LANE, LANE)
        )


def pick_rows(cols_ref, start, count, first, width):
    column = cols_ref[pl.ds(start, count), 0:1]
    return one_hot(column == iota((count, width), 1) + first)


def spread_rows(index_ref, start, count):
    tiles = index_ref.shape[0]
    base = iota((count, LANE), 0) + start
    return jnp.concatenate([one_hot(index_ref[t : t + 1, :] == base) for t in range(tiles)], axis=1)


def sigmoid(v):
    return 0.5 * jnp.tanh(0.5 * v) + 0.5


def live_rows(count_ref, start, count):
    return (iota((count, 1), 0) + start < count_ref[0] * LANE).astype(F32)


def normalize(values):
    centred = values - jnp.mean(values, axis=1, keepdims=True)
    inverse = lax.rsqrt(jnp.mean(centred * centred, axis=1, keepdims=True) + epsilon)
    return centred * inverse, inverse


def normalize_back(upstream, normed, inverse):
    return inverse * (
        upstream
        - jnp.mean(upstream, axis=1, keepdims=True)
        - normed * jnp.mean(upstream * normed, axis=1, keepdims=True)
    )


def loop(count, body, rows=ROWS):
    def step(i, carry):
        body(pl.multiple_of(i * rows, rows), i)
        return carry

    if count == rows:
        body(0, 0)
    else:
        lax.fori_loop(0, count // rows, step, 0)


def outgoing_kernel(rows_ref, node_ref, out_ref):
    nodes, halo = node_ref.shape[0], rows_ref.shape[1]
    spread = one_hot(rows_ref[...] == iota((nodes, halo), 0))
    out_ref[...] = dot_lt(spread, node_ref[...]).reshape(out_ref.shape).astype(BF)


def own_kernel(
    send_ref,
    recv_ref,
    node,
    w_edge,
    edge,
    node_turned,
    edge_turned,
    begun,
    send_cols,
    recv_cols,
):
    nodes, width = node.shape
    columns_of(send_ref, send_cols)
    columns_of(recv_ref, recv_cols)
    node_ref = node.ready()

    def body(start, i):
        here = pl.ds(start, BIG)
        from_send = dot(pick_rows(send_cols, start, BIG, 0, nodes), node_ref[...]).astype(BF)
        from_recv = dot(pick_rows(recv_cols, start, BIG, 0, nodes), node_ref[...]).astype(BF)
        w_ref = w_edge.ready()
        found = dot(from_send, w_ref[width : 2 * width, :]) + dot(
            from_recv, w_ref[2 * width : 3 * width, :]
        )
        edge_ref = edge.ready()
        begun.buffer[here, :] = found + dot(edge_ref[here, :], w_ref[0:width, :])
        begun.send(i)

    loop(edge.shape[0], body, edge.shape[0])
    for source, out in ((node_ref, node_turned), (edge.buffer, edge_turned)):
        for i in range(0, source.shape[0], BIG):
            out.buffer[:, i : i + BIG] = source[i : i + BIG, :].T
        out.send(0)


def deal(place_ref, depth, pieces, send, keep):
    core, column, member = place_ref[0], place_ref[1], place_ref[2]
    half = pieces[0][0].shape[1] // 2
    rows = sum(count for _, count in pieces)
    part = rows // 4
    for which, out in ((1 - core, send), (core, keep)):

        def step(s, carry):
            line = (column + s) % 4
            for z in range(depth):
                patch = (line * depth + z) * 2 + which
                found = []
                for ref, count in pieces:
                    if ref.shape[0] == count:
                        found.append(ref[...])
                    else:
                        found.append(ref[pl.ds(pl.multiple_of(patch * count, 8), count), :])
                block = jnp.concatenate(found, axis=0).astype(BF)
                out.buffer[s, z * rows : (z + 1) * rows, :] = block[:, 0:half]
                at = pl.multiple_of((s * depth + z) * part, 16)
                for x in range(4):
                    out.buffer[4 + (x - member + 4) % 4, pl.ds(at, part), :] = block[
                        x * part : (x + 1) * part, half:
                    ]
            out.send(s)
            return carry

        lax.fori_loop(0, 4, step, 0)
        for s in range(4, 8):
            out.send(s)


def main_kernel(
    patches,
    place_ref,
    count_ref,
    send_ref,
    recv_ref,
    gain_edge_ref,
    gain_node_ref,
    incoming,
    w_edge_send,
    begun,
    w_edge_out,
    node,
    w_node,
    w_node_out,
    node_cot,
    node_turned,
    edge_cot,
    edge_turned,
    grad_first,
    first_out,
    from_send,
    from_recv,
    outward,
    piece_send,
    piece_keep,
    send_cols,
    recv_cols,
    hidden_ref,
    slope_ref,
    normed_ref,
    inverse_ref,
    message,
    gathered,
    node_hidden,
    grad_second,
    spread_recv,
    back_ref,
    gains,
    sum_in,
    sum_out,
    edge_sum_in,
    edge_sum_out,
):
    nodes, width = node.shape
    edges = begun.shape[0]
    halo = incoming.shape[0] * incoming.shape[1]
    columns_of(send_ref, send_cols)
    columns_of(recv_ref, recv_cols)
    halo_ref, w_send_ref, w_edge_out_ref = (
        incoming.ready()[...].astype(F32).reshape(halo, width).astype(BF),
        w_edge_send.ready(),
        w_edge_out.ready(),
    )

    def edge_body(start, i):
        here = pl.ds(start, BIG)
        latent = dot(pick_rows(send_cols, start, BIG, nodes, halo), halo_ref)
        more = dot(latent.astype(BF), w_send_ref[...])
        first = begun.part(i)[here, :] + more
        squash = sigmoid(first)
        hidden = (first * squash).astype(BF)
        hidden_ref[here, :] = hidden
        slope_ref[here, :] = (squash * (1.0 + first * (1.0 - squash))).astype(BF)
        normed, inverse = normalize(dot(hidden, w_edge_out_ref[...]))
        normed_ref[here, :] = normed.astype(BF)
        inverse_ref[here, :] = jnp.broadcast_to(inverse, (BIG, LANE))
        live = live_rows(count_ref, start, BIG)
        message[here, :] = (live * (gain_edge_ref[...] * normed)).astype(BF)

    loop(edges, edge_body, BIG)
    gains[...] = jnp.zeros_like(gains)
    node_ref, w_node_ref, w_node_out_ref = node.ready(), w_node.ready(), w_node_out.ready()

    def node_body(start, i):
        here = pl.ds(start, BIG)
        spread = spread_rows(recv_ref, start, BIG)
        spread_recv[here, :] = spread
        taken = dot(spread, message[...]).astype(BF)
        gathered[here, :] = taken
        first = dot(node_ref[here, :], w_node_ref[0:width, :]) + dot(
            taken, w_node_ref[width : 2 * width, :]
        )
        squash = sigmoid(first)
        hidden = (first * squash).astype(BF)
        node_hidden[here, :] = hidden
        slope = squash * (1.0 + first * (1.0 - squash))
        normed, inverse = normalize(dot(hidden, w_node_out_ref[...]))
        upstream = node_cot.part(i)[here, :].astype(F32)
        gains[1:2, :] += jnp.sum(upstream * normed, axis=0, keepdims=True)
        second = normalize_back(upstream * gain_node_ref[...], normed, inverse).astype(BF)
        grad_second[here, :] = second
        grad = (dot_rt(second, w_node_out_ref[...]) * slope).astype(BF)
        grad_first.buffer[here, :] = grad
        back_ref[here, :] = dot_rt(grad, w_node_ref[width : 2 * width, :]).astype(BF)
        grad_first.send(i)

    loop(nodes, node_body, BIG)
    node_turned_ref = node_turned.ready()
    sum_out[...] = dot_lt(node_hidden[...], grad_second[...])
    sum_in[0:width, :] = dot(node_turned_ref[...], grad_first.buffer[...])
    sum_in[width : 2 * width, :] = dot_lt(gathered[...], grad_first.buffer[...])

    def back_body(start, i):
        here = pl.ds(start, BIG)
        live = live_rows(count_ref, start, BIG)
        taken = dot(pick_rows(recv_cols, start, BIG, 0, nodes), back_ref[...])
        arrived = live * (edge_cot.part(i)[here, :].astype(F32) + taken)
        normed = normed_ref[here, :].astype(F32)
        gains[0:1, :] += jnp.sum(arrived * normed, axis=0, keepdims=True)
        second = normalize_back(
            arrived * gain_edge_ref[...], normed, inverse_ref[here, 0:1]
        ).astype(BF)
        grad_second[here, :] = second
        first_out.buffer[here, :] = (
            dot_rt(second, w_edge_out_ref[...]) * slope_ref[here, :].astype(F32)
        ).astype(BF)
        first_out.send(i)

    loop(edges, back_body, BIG)
    first_ref = first_out.buffer
    from_send.buffer[...] = dot(
        spread_rows(send_ref, 0, nodes + halo), first_ref[...]
    ).astype(BF)
    from_send.send(0)
    from_recv.buffer[...] = dot(spread_recv[...], first_ref[...]).astype(BF)
    from_recv.send(0)
    sent, received = from_send.buffer, from_recv.buffer
    back = dot_rt(sent[nodes : nodes + halo, :], w_send_ref[...])
    outward.buffer[...] = back.reshape(outward.shape).astype(BF)
    outward.send(0)
    edge_sum_out[...] = dot_lt(hidden_ref[...], grad_second[...])
    edge_sum_in[0:width, :] = dot(edge_turned.ready()[...], first_ref[...])
    edge_sum_in[width : 2 * width, :] = dot(node_turned_ref[...], sent[0:nodes, :]) + dot_lt(
        halo_ref, sent[nodes : nodes + halo, :]
    )
    edge_sum_in[2 * width : 3 * width, :] = dot(node_turned_ref[...], received[...])
    each = width // patches
    pieces = (
        (sum_in, 2 * each),
        (sum_out, each),
        (edge_sum_in, 3 * each),
        (edge_sum_out, each),
        (gains, 8),
    )
    deal(place_ref, patches // 8, pieces, piece_send, piece_keep)


def edge_grad_kernel(count_ref, w_own, first, cot, edge_grad, token):
    token.buffer[...] = jnp.zeros(token.shape, F32)
    token.send(0)
    w_ref = w_own.ready()

    def edge_body(start, i):
        here = pl.ds(start, ROWS)
        live = live_rows(count_ref, start, ROWS)
        edge_grad.buffer[here, :] = (
            live * cot.part(i)[here, :].astype(F32) + dot_rt(first.part(i)[here, :], w_ref[...])
        ).astype(BF)
        edge_grad.send(i)

    loop(cot.shape[0], edge_body)


def node_grad_kernel(
    rows_ref, w_node, first, cot, w_both, from_send, from_recv, returned, out, token
):
    token.buffer[...] = jnp.zeros(token.shape, F32)
    token.send(0)
    nodes, width = first.shape
    halo = returned.shape[0] * returned.shape[1]
    w_node_ref, w_ref = w_node.ready(), w_both.ready()
    returned_ref = returned.ready()[...].astype(F32).reshape(halo, width).astype(BF)

    def body(start, i):
        here = pl.ds(start, ROWS)
        spread = one_hot(rows_ref[...] == iota((ROWS, halo), 0) + start)
        out.buffer[here, :] = (
            cot.part(i)[here, :].astype(F32)
            + dot_rt(first.part(i)[here, :], w_node_ref[...])
            + dot(spread, returned_ref)
            + dot_rt(from_send.part(i)[here, :], w_ref[0:width, :])
            + dot_rt(from_recv.part(i)[here, :], w_ref[width : 2 * width, :])
        ).astype(BF)
        out.send(i)

    loop(nodes, body)


def pair_kernel(keep_ref, got_ref, *outs):
    for s in range(8):
        outs[s][...] = (keep_ref[s].astype(F32) + got_ref[s].astype(F32)).astype(BF)


def sum_of(refs):
    a, b, c, d = [ref[...].astype(F32) for ref in refs]
    return (a + b) + (c + d)


def right_kernel(a, b, c, d, *outs):
    total = sum_of((a, b, c, d))
    rows = total.shape[0] // 4
    for s in range(4):
        outs[s][...] = total[s * rows : (s + 1) * rows].astype(BF)


def four_kernel(*refs):
    left, right, out = sum_of(refs[0:4]), sum_of(refs[4:8]), refs[8]
    depth = out.shape[0]
    many, few = left.shape[0] // depth, right.shape[0] // depth
    for z in range(depth):
        out[z] = jnp.concatenate(
            [left[z * many : (z + 1) * many], right[z * few : (z + 1) * few]], axis=0
        ).astype(BF)


def depth_kernel(got_ref, out_ref):
    total = got_ref[0].astype(F32)
    for i in range(1, got_ref.shape[0]):
        total = total + got_ref[i].astype(F32)
    out_ref[...] = total.astype(BF)


def finish_kernel(
    factor,
    place_ref,
    a,
    b,
    c,
    d,
    edge_in_ref,
    edge_out_ref,
    node_in_ref,
    node_out_ref,
    gain_ref,
    left,
    right,
):
    member = place_ref[2]
    rows, half = left.shape[1:]
    for s, ref in enumerate((a, b, c, d)):
        source = (member - s + 4) % 4
        values = ref[...].astype(F32)
        left[source] = values[0:rows]
        right[source] = values[rows : rows + right.shape[1]]
    total = ((left[0] + left[1]) + (left[2] + left[3])) * factor
    other = right[...].reshape(rows, half) * factor
    at = 0
    for out in (node_in_ref, node_out_ref, edge_in_ref, edge_out_ref, gain_ref):
        out[:, 0:half] = total[at : at + out.shape[0], :]
        out[:, half : 2 * half] = other[at : at + out.shape[0], :]
        at += out.shape[0]


VM = pl.BlockSpec(memory_space=pltpu.VMEM)
SM = pl.BlockSpec(memory_space=pltpu.SMEM)

TOKEN = ((8, LANE), F32, 1)


class Moved:
    def __init__(self, far, buffer, semaphores, parts, first, outward):
        self.far, self.buffer, self.semaphores = far, buffer, semaphores
        self.parts, self.first, self.outward = parts, first, outward
        self.shape = buffer.shape
        self.step = buffer.shape[0] // parts

    def copy(self, i):
        near = self.buffer.at[pl.ds(i * self.step, self.step)]
        far = self.far.at[pl.ds(self.first + i * self.step, self.step)]
        ends = (near, far) if self.outward else (far, near)
        return pltpu.make_async_copy(*ends, self.semaphores.at[i])

    def send(self, i):
        self.copy(i).start()

    def part(self, i):
        self.copy(i).wait()
        return self.buffer

    def ready(self):
        for i in range(self.parts):
            self.copy(i).wait()
        return self.buffer


class Part:
    def __init__(self, array, parts=1, first=0, rows=None):
        self.array, self.parts, self.first = array, parts, first
        self.rows = array.shape[0] if rows is None else rows


def call(kernel, outs, ins, scratch=(), scalars=0, flops=0, fetch=(), store=(), limit=None, after=()):
    ins = list(ins)
    fetch = [f if isinstance(f, Part) else Part(f) for f in fetch]
    shapes = [jax.ShapeDtypeStruct(s, d) for s, d in list(outs) + [o[:2] for o in store]]
    single = len(shapes) == 1
    buffers = [((f.rows, *f.array.shape[1:]), f.array.dtype) for f in fetch]
    size = sum(int(a.size) * a.dtype.itemsize for a in ins + shapes)
    held = list(scratch) + buffers + [o[:2] for o in store]
    bytes_here = sum(
        functools.reduce(lambda x, y: x * y, s) * jnp.dtype(d).itemsize for s, d in held
    )
    many, kept, given = len(fetch), len(store), len(outs)

    def take(refs, count):
        return refs[:count], refs[count:]

    def body(*refs):
        args, refs = take(refs, len(ins))
        _, refs = take(refs, len(after))
        sources, refs = take(refs, many)
        results, refs = take(refs, given)
        targets, refs = take(refs, kept)
        own, refs = take(refs, len(scratch))
        slots, refs = take(refs, many)
        rooms, refs = take(refs, kept)
        marks, ends = take(refs, many)
        arriving = [
            Moved(src, slot, mark, f.parts, f.first, False)
            for src, f, slot, mark in zip(sources, fetch, slots, marks)
        ]
        for one in arriving:
            for i in range(one.parts):
                one.send(i)
        leaving = [
            Moved(t, room, end, o[2], 0, True)
            for t, room, end, o in zip(targets, rooms, ends, store)
        ]
        kernel(*args, *arriving, *results, *leaving, *own)
        for one in leaving:
            one.ready()

    far = pl.BlockSpec(memory_space=pltpu.HBM)
    out_specs = [VM] * given + [far] * kept
    return pl.pallas_call(
        body,
        out_shape=shapes[0] if single else shapes,
        in_specs=[SM] * scalars
        + [VM] * (len(ins) - scalars)
        + [pl.BlockSpec(memory_space=pl.ANY)] * len(after)
        + [far] * many,
        out_specs=out_specs[0] if single else out_specs,
        scratch_shapes=[pltpu.VMEM(s, d) for s, d in held]
        + [pltpu.SemaphoreType.DMA((f.parts,)) for f in fetch]
        + [pltpu.SemaphoreType.DMA((o[2],)) for o in store],
        compiler_params=pltpu.CompilerParams(
            vmem_limit_bytes=bytes_here + 4 * 2**20 if limit is None else limit
        ),
        cost_estimate=pl.CostEstimate(flops=flops, bytes_accessed=size, transcendentals=0),
    )(*ins, *after, *[f.array for f in fetch])


def main_call(
    patches,
    piece,
    place,
    tile_count,
    senders,
    receivers,
    gain_edge,
    gain_node,
    incoming,
    begun,
    node,
    n_cot,
    node_turned,
    e_cot,
    edge_turned,
    w_edge_in,
    w_edge_out,
    w_node_in,
    w_node_out,
):
    nodes, width = node.shape
    edges, halo = e_cot.shape[0], incoming.shape[0] * incoming.shape[1]

    def wide(rows, kind=BF, step=ROWS):
        return ((rows, width), kind, rows // step)

    return call(
        functools.partial(main_kernel, patches),
        [],
        [place, tile_count, senders, receivers, gain_edge, gain_node],
        [((edges, LANE), jnp.int32)] * 2
        + [((edges, width), BF)] * 3
        + [((edges, LANE), F32)]
        + [((edges, width), BF)]
        + [((nodes, width), BF)] * 3
        + [((nodes, edges), BF), ((nodes, width), BF)]
        + [
            ((8, width), F32),
            ((2 * width, width), F32),
            ((width, width), F32),
            ((3 * width, width), F32),
            ((width, width), F32),
        ],
        scalars=2,
        flops=52 * nodes * width * width,
        fetch=[
            incoming,
            Part(w_edge_in, 1, width, width),
            Part(begun, edges // BIG),
            w_edge_out,
            node,
            w_node_in,
            w_node_out,
            Part(n_cot, nodes // BIG),
            node_turned,
            Part(e_cot, edges // BIG),
            edge_turned,
        ],
        store=[
            wide(nodes, BF, BIG),
            wide(edges, BF, BIG),
            wide(nodes + halo, BF, nodes + halo),
            wide(nodes, BF, nodes),
            ((patches, halo // patches, width), BF, 1),
            piece,
            piece,
        ],
        limit=FULL,
    )


def local(
    node_tape,
    edge_tape,
    node_cot,
    edge_cot,
    w_edge_in,
    w_edge_out,
    gain_edge,
    w_node_in,
    w_node_out,
    gain_node,
    senders,
    receivers,
    tile_count,
    send_rows,
):
    node, edge = node_tape[0], edge_tape[0]
    n_cot, e_cot = node_cot[0], edge_cot[0]
    nodes, width = node.shape
    edges = edge.shape[0]
    halo = send_rows.shape[1]
    patches = lax.axis_size("patch")
    members = lax.axis_size("group")
    depth = patches // 8
    here = lax.axis_index("patch")
    place = jnp.stack([here % 2, here // (2 * depth), lax.axis_index("group")]).astype(jnp.int32)
    gain_edge = gain_edge.reshape(1, width)
    gain_node = gain_node.reshape(1, width)
    twins = [(i, i ^ 1) for i in range(patches)]
    column = 2 * depth
    lines = [[y * column + 2 * z + c for z in range(depth)] for y in range(4) for c in range(2)]
    unit = 2 * width * width

    def to_member(x, shift):
        return lax.ppermute(x, "group", [(g, (g + shift) % members) for g in range(members)])

    def to_column(x, shift):
        return lax.ppermute(x, "patch", [(i, (i + shift * column) % patches) for i in range(patches)])

    def along_depth(x):
        return lax.all_to_all(x, "patch", 0, 0, axis_index_groups=lines, tiled=True)

    parts = edges // ROWS

    def wide(rows, kind=BF):
        return ((rows, width), kind, rows // ROWS)

    parts = edges // ROWS

    def wide(rows, kind=BF):
        return ((rows, width), kind, rows // ROWS)

    outgoing = call(
        outgoing_kernel,
        [((patches, halo // patches, width), BF)],
        [send_rows, node],
        flops=2 * halo * nodes * width,
        limit=16 * 2**20,
    )
    incoming = lax.all_to_all(outgoing, "patch", split_axis=0, concat_axis=0, tiled=True)
    node_turned, edge_turned, begun = call(
        own_kernel,
        [],
        [senders, receivers],
        [((edges, LANE), jnp.int32)] * 2,
        flops=7 * edges * unit,
        fetch=[node, w_edge_in, edge],
        store=[((width, nodes), BF, 1), ((width, edges), BF, 1), ((edges, width), F32, edges // BIG)],
        limit=FULL,
    )
    each = width // patches
    rows, half = 8 * each, width // 2
    piece = ((8, depth * rows, half), BF, 8)
    node_first, grad_first, from_send, from_recv, outward, send, keep = main_call(
        patches,
        piece,
        place,
        tile_count,
        senders,
        receivers,
        gain_edge,
        gain_node,
        incoming,
        begun,
        node,
        n_cot,
        node_turned,
        e_cot,
        edge_turned,
        w_edge_in,
        w_edge_out,
        w_node_in,
        w_node_out,
    )
    got = lax.ppermute(send, "patch", twins)
    edge_grad, edge_token = call(
        edge_grad_kernel,
        [],
        [tile_count],
        scalars=1,
        flops=nodes * unit,
        fetch=[Part(w_edge_in, 1, 0, width), Part(grad_first, parts), Part(e_cot, parts)],
        store=[wide(edges), TOKEN],
        limit=FULL,
    )
    sums = call(pair_kernel, [(keep.shape[1:], BF)] * 8, [keep, got], after=[edge_token])
    columns = [sums[0]] + [to_column(sums[s], s) for s in range(1, 4)]
    rights = call(
        right_kernel,
        [((depth * rows // 4, half), BF)] * 4,
        [sums[4]] + [to_member(sums[4 + s], s) for s in range(1, 4)],
    )
    columns += [rights[0]] + [to_column(rights[s], s) for s in range(1, 4)]
    returned = lax.all_to_all(outward, "patch", split_axis=0, concat_axis=0, tiled=True)
    blocks = call(
        four_kernel,
        [((depth, rows + rows // 4, half), BF)],
        columns,
        flops=8 * nodes * unit,
    )
    lines_got = along_depth(blocks)
    node_grad, node_token = call(
        node_grad_kernel,
        [],
        [send_rows],
        flops=3 * nodes * unit,
        fetch=[
            Part(w_node_in, 1, 0, width),
            Part(node_first, nodes // ROWS),
            Part(n_cot, nodes // ROWS),
            Part(w_edge_in, 1, width, 2 * width),
            Part(from_send, nodes // ROWS, 0, nodes),
            Part(from_recv, nodes // ROWS),
            returned,
        ],
        store=[wide(nodes), TOKEN],
        limit=FULL,
    )
    mine = call(
        depth_kernel,
        [((rows + rows // 4, half), BF)],
        [lines_got],
        after=[node_token],
    )
    shared = [mine] + [to_member(mine, s) for s in range(1, 4)]
    factor = float(members * patches * edges) ** (-0.5)
    out_edge_in, out_edge_out, out_node_in, out_node_out, out_gain = call(
        functools.partial(finish_kernel, factor),
        [
            ((3 * each, width), F32),
            ((each, width), F32),
            ((2 * each, width), F32),
            ((each, width), F32),
            ((8, width), F32),
        ],
        [place] + shared,
        [((4, rows, half), F32), ((4, rows // 4, half), F32)],
        scalars=1,
    )
    out_gain = lax.dynamic_slice(out_gain, (0, here * each), (2, each))
    return (
        edge_grad[None],
        node_grad[None],
        out_edge_in,
        out_edge_out,
        out_gain[0],
        out_node_in,
        out_node_out,
        out_gain[1],
    )


def solution(mesh):
    placed = (
        P("group", "patch", None),
        P("group", "patch", None),
        P("group", "patch", None),
        P("group", "patch", None),
        P(),
        P(),
        P(),
        P(),
        P(),
        P(),
        P("patch", None),
        P("patch", None),
        P("patch"),
        P("patch", None),
    )
    return jax.shard_map(
        local,
        mesh=mesh,
        in_specs=placed,
        out_specs=(
            P("group", "patch", None),
            P("group", "patch", None),
            P("patch", None),
            P("patch", None),
            P("patch"),
            P("patch", None),
            P("patch", None),
            P("patch"),
        ),
        check_vma=False,
    )
```

```python
import functools

import jax
import jax.numpy as jnp
from jax import lax
from jax.experimental import pallas as pl
from jax.experimental.pallas import tpu as pltpu
from jax.sharding import PartitionSpec as P

epsilon = 1e-05
BF = jnp.bfloat16
F32 = jnp.float32
LANE = 128
ROWS = 256
BIG = 1024
FULL = 60 * 2**20


def dot(a, b):
    return lax.dot_general(a, b, (((1,), (0,)), ((), ())), preferred_element_type=F32)


def dot_rt(a, b):
    return lax.dot_general(a, b, (((1,), (1,)), ((), ())), preferred_element_type=F32)


def dot_lt(a, b):
    return lax.dot_general(a, b, (((0,), (0,)), ((), ())), preferred_element_type=F32)


def iota(shape, dim):
    return lax.broadcasted_iota(jnp.int32, shape, dim)


def one_hot(mask):
    return jnp.where(mask, 1.0, 0.0).astype(BF)


def columns_of(index_ref, out_ref):
    tiles = index_ref.shape[0]
    full = jnp.concatenate(
        [index_ref[...], jnp.zeros((LANE - tiles, LANE), jnp.int32)], axis=0
    )
    turned = full.T
    for t in range(tiles):
        out_ref[t * LANE : (t + 1) * LANE, :] = jnp.broadcast_to(
            turned[:, t : t + 1], (LANE, LANE)
        )


def pick_rows(cols_ref, start, count, first, width):
    column = cols_ref[pl.ds(start, count), 0:1]
    return one_hot(column == iota((count, width), 1) + first)


def spread_rows(index_ref, start, count):
    tiles = index_ref.shape[0]
    base = iota((count, LANE), 0) + start
    return jnp.concatenate([one_hot(index_ref[t : t + 1, :] == base) for t in range(tiles)], axis=1)


def sigmoid(v):
    return 0.5 * jnp.tanh(0.5 * v) + 0.5


def live_rows(count_ref, start, count):
    return (iota((count, 1), 0) + start < count_ref[0] * LANE).astype(F32)


def normalize(values):
    centred = values - jnp.mean(values, axis=1, keepdims=True)
    inverse = lax.rsqrt(jnp.mean(centred * centred, axis=1, keepdims=True) + epsilon)
    return centred * inverse, inverse


def normalize_back(upstream, normed, inverse):
    return inverse * (
        upstream
        - jnp.mean(upstream, axis=1, keepdims=True)
        - normed * jnp.mean(upstream * normed, axis=1, keepdims=True)
    )


def loop(count, body, rows=ROWS):
    def step(i, carry):
        body(pl.multiple_of(i * rows, rows), i)
        return carry

    if count == rows:
        body(0, 0)
    else:
        lax.fori_loop(0, count // rows, step, 0)


def outgoing_kernel(rows_ref, node_ref, out_ref):
    nodes, halo = node_ref.shape[0], rows_ref.shape[1]
    spread = one_hot(rows_ref[...] == iota((nodes, halo), 0))
    out_ref[...] = dot_lt(spread, node_ref[...]).reshape(out_ref.shape).astype(BF)


def own_kernel(
    send_ref,
    recv_ref,
    node,
    w_edge,
    edge,
    node_turned,
    edge_turned,
    begun,
    send_cols,
    recv_cols,
):
    nodes, width = node.shape
    columns_of(send_ref, send_cols)
    columns_of(recv_ref, recv_cols)
    node_ref = node.ready()

    def body(start, i):
        here = pl.ds(start, BIG)
        from_send = dot(pick_rows(send_cols, start, BIG, 0, nodes), node_ref[...]).astype(BF)
        from_recv = dot(pick_rows(recv_cols, start, BIG, 0, nodes), node_ref[...]).astype(BF)
        w_ref = w_edge.ready()
        found = dot(from_send, w_ref[width : 2 * width, :]) + dot(
            from_recv, w_ref[2 * width : 3 * width, :]
        )
        edge_ref = edge.ready()
        begun.buffer[here, :] = found + dot(edge_ref[here, :], w_ref[0:width, :])
        begun.send(i)

    loop(edge.shape[0], body, edge.shape[0])
    for source, out in ((node_ref, node_turned), (edge.buffer, edge_turned)):
        for i in range(0, source.shape[0], BIG):
            out.buffer[:, i : i + BIG] = source[i : i + BIG, :].T
        out.send(0)


def deal(place_ref, depth, pieces, send, keep):
    core, column, member = place_ref[0], place_ref[1], place_ref[2]
    half = pieces[0][0].shape[1] // 2
    rows = sum(count for _, count in pieces)
    part = rows // 4
    for which, out in ((1 - core, send), (core, keep)):

        def step(s, carry):
            line = (column + s) % 4
            for z in range(depth):
                patch = (line * depth + z) * 2 + which
                found = []
                for ref, count in pieces:
                    if ref.shape[0] == count:
                        found.append(ref[...])
                    else:
                        found.append(ref[pl.ds(pl.multiple_of(patch * count, 8), count), :])
                block = jnp.concatenate(found, axis=0).astype(BF)
                out.buffer[s, z * rows : (z + 1) * rows, :] = block[:, 0:half]
                at = pl.multiple_of((s * depth + z) * part, 16)
                for x in range(4):
                    out.buffer[4 + (x - member + 4) % 4, pl.ds(at, part), :] = block[
                        x * part : (x + 1) * part, half:
                    ]
            out.send(s)
            return carry

        lax.fori_loop(0, 4, step, 0)
        for s in range(4, 8):
            out.send(s)


def main_kernel(
    patches,
    place_ref,
    count_ref,
    send_ref,
    recv_ref,
    gain_edge_ref,
    gain_node_ref,
    incoming,
    w_edge_send,
    begun,
    w_edge_out,
    node,
    w_node,
    w_node_out,
    node_cot,
    node_turned,
    edge_cot,
    edge_turned,
    grad_first,
    first_out,
    from_send,
    from_recv,
    outward,
    piece_send,
    piece_keep,
    send_cols,
    recv_cols,
    hidden_ref,
    slope_ref,
    normed_ref,
    inverse_ref,
    message,
    gathered,
    node_hidden,
    grad_second,
    spread_recv,
    back_ref,
    gains,
    sum_in,
    sum_out,
    edge_sum_in,
    edge_sum_out,
):
    nodes, width = node.shape
    edges = begun.shape[0]
    halo = incoming.shape[0] * incoming.shape[1]
    columns_of(send_ref, send_cols)
    columns_of(recv_ref, recv_cols)
    halo_ref, w_send_ref, w_edge_out_ref = (
        incoming.ready()[...].astype(F32).reshape(halo, width).astype(BF),
        w_edge_send.ready(),
        w_edge_out.ready(),
    )

    def edge_body(start, i):
        here = pl.ds(start, BIG)
        latent = dot(pick_rows(send_cols, start, BIG, nodes, halo), halo_ref)
        more = dot(latent.astype(BF), w_send_ref[...])
        first = begun.part(i)[here, :] + more
        squash = sigmoid(first)
        hidden = (first * squash).astype(BF)
        hidden_ref[here, :] = hidden
        slope_ref[here, :] = (squash * (1.0 + first * (1.0 - squash))).astype(BF)
        normed, inverse = normalize(dot(hidden, w_edge_out_ref[...]))
        normed_ref[here, :] = normed.astype(BF)
        inverse_ref[here, :] = jnp.broadcast_to(inverse, (BIG, LANE))
        live = live_rows(count_ref, start, BIG)
        message[here, :] = (live * (gain_edge_ref[...] * normed)).astype(BF)

    loop(edges, edge_body, BIG)
    gains[...] = jnp.zeros_like(gains)
    node_ref, w_node_ref, w_node_out_ref = node.ready(), w_node.ready(), w_node_out.ready()

    def node_body(start, i):
        here = pl.ds(start, BIG)
        spread = spread_rows(recv_ref, start, BIG)
        spread_recv[here, :] = spread
        taken = dot(spread, message[...]).astype(BF)
        gathered[here, :] = taken
        first = dot(node_ref[here, :], w_node_ref[0:width, :]) + dot(
            taken, w_node_ref[width : 2 * width, :]
        )
        squash = sigmoid(first)
        hidden = (first * squash).astype(BF)
        node_hidden[here, :] = hidden
        slope = squash * (1.0 + first * (1.0 - squash))
        normed, inverse = normalize(dot(hidden, w_node_out_ref[...]))
        upstream = node_cot.part(i)[here, :].astype(F32)
        gains[1:2, :] += jnp.sum(upstream * normed, axis=0, keepdims=True)
        second = normalize_back(upstream * gain_node_ref[...], normed, inverse).astype(BF)
        grad_second[here, :] = second
        grad = (dot_rt(second, w_node_out_ref[...]) * slope).astype(BF)
        grad_first.buffer[here, :] = grad
        back_ref[here, :] = dot_rt(grad, w_node_ref[width : 2 * width, :]).astype(BF)
        grad_first.send(i)

    loop(nodes, node_body, BIG)
    node_turned_ref = node_turned.ready()
    sum_out[...] = dot_lt(node_hidden[...], grad_second[...])
    sum_in[0:width, :] = dot(node_turned_ref[...], grad_first.buffer[...])
    sum_in[width : 2 * width, :] = dot_lt(gathered[...], grad_first.buffer[...])

    def back_body(start, i):
        here = pl.ds(start, BIG)
        live = live_rows(count_ref, start, BIG)
        taken = dot(pick_rows(recv_cols, start, BIG, 0, nodes), back_ref[...])
        arrived = live * (edge_cot.part(i)[here, :].astype(F32) + taken)
        normed = normed_ref[here, :].astype(F32)
        gains[0:1, :] += jnp.sum(arrived * normed, axis=0, keepdims=True)
        second = normalize_back(
            arrived * gain_edge_ref[...], normed, inverse_ref[here, 0:1]
        ).astype(BF)
        grad_second[here, :] = second
        first_out.buffer[here, :] = (
            dot_rt(second, w_edge_out_ref[...]) * slope_ref[here, :].astype(F32)
        ).astype(BF)
        first_out.send(i)

    loop(edges, back_body, BIG)
    first_ref = first_out.buffer
    from_send.buffer[...] = dot(
        spread_rows(send_ref, 0, nodes + halo), first_ref[...]
    ).astype(BF)
    from_send.send(0)
    from_recv.buffer[...] = dot(spread_recv[...], first_ref[...]).astype(BF)
    from_recv.send(0)
    sent, received = from_send.buffer, from_recv.buffer
    back = dot_rt(sent[nodes : nodes + halo, :], w_send_ref[...])
    outward.buffer[...] = back.reshape(outward.shape).astype(BF)
    outward.send(0)
    edge_sum_out[...] = dot_lt(hidden_ref[...], grad_second[...])
    edge_sum_in[0:width, :] = dot(edge_turned.ready()[...], first_ref[...])
    edge_sum_in[width : 2 * width, :] = dot(node_turned_ref[...], sent[0:nodes, :]) + dot_lt(
        halo_ref, sent[nodes : nodes + halo, :]
    )
    edge_sum_in[2 * width : 3 * width, :] = dot(node_turned_ref[...], received[...])
    each = width // patches
    pieces = (
        (sum_in, 2 * each),
        (sum_out, each),
        (edge_sum_in, 3 * each),
        (edge_sum_out, each),
        (gains, 8),
    )
    deal(place_ref, patches // 8, pieces, piece_send, piece_keep)


def edge_grad_kernel(count_ref, w_own, first, cot, edge_grad):
    w_ref = w_own.ready()

    def edge_body(start, i):
        here = pl.ds(start, ROWS)
        live = live_rows(count_ref, start, ROWS)
        edge_grad.buffer[here, :] = (
            live * cot.part(i)[here, :].astype(F32) + dot_rt(first.part(i)[here, :], w_ref[...])
        ).astype(BF)
        edge_grad.send(i)

    loop(cot.shape[0], edge_body)


def node_grad_kernel(
    rows_ref, w_node, first, cot, w_both, from_send, from_recv, returned, out, token
):
    token.buffer[...] = jnp.zeros(token.shape, F32)
    token.send(0)
    nodes, width = first.shape
    halo = returned.shape[0] * returned.shape[1]
    w_node_ref, w_ref = w_node.ready(), w_both.ready()
    returned_ref = returned.ready()[...].astype(F32).reshape(halo, width).astype(BF)

    def body(start, i):
        here = pl.ds(start, ROWS)
        spread = one_hot(rows_ref[...] == iota((ROWS, halo), 0) + start)
        out.buffer[here, :] = (
            cot.part(i)[here, :].astype(F32)
            + dot_rt(first.part(i)[here, :], w_node_ref[...])
            + dot(spread, returned_ref)
            + dot_rt(from_send.part(i)[here, :], w_ref[0:width, :])
            + dot_rt(from_recv.part(i)[here, :], w_ref[width : 2 * width, :])
        ).astype(BF)
        out.send(i)

    loop(nodes, body)


def pair_kernel(keep_ref, got_ref, *outs):
    for s in range(8):
        outs[s][...] = (keep_ref[s].astype(F32) + got_ref[s].astype(F32)).astype(BF)


def sum_of(refs):
    a, b, c, d = [ref[...].astype(F32) for ref in refs]
    return (a + b) + (c + d)


def right_kernel(a, b, c, d, *outs):
    total = sum_of((a, b, c, d))
    rows = total.shape[0] // 4
    for s in range(4):
        outs[s][...] = total[s * rows : (s + 1) * rows].astype(BF)


def four_kernel(*refs):
    left, right, out = sum_of(refs[0:4]), sum_of(refs[4:8]), refs[8]
    depth = out.shape[0]
    many, few = left.shape[0] // depth, right.shape[0] // depth
    for z in range(depth):
        out[z] = jnp.concatenate(
            [left[z * many : (z + 1) * many], right[z * few : (z + 1) * few]], axis=0
        ).astype(BF)


def depth_kernel(got_ref, out_ref):
    total = got_ref[0].astype(F32)
    for i in range(1, got_ref.shape[0]):
        total = total + got_ref[i].astype(F32)
    out_ref[...] = total.astype(BF)


def finish_kernel(
    factor,
    place_ref,
    a,
    b,
    c,
    d,
    edge_in_ref,
    edge_out_ref,
    node_in_ref,
    node_out_ref,
    gain_ref,
    left,
    right,
):
    member = place_ref[2]
    rows, half = left.shape[1:]
    for s, ref in enumerate((a, b, c, d)):
        source = (member - s + 4) % 4
        values = ref[...].astype(F32)
        left[source] = values[0:rows]
        right[source] = values[rows : rows + right.shape[1]]
    total = ((left[0] + left[1]) + (left[2] + left[3])) * factor
    other = right[...].reshape(rows, half) * factor
    at = 0
    for out in (node_in_ref, node_out_ref, edge_in_ref, edge_out_ref, gain_ref):
        out[:, 0:half] = total[at : at + out.shape[0], :]
        out[:, half : 2 * half] = other[at : at + out.shape[0], :]
        at += out.shape[0]


VM = pl.BlockSpec(memory_space=pltpu.VMEM)
SM = pl.BlockSpec(memory_space=pltpu.SMEM)

TOKEN = ((8, LANE), F32, 1)


class Moved:
    def __init__(self, far, buffer, semaphores, parts, first, outward):
        self.far, self.buffer, self.semaphores = far, buffer, semaphores
        self.parts, self.first, self.outward = parts, first, outward
        self.shape = buffer.shape
        self.step = buffer.shape[0] // parts

    def copy(self, i):
        near = self.buffer.at[pl.ds(i * self.step, self.step)]
        far = self.far.at[pl.ds(self.first + i * self.step, self.step)]
        ends = (near, far) if self.outward else (far, near)
        return pltpu.make_async_copy(*ends, self.semaphores.at[i])

    def send(self, i):
        self.copy(i).start()

    def part(self, i):
        self.copy(i).wait()
        return self.buffer

    def ready(self):
        for i in range(self.parts):
            self.copy(i).wait()
        return self.buffer


class Part:
    def __init__(self, array, parts=1, first=0, rows=None):
        self.array, self.parts, self.first = array, parts, first
        self.rows = array.shape[0] if rows is None else rows


def call(kernel, outs, ins, scratch=(), scalars=0, flops=0, fetch=(), store=(), limit=None, after=(), through=None):
    ins = list(ins)
    passed = [] if through is None else [through]
    fetch = [f if isinstance(f, Part) else Part(f) for f in fetch]
    shapes = [jax.ShapeDtypeStruct(s, d) for s, d in list(outs) + [o[:2] for o in store]]
    shapes += [jax.ShapeDtypeStruct(p.shape, p.dtype) for p in passed]
    single = len(shapes) == 1
    buffers = [((f.rows, *f.array.shape[1:]), f.array.dtype) for f in fetch]
    size = sum(int(a.size) * a.dtype.itemsize for a in ins + shapes)
    held = list(scratch) + buffers + [o[:2] for o in store]
    bytes_here = sum(
        functools.reduce(lambda x, y: x * y, s) * jnp.dtype(d).itemsize for s, d in held
    )
    many, kept, given = len(fetch), len(store), len(outs)

    def take(refs, count):
        return refs[:count], refs[count:]

    def body(*refs):
        args, refs = take(refs, len(ins))
        _, refs = take(refs, len(after))
        sources, refs = take(refs, many)
        _, refs = take(refs, len(passed))
        results, refs = take(refs, given)
        targets, refs = take(refs, kept)
        _, refs = take(refs, len(passed))
        own, refs = take(refs, len(scratch))
        slots, refs = take(refs, many)
        rooms, refs = take(refs, kept)
        marks, ends = take(refs, many)
        arriving = [
            Moved(src, slot, mark, f.parts, f.first, False)
            for src, f, slot, mark in zip(sources, fetch, slots, marks)
        ]
        for one in arriving:
            for i in range(one.parts):
                one.send(i)
        leaving = [
            Moved(t, room, end, o[2], 0, True)
            for t, room, end, o in zip(targets, rooms, ends, store)
        ]
        kernel(*args, *arriving, *results, *leaving, *own)
        for one in leaving:
            one.ready()

    far = pl.BlockSpec(memory_space=pltpu.HBM)
    out_specs = [VM] * given + [far] * (kept + len(passed))
    return pl.pallas_call(
        body,
        out_shape=shapes[0] if single else shapes,
        in_specs=[SM] * scalars
        + [VM] * (len(ins) - scalars)
        + [pl.BlockSpec(memory_space=pl.ANY)] * len(after)
        + [far] * (many + len(passed)),
        out_specs=out_specs[0] if single else out_specs,
        scratch_shapes=[pltpu.VMEM(s, d) for s, d in held]
        + [pltpu.SemaphoreType.DMA((f.parts,)) for f in fetch]
        + [pltpu.SemaphoreType.DMA((o[2],)) for o in store],
        compiler_params=pltpu.CompilerParams(
            vmem_limit_bytes=bytes_here + 4 * 2**20 if limit is None else limit
        ),
        cost_estimate=pl.CostEstimate(flops=flops, bytes_accessed=size, transcendentals=0),
        input_output_aliases={len(ins) + len(after) + many: given + kept} if passed else {},
    )(*ins, *after, *[f.array for f in fetch], *passed)


def main_call(
    patches,
    piece,
    place,
    tile_count,
    senders,
    receivers,
    gain_edge,
    gain_node,
    incoming,
    begun,
    node,
    n_cot,
    node_turned,
    e_cot,
    edge_turned,
    w_edge_in,
    w_edge_out,
    w_node_in,
    w_node_out,
):
    nodes, width = node.shape
    edges, halo = e_cot.shape[0], incoming.shape[0] * incoming.shape[1]

    def wide(rows, kind=BF, step=ROWS):
        return ((rows, width), kind, rows // step)

    return call(
        functools.partial(main_kernel, patches),
        [],
        [place, tile_count, senders, receivers, gain_edge, gain_node],
        [((edges, LANE), jnp.int32)] * 2
        + [((edges, width), BF)] * 3
        + [((edges, LANE), F32)]
        + [((edges, width), BF)]
        + [((nodes, width), BF)] * 3
        + [((nodes, edges), BF), ((nodes, width), BF)]
        + [
            ((8, width), F32),
            ((2 * width, width), F32),
            ((width, width), F32),
            ((3 * width, width), F32),
            ((width, width), F32),
        ],
        scalars=2,
        flops=52 * nodes * width * width,
        fetch=[
            incoming,
            Part(w_edge_in, 1, width, width),
            Part(begun, edges // BIG),
            w_edge_out,
            node,
            w_node_in,
            w_node_out,
            Part(n_cot, nodes // BIG),
            node_turned,
            Part(e_cot, edges // BIG),
            edge_turned,
        ],
        store=[
            wide(nodes, BF, BIG),
            wide(edges, BF, BIG),
            wide(nodes + halo, BF, nodes + halo),
            wide(nodes, BF, nodes),
            ((patches, halo // patches, width), BF, 1),
            piece,
            piece,
        ],
        limit=FULL,
    )


def local(
    node_tape,
    edge_tape,
    node_cot,
    edge_cot,
    w_edge_in,
    w_edge_out,
    gain_edge,
    w_node_in,
    w_node_out,
    gain_node,
    senders,
    receivers,
    tile_count,
    send_rows,
):
    node, edge = node_tape[0], edge_tape[0]
    n_cot, e_cot = node_cot[0], edge_cot[0]
    nodes, width = node.shape
    edges = edge.shape[0]
    halo = send_rows.shape[1]
    patches = lax.axis_size("patch")
    members = lax.axis_size("group")
    depth = patches // 8
    here = lax.axis_index("patch")
    place = jnp.stack([here % 2, here // (2 * depth), lax.axis_index("group")]).astype(jnp.int32)
    gain_edge = gain_edge.reshape(1, width)
    gain_node = gain_node.reshape(1, width)
    twins = [(i, i ^ 1) for i in range(patches)]
    column = 2 * depth
    lines = [[y * column + 2 * z + c for z in range(depth)] for y in range(4) for c in range(2)]
    unit = 2 * width * width

    def to_member(x, shift):
        return lax.ppermute(x, "group", [(g, (g + shift) % members) for g in range(members)])

    def to_column(x, shift):
        return lax.ppermute(x, "patch", [(i, (i + shift * column) % patches) for i in range(patches)])

    def along_depth(x):
        return lax.all_to_all(x, "patch", 0, 0, axis_index_groups=lines, tiled=True)

    parts = edges // ROWS

    def wide(rows, kind=BF):
        return ((rows, width), kind, rows // ROWS)

    parts = edges // ROWS

    def wide(rows, kind=BF):
        return ((rows, width), kind, rows // ROWS)

    outgoing = call(
        outgoing_kernel,
        [((patches, halo // patches, width), BF)],
        [send_rows, node],
        flops=2 * halo * nodes * width,
        limit=16 * 2**20,
    )
    incoming = lax.all_to_all(outgoing, "patch", split_axis=0, concat_axis=0, tiled=True)
    node_turned, edge_turned, begun = call(
        own_kernel,
        [],
        [senders, receivers],
        [((edges, LANE), jnp.int32)] * 2,
        flops=7 * edges * unit,
        fetch=[node, w_edge_in, edge],
        store=[((width, nodes), BF, 1), ((width, edges), BF, 1), ((edges, width), F32, edges // BIG)],
        limit=FULL,
    )
    each = width // patches
    rows, half = 8 * each, width // 2
    piece = ((8, depth * rows, half), BF, 8)
    node_first, grad_first, from_send, from_recv, outward, send, keep = main_call(
        patches,
        piece,
        place,
        tile_count,
        senders,
        receivers,
        gain_edge,
        gain_node,
        incoming,
        begun,
        node,
        n_cot,
        node_turned,
        e_cot,
        edge_turned,
        w_edge_in,
        w_edge_out,
        w_node_in,
        w_node_out,
    )
    got = lax.ppermute(send, "patch", twins)
    edge_grad, keep = call(
        edge_grad_kernel,
        [],
        [tile_count],
        scalars=1,
        flops=nodes * unit,
        fetch=[Part(w_edge_in, 1, 0, width), Part(grad_first, parts), Part(e_cot, parts)],
        store=[wide(edges)],
        limit=FULL,
        through=keep,
    )
    sums = call(pair_kernel, [(keep.shape[1:], BF)] * 8, [keep, got])
    columns = [sums[0]] + [to_column(sums[s], s) for s in range(1, 4)]
    rights = call(
        right_kernel,
        [((depth * rows // 4, half), BF)] * 4,
        [sums[4]] + [to_member(sums[4 + s], s) for s in range(1, 4)],
    )
    columns += [rights[0]] + [to_column(rights[s], s) for s in range(1, 4)]
    returned = lax.all_to_all(outward, "patch", split_axis=0, concat_axis=0, tiled=True)
    blocks = call(
        four_kernel,
        [((depth, rows + rows // 4, half), BF)],
        columns,
        flops=8 * nodes * unit,
    )
    lines_got = along_depth(blocks)
    node_grad, node_token = call(
        node_grad_kernel,
        [],
        [send_rows],
        flops=3 * nodes * unit,
        fetch=[
            Part(w_node_in, 1, 0, width),
            Part(node_first, nodes // ROWS),
            Part(n_cot, nodes // ROWS),
            Part(w_edge_in, 1, width, 2 * width),
            Part(from_send, nodes // ROWS, 0, nodes),
            Part(from_recv, nodes // ROWS),
            returned,
        ],
        store=[wide(nodes), TOKEN],
        limit=FULL,
    )
    mine = call(
        depth_kernel,
        [((rows + rows // 4, half), BF)],
        [lines_got],
        after=[node_token],
    )
    shared = [mine] + [to_member(mine, s) for s in range(1, 4)]
    factor = float(members * patches * edges) ** (-0.5)
    out_edge_in, out_edge_out, out_node_in, out_node_out, out_gain = call(
        functools.partial(finish_kernel, factor),
        [
            ((3 * each, width), F32),
            ((each, width), F32),
            ((2 * each, width), F32),
            ((each, width), F32),
            ((8, width), F32),
        ],
        [place] + shared,
        [((4, rows, half), F32), ((4, rows // 4, half), F32)],
        scalars=1,
    )
    out_gain = lax.dynamic_slice(out_gain, (0, here * each), (2, each))
    return (
        edge_grad[None],
        node_grad[None],
        out_edge_in,
        out_edge_out,
        out_gain[0],
        out_node_in,
        out_node_out,
        out_gain[1],
    )


def solution(mesh):
    placed = (
        P("group", "patch", None),
        P("group", "patch", None),
        P("group", "patch", None),
        P("group", "patch", None),
        P(),
        P(),
        P(),
        P(),
        P(),
        P(),
        P("patch", None),
        P("patch", None),
        P("patch"),
        P("patch", None),
    )
    return jax.shard_map(
        local,
        mesh=mesh,
        in_specs=placed,
        out_specs=(
            P("group", "patch", None),
            P("group", "patch", None),
            P("patch", None),
            P("patch", None),
            P("patch"),
            P("patch", None),
            P("patch", None),
            P("patch"),
        ),
        check_vma=False,
    )
```
